256 devices in a mesh: gx: 16 (over y, x), gy: 16 (over z, core).
Axes of the slice: x: 4, y: 4, z: 8, core: 2. Of those that a mesh axis runs over, the one named last changes fastest.
Arguments:
- thermal_anomaly: float32 [75, 128, 2048], P(None, 'gy', 'gx'), may hold values from -6 to 6
- saltiness_anomaly: float32 [75, 128, 2048], P(None, 'gy', 'gx'), may hold values from -6 to 6
- east_face_speed: float32 [75, 128, 2048], P(None, 'gy', 'gx'), may hold values from -3 to 3
- north_face_speed: float32 [75, 128, 2048], P(None, 'gy', 'gx'), may hold values from -3 to 3
- sea_elevation: float32 [128, 2048], P('gy', 'gx'), may hold values from -2 to 2
- water_land_flag: int32 [128, 2048], P('gy', 'gx'), may hold values 0 or 1
- bottom_layer_index: int32 [128, 2048], P('gy', 'gx'), may hold values from 18 to 75
Outputs:
- temperature_next: float32 [75, 128, 2048], P(None, 'gy', 'gx')
- salinity_next: float32 [75, 128, 2048], P(None, 'gy', 'gx')
- east_velocity_next: float32 [75, 128, 2048], P(None, 'gy', 'gx')
- north_velocity_next: float32 [75, 128, 2048], P(None, 'gy', 'gx')
- surface_next: float32 [128, 2048], P('gy', 'gx')
The draws below stay inside these ranges and needn't reach their ends.
Inputs may be any that keep to these rules, and one draw needn't show every extreme that they name: `water_land_flag`: 1 marks an ocean column, 0 land. `bottom_layer_index`: levels of a column counted from the top; only used where water_land_flag is 1.
All inputs are finite; a program needn't handle non-finite values. No bound on the sum of `water_land_flag` on one device may be relied on, other than what follows from the above.
Results may differ from the reference program's by a relative error of at most 0.00002.
Values sent between devices are 32-bit elements; how exact they have to be, the bound alone decides.
A program may use at most 64 MiB of HBM per device.

```python
import jax
import jax.numpy as jnp

VERTICAL_LAYERS = 75
SUBSTEPS = 8
LONGITUDE_LINES = 2048
LATITUDE_LINES = 128


def place_ends(array, rng, least, high):
    extent = array.shape
    spot = [jax.random.randint(jax.random.fold_in(rng, axis), (), 0, extent[axis]) for axis in range(len(extent))]
    array = array.at[tuple(spot)].set(least)
    longest = extent.index(max(extent))
    spot[longest] = (spot[longest] + 1) % extent[longest]
    return array.at[tuple(spot)].set(high)


def levels(stream_key, extent, cuts, smallest, high):
    level, own = 1.0, jax.random.fold_in(stream_key, 6)
    for dim, blocks in cuts:
        draws = jnp.exp(jax.random.uniform(jax.random.fold_in(own, dim), (blocks,), jnp.float32, smallest / len(cuts), high / len(cuts)))
        level = level * jnp.repeat(draws, extent[dim] // blocks).reshape([-1 if axis == dim else 1 for axis in range(len(extent))])
    return level


def centred(rng, shape, spread, limit, shards=(), kind=jnp.bfloat16):
    array = jax.random.normal(rng, shape, jnp.float32) * spread
    if len(shards) > 0:
        array = levels(rng, shape, shards, -0.22, 0.18) * array
    return jnp.clip(array, min=-limit, max=limit).astype(kind)


def setup_inputs(seed: int = 0) -> dict:
    key_of = jax.random.split(jax.random.key(seed), 8)
    thermal_anomaly = centred(key_of[0], (VERTICAL_LAYERS, LATITUDE_LINES, LONGITUDE_LINES), 1.0, 6.0, ((1, 16), (2, 16)), jnp.float32)
    saltiness_anomaly = centred(key_of[1], (VERTICAL_LAYERS, LATITUDE_LINES, LONGITUDE_LINES), 1.0, 6.0, ((1, 16), (2, 16)), jnp.float32)
    east_face_speed = centred(key_of[2], (VERTICAL_LAYERS, LATITUDE_LINES, LONGITUDE_LINES), 0.5, 3.0, ((1, 16), (2, 16)), jnp.float32)
    north_face_speed = centred(key_of[3], (VERTICAL_LAYERS, LATITUDE_LINES, LONGITUDE_LINES), 0.5, 3.0, ((1, 16), (2, 16)), jnp.float32)
    sea_elevation = centred(key_of[4], (LATITUDE_LINES, LONGITUDE_LINES), 0.3, 2.0, ((0, 16), (1, 16)), jnp.float32)
    water_land_flag = place_ends((jax.random.randint(key_of[5], (LATITUDE_LINES, LONGITUDE_LINES), 0, 10) < 9).astype(jnp.int32), jax.random.fold_in(key_of[5], 1), 0, 1)
    bottom_layer_index = place_ends(jax.random.randint(key_of[6], (LATITUDE_LINES, LONGITUDE_LINES), max(1, VERTICAL_LAYERS // 4), VERTICAL_LAYERS + 1), jax.random.fold_in(key_of[6], 1), max(1, VERTICAL_LAYERS // 4), VERTICAL_LAYERS).astype(jnp.int32)
    return {"thermal_anomaly": thermal_anomaly, "saltiness_anomaly": saltiness_anomaly, "east_face_speed": east_face_speed, "north_face_speed": north_face_speed, "sea_elevation": sea_elevation, "water_land_flag": water_land_flag, "bottom_layer_index": bottom_layer_index}


time_step = 0.4
viscosity = 0.025
diffusion = 0.01
tracer_step = 0.2
gravity = 4.0
coriolis_base = 0.2
coriolis_slope = 0.3


def from_east(field):
    return jnp.roll(field, -1, axis=-1)


def from_west(field):
    return jnp.roll(field, 1, axis=-1)


def from_north(field):
    return jnp.concatenate([field[..., 1:, :], jnp.zeros_like(field[..., :1, :])], axis=-2)


def from_south(field):
    return jnp.concatenate([jnp.zeros_like(field[..., :1, :]), field[..., :-1, :]], axis=-2)


def laplacian(field):
    return from_east(field) + from_west(field) + from_north(field) + from_south(field) - 4.0 * field


def layer_thickness(count):
    position = jnp.arange(count, dtype=jnp.float32)
    return ((0.5 + (position + 0.5) / count) / count)[:, None, None]


def hydrostatic_load_from(thermal_flooded, saltiness_flooded, layer_span):
    water_mass_per_volume = -0.2 * thermal_flooded + 0.8 * saltiness_flooded - 0.05 * thermal_flooded * thermal_flooded
    weighted = water_mass_per_volume * layer_span
    return jnp.cumsum(weighted, axis=0) - 0.5 * weighted


def reference(thermal_anomaly, saltiness_anomaly, east_face_speed, north_face_speed, sea_elevation, water_land_flag, bottom_layer_index):
    columns = water_land_flag * bottom_layer_index
    level_index = jnp.arange(VERTICAL_LAYERS, dtype=jnp.int32)[:, None, None]
    flooded_box_flag = (level_index < columns[None]).astype(jnp.float32)
    layer_span = layer_thickness(VERTICAL_LAYERS)
    wet_u = flooded_box_flag * from_east(flooded_box_flag)
    wet_v = flooded_box_flag * from_north(flooded_box_flag)
    depth_u = jnp.sum(layer_span * wet_u, axis=0)
    depth_v = jnp.sum(layer_span * wet_v, axis=0)
    open_u = wet_u[0]
    open_v = wet_v[0]
    ocean = flooded_box_flag[0]
    safe_u = depth_u + (1.0 - open_u)
    safe_v = depth_v + (1.0 - open_v)
    thermal_flooded = thermal_anomaly * flooded_box_flag
    saltiness_flooded = saltiness_anomaly * flooded_box_flag
    east_flooded_flag = east_face_speed * wet_u
    north_flooded_flag = north_face_speed * wet_v
    hydrostatic_load = hydrostatic_load_from(thermal_flooded, saltiness_flooded, layer_span)
    latitude = (jnp.arange(LATITUDE_LINES, dtype=jnp.float32) + 0.5) / LATITUDE_LINES
    coriolis = (coriolis_base + coriolis_slope * latitude)[:, None]
    v_at_u = 0.25 * (((north_flooded_flag + from_east(north_flooded_flag)) + from_south(north_flooded_flag)) + from_south(from_east(north_flooded_flag)))
    u_at_v = 0.25 * (((east_flooded_flag + from_west(east_flooded_flag)) + from_north(east_flooded_flag)) + from_north(from_west(east_flooded_flag)))
    u_star = wet_u * (east_flooded_flag + time_step * (-(from_east(hydrostatic_load) - hydrostatic_load) + coriolis * v_at_u - viscosity * laplacian(laplacian(east_flooded_flag))))
    v_star = wet_v * (north_flooded_flag + time_step * (-(from_north(hydrostatic_load) - hydrostatic_load) - coriolis * u_at_v - viscosity * laplacian(laplacian(north_flooded_flag))))
    start_u = jnp.sum(layer_span * east_flooded_flag, axis=0)
    start_v = jnp.sum(layer_span * north_flooded_flag, axis=0)
    total_u = jnp.sum(layer_span * u_star, axis=0)
    total_v = jnp.sum(layer_span * v_star, axis=0)
    forcing_u = (total_u - start_u) / time_step
    forcing_v = (total_v - start_v) / time_step
    sub_step = time_step / SUBSTEPS
    level_now = ocean * sea_elevation
    trans_u = start_u
    trans_v = start_v
    summed_u = jnp.zeros_like(start_u)
    summed_v = jnp.zeros_like(start_v)
    for substep in range(SUBSTEPS):
        trans_u = open_u * (trans_u + sub_step * (forcing_u - gravity * depth_u * (from_east(level_now) - level_now)))
        trans_v = open_v * (trans_v + sub_step * (forcing_v - gravity * depth_v * (from_north(level_now) - level_now)))
        level_now = ocean * (level_now - sub_step * ((trans_u - from_west(trans_u)) + (trans_v - from_south(trans_v))))
        summed_u = summed_u + trans_u
        summed_v = summed_v + trans_v
    mean_u = summed_u / SUBSTEPS
    mean_v = summed_v / SUBSTEPS
    u_new = wet_u * (u_star + (mean_u - total_u) / safe_u)
    v_new = wet_v * (v_star + (mean_v - total_v) / safe_v)
    carried_fields = jnp.stack([thermal_flooded, saltiness_flooded])
    flux_east = u_new * (0.5 * (carried_fields + from_east(carried_fields)))
    flux_north = v_new * (0.5 * (carried_fields + from_north(carried_fields)))
    advected = flooded_box_flag * (carried_fields - tracer_step * ((flux_east - from_west(flux_east)) + (flux_north - from_south(flux_north))))
    mixed = flooded_box_flag * (advected - diffusion * laplacian(laplacian(advected)))
    return mixed[0], mixed[1], u_new, v_new, level_now
```

```python
import functools

import jax
import jax.numpy as jnp
from jax import lax
from jax.experimental import pallas as pl
from jax.experimental.pallas import tpu as pltpu
from jax.sharding import PartitionSpec as P

MESH = pl.DeviceIdType.MESH
K = 75
NC = 5
LC = K // NC
SUBSTEPS = 8
ROWS = 8
LANES = 128

DT = 0.4
NU = 0.025
KAPPA = 0.01
DTT = 0.2
GRAVITY = 4.0
DB = DT / SUBSTEPS

AROUND = [(dx, dy) for dy in (-1, 0, 1) for dx in (-1, 0, 1) if (dx, dy) != (0, 0)]
CORNERS = [(dx, dy) for dx, dy in AROUND if dx != 0 and dy != 0]


class Wires:
    def __init__(self, send, recv, gx, gy, nx, ny):
        self.send, self.recv = send, recv
        self.gx, self.gy, self.nx, self.ny = gx, gy, nx, ny
        self.used = 0

    def slots(self, count=1):
        first = self.used
        self.used += count
        return first

    def device(self, dx, dy):
        return (lax.rem(self.gx + dx + self.nx, self.nx), lax.rem(self.gy + dy + self.ny, self.ny))

    def copy(self, src, dst, slot, dx, dy):
        return pltpu.make_async_remote_copy(
            src_ref=src,
            dst_ref=dst,
            send_sem=self.send.at[slot],
            recv_sem=self.recv.at[slot],
            device_id=self.device(dx, dy),
            device_id_type=MESH,
        )


N_WIRES = 128


def kernel(
    nx,
    ny,
    t_in,
    s_in,
    u_in,
    v_in,
    h_in,
    flag_in,
    bottom_in,
    t_out,
    s_out,
    u_out,
    v_out,
    h_out,
    X,
    D2,
    flag_v,
    bottom_v,
    CU,
    CV,
    CC,
    PC,
    pack,
    PE,
    PW,
    F2,
    DV,
    U1B,
    V1X,
    pu1,
    PU1,
    AX,
    packa,
    QE,
    QW,
    UN,
    VN,
    TN,
    SN,
    HN,
    load_sem,
    send_sem,
    recv_sem,
    out_sem,
):
    gx, gy = lax.axis_index("gx"), lax.axis_index("gy")
    wires = Wires(send_sem, recv_sem, gx, gy, nx, ny)
    sent = []

    loads = [
        pltpu.make_async_copy(h_in, D2.at[1, 1, pl.ds(8, 8), :], load_sem.at[4]),
        pltpu.make_async_copy(flag_in, flag_v, load_sem.at[5]),
        pltpu.make_async_copy(bottom_in, bottom_v, load_sem.at[6]),
        pltpu.make_async_copy(u_in, X.at[0, :, pl.ds(8, 8), :], load_sem.at[0]),
        pltpu.make_async_copy(v_in, X.at[1, :, pl.ds(8, 8), :], load_sem.at[1]),
        pltpu.make_async_copy(t_in, X.at[2, :, pl.ds(8, 8), :], load_sem.at[2]),
        pltpu.make_async_copy(s_in, X.at[3, :, pl.ds(8, 8), :], load_sem.at[3]),
    ]
    for load in loads:
        load.start()

    barrier = pltpu.get_barrier_semaphore()
    for dx, dy in AROUND:
        pl.semaphore_signal(barrier, inc=1, device_id=wires.device(dx, dy), device_id_type=MESH)

    lane = lax.broadcasted_iota(jnp.int32, (ROWS, LANES), 1)
    lane4 = lax.rem(lane, 4)
    lane_group = lax.div(lane, 4).astype(jnp.float32)
    row = lax.broadcasted_iota(jnp.int32, (ROWS, LANES), 0)
    first, last = lane == 0, lane == LANES - 1
    low2, at1, at2 = lane4 < 2, lane4 == 1, lane4 == 2
    has_south, has_north = gy > 0, gy < ny - 1

    def roll(x, shift):
        return pltpu.roll(x, shift % LANES, 1)

    def east(x, halo):
        return roll(jnp.where(first, halo, x), LANES - 1)

    def west(x, halo):
        return roll(jnp.where(last, halo, x), 1)

    def unpacked(packed, i):
        return roll(packed, LANES - 2 - 4 * i)

    @pl.when(jnp.logical_not(has_south))
    def _():
        AX[:, :, 6:8, :] = jnp.zeros((2, K, 2, LANES), jnp.float32)

    @pl.when(jnp.logical_not(has_north))
    def _():
        AX[:, :, 16:18, :] = jnp.zeros((2, K, 2, LANES), jnp.float32)

    for load in loads[:3]:
        load.wait()
    D2[0, 1, 8:16, :] = (flag_v[...] * bottom_v[...]).astype(jnp.float32)

    pl.semaphore_wait(barrier, len(AROUND))

    def spread(src, dst_of):
        copies = []
        for dx, dy in AROUND:
            copy = wires.copy(src, dst_of(1 - dx, 8 * (1 - dy)), wires.slots(), dx, dy)
            copy.start()
            copies.append(copy)
        sent.extend(copies)
        return copies

    got_d2 = spread(
        D2.at[:, 1, pl.ds(8, 8), :], lambda tile, r: D2.at[:, tile, pl.ds(r, 8), :]
    )

    for load in loads[3:]:
        load.wait()
    uv_slot = wires.slots(2 * NC)
    ts_slot = wires.slots(2 * NC)

    def uv_copy(c, up):
        src, dst, dy = (14, 6, 1) if up else (8, 16, -1)
        levels = pl.ds(c * LC, LC)
        return wires.copy(
            X.at[pl.ds(0, 2), levels, pl.ds(src, 2), :],
            X.at[pl.ds(0, 2), levels, pl.ds(dst, 2), :],
            uv_slot + 2 * c + int(up),
            0,
            dy,
        )

    def ts_copy(c, up):
        src, dst, dy = (15, 7, 1) if up else (8, 16, -1)
        levels = pl.ds(c * LC, LC)
        return wires.copy(
            X.at[pl.ds(2, 2), levels, pl.ds(src, 1), :],
            X.at[pl.ds(2, 2), levels, pl.ds(dst, 1), :],
            ts_slot + 2 * c + int(up),
            0,
            dy,
        )

    @pl.loop(0, NC)
    def _(c):
        for up in (True, False):
            uv_copy(c, up).start()
            ts_copy(c, up).start()

    @pl.loop(0, NC)
    def _(c):
        for f in range(4):
            held = jnp.zeros((ROWS, LANES), jnp.float32)
            for i in range(LC):
                edge = roll(X[f, c * LC + i, 8:16, :], 4 * i + 2)
                held = jnp.where(lane_group == i, edge, held)
            pack[f, c] = held

    got_packs = []

    def side_packs(src, to_east, to_west, corners):
        copies = [
            wires.copy(src, to_east, wires.slots(), 1, 0),
            wires.copy(src, to_west, wires.slots(), -1, 0),
        ]
        for dx, dy, corner_src, corner_dst in corners:
            copies.append(wires.copy(corner_src, corner_dst, wires.slots(), dx, dy))
        for copy in copies:
            copy.start()
        sent.extend(copies)
        return copies

    def corner_copies(src, west_side, east_side):
        out = []
        for dx, dy in CORNERS:
            side = west_side if dx > 0 else east_side
            r_src, r_dst = (7, 0) if dy > 0 else (0, 9)
            out.append(
                (dx, dy, src.at[:, :, pl.ds(r_src, 1), :], side.at[:, :, pl.ds(r_dst, 1), :])
            )
        return out

    uv_pack = pack.at[pl.ds(0, 2)]
    got_packs = side_packs(
        pack,
        PW.at[:, :, pl.ds(1, 8), :],
        PE.at[:, :, pl.ds(1, 8), :],
        corner_copies(uv_pack, PW.at[pl.ds(0, 2)], PE.at[pl.ds(0, 2)]),
    )

    for copy in got_d2:
        copy.wait_recv()
    row24 = lax.broadcasted_iota(jnp.int32, (24, LANES), 0)
    lane24 = lax.broadcasted_iota(jnp.int32, (24, LANES), 1)
    first24, last24 = lane24 == 0, lane24 == LANES - 1
    inside = jnp.logical_and(
        jnp.logical_or(row24 >= 8, has_south), jnp.logical_or(row24 < 16, has_north)
    )

    def ring_east(c, h):
        return (
            roll(jnp.where(first24, h, c), LANES - 1),
            roll(jnp.where(first24, c, h), LANES - 1),
        )

    def ring_west(c, h):
        return (
            roll(jnp.where(last24, h, c), 1),
            roll(jnp.where(last24, c, h), 1),
        )

    def north24(x):
        return pltpu.roll(x, 23, 0)

    def south24(x):
        return pltpu.roll(x, 1, 0)

    def sides(ref, f):
        return ref[f, 1], jnp.where(lane24 < 64, ref[f, 2], ref[f, 0])

    col = [jnp.where(inside, x, 0.0) for x in sides(D2, 0)]
    ocean = [x > 0.0 for x in col]
    level0 = [jnp.where(o, x, 0.0) for o, x in zip(ocean, sides(D2, 1))]
    cu = [jnp.minimum(a, b) for a, b in zip(col, ring_east(*col))]
    cv = [jnp.minimum(a, north24(a)) for a in col]

    def depth(c):
        return c * (0.5 / K + c * (0.5 / (K * K)))

    CC[...] = col[0]
    CU[...] = cu[0]
    CV[...] = cv[0]

    def four(x):
        edge = [jnp.broadcast_to(x[:, l : l + 1], x.shape) for l in (126, 127, 0, 1)]
        l4 = lax.rem(lax.broadcasted_iota(jnp.int32, x.shape, 1), 4)
        return jnp.where(l4 < 2, jnp.where(l4 == 0, edge[0], edge[1]), jnp.where(l4 == 2, edge[2], edge[3]))

    PC[0] = four(col[1])
    PC[1] = four(cu[1])
    PC[2] = four(cv[1])
    col_own4 = four(col[0][8:16])

    def start_sums(c, carry):
        su, sv = carry
        base = (c * LC).astype(jnp.float32)
        cu0, cv0 = CU[8:16, :] - base, CV[8:16, :] - base
        for i in range(LC):
            dz = 0.5 / K + (base + (i + 0.5)) * (1.0 / (K * K))
            su = su + jnp.where(cu0 > i, X[0, c * LC + i, 8:16, :], 0.0) * dz
            sv = sv + jnp.where(cv0 > i, X[1, c * LC + i, 8:16, :], 0.0) * dz
        return su, sv

    zero = jnp.zeros((ROWS, LANES), jnp.float32)
    start_u, start_v = lax.fori_loop(0, NC, start_sums, (zero, zero))
    F2[0, 1, 8:16, :] = start_u
    F2[1, 1, 8:16, :] = start_v
    got_start = spread(
        F2.at[pl.ds(0, 2), 1, pl.ds(8, 8), :],
        lambda tile, r: F2.at[pl.ds(0, 2), tile, pl.ds(r, 8), :],
    )

    for copy in got_packs:
        copy.wait_recv()
    at_wall = jnp.where(
        jnp.logical_or(
            jnp.logical_and(row == 0, jnp.logical_not(has_south)),
            jnp.logical_and(row == ROWS - 1, jnp.logical_not(has_north)),
        ),
        19.0,
        20.0,
    )
    latitude = (row + gy * ROWS).astype(jnp.float32)
    f4 = (0.25 * DT) * (0.2 + 0.3 * (latitude + 0.5) / (ROWS * ny))
    centre_uv = 1.0 - (DT * NU) * at_wall
    centre_ts = 1.0 - KAPPA * at_wall

    v1_slot = wires.slots(NC)

    def v1_copy(c):
        levels = pl.ds(c * LC, LC)
        return wires.copy(
            V1X.at[levels, pl.ds(15, 1), :], V1X.at[levels, pl.ds(7, 1), :], v1_slot + c, 0, 1
        )

    def edge_terms(a, y):
        return (
            2.0 * y
            - 8.0 * a
            + jnp.where(at2, roll(a, LANES - 1), roll(a, 1))
        )

    def spread_terms(a, y, halo_a, halo_q):
        z = 2.0 * y - 8.0 * a
        return east(z + east(a, halo_a), halo_q) + west(z + west(a, halo_a), halo_q)

    def weight(t, s, dz):
        return (0.8 * s - t * (0.2 + 0.05 * t)) * dz

    def momentum(c, carry):
        cum_e, cum_n, sum_u, sum_v = carry
        for up in (True, False):
            uv_copy(c, up).wait_recv()
            ts_copy(c, up).wait_recv()
        base = (c * LC).astype(jnp.float32)
        packed_level = lane_group + base
        dz_packed = DT * (0.5 / K + (packed_level + 0.5) * (1.0 / (K * K)))

        def halo(f, depths, r):
            raw = jnp.where(low2, PW[f, c, r : r + 8, :], PE[f, c, r : r + 8, :])
            return jnp.where(packed_level < PC[depths, r + 7 : r + 15, :], raw, 0.0)

        us, uc, un = [halo(0, 1, r) for r in range(3)]
        vs, vc, vn = [halo(1, 2, r) for r in range(3)]
        pack_uq = edge_terms(uc, un + us)
        pack_vq = edge_terms(vc, vn + vs)
        pack_cross = jnp.where(at1, uc + un, vc + vs)
        pack_w = weight(halo(2, 0, 1), halo(3, 0, 1), dz_packed)

        cu5 = [CU[r : r + 8, :] - base for r in range(6, 11)]
        cv5 = [CV[r : r + 8, :] - base for r in range(6, 11)]
        cc0, ccn = CC[8:16, :] - base, CC[9:17, :] - base
        held = zero
        for i in range(LC):
            k = c * LC + i
            dz = 0.5 / K + (base + (i + 0.5)) * (1.0 / (K * K))
            uss, us, u, un, unn = [
                jnp.where(cu5[r] > i, X[0, k, r + 6 : r + 14, :], 0.0) for r in range(5)
            ]
            vss, vs, v, vn, vnn = [
                jnp.where(cv5[r] > i, X[1, k, r + 6 : r + 14, :], 0.0) for r in range(5)
            ]
            w = weight(
                jnp.where(cc0 > i, X[2, k, 8:16, :], 0.0),
                jnp.where(cc0 > i, X[3, k, 8:16, :], 0.0),
                DT * dz,
            )
            wn = weight(
                jnp.where(ccn > i, X[2, k, 9:17, :], 0.0),
                jnp.where(ccn > i, X[3, k, 9:17, :], 0.0),
                DT * dz,
            )
            step_e = east(w, unpacked(pack_w, i)) - w
            step_n = wn - w
            cum_e = cum_e + step_e
            cum_n = cum_n + step_n
            cross = unpacked(pack_cross, i)
            uu = u + un
            vv = v + vs
            uu = uu + west(uu, cross)
            vv = vv + east(vv, cross)
            yu, yv = un + us, vn + vs
            far_u = unn + uss + spread_terms(u, yu, unpacked(uc, i), unpacked(pack_uq, i))
            far_v = vnn + vss + spread_terms(v, yv, unpacked(vc, i), unpacked(pack_vq, i))
            u1 = centre_uv * u + (8.0 * DT * NU) * yu + f4 * vv - (cum_e - 0.5 * step_e) - (DT * NU) * far_u
            v1 = centre_uv * v + (8.0 * DT * NU) * yv - f4 * uu - (cum_n - 0.5 * step_n) - (DT * NU) * far_v
            u1 = jnp.where(cu5[2] > i, u1, 0.0)
            v1 = jnp.where(cv5[2] > i, v1, 0.0)
            sum_u = sum_u + u1 * dz
            sum_v = sum_v + v1 * dz
            U1B[k] = u1
            V1X[k, 8:16, :] = v1
            held = jnp.where(lane_group == i, roll(u1, 4 * i + 2), held)
        pu1[c] = held
        v1_copy(c).start()
        return cum_e, cum_n, sum_u, sum_v

    _, _, total_u, total_v = lax.fori_loop(0, NC, momentum, (zero, zero, zero, zero))

    F2[2, 1, 8:16, :] = total_u
    F2[3, 1, 8:16, :] = total_v
    got_total = spread(
        F2.at[pl.ds(2, 2), 1, pl.ds(8, 8), :],
        lambda tile, r: F2.at[pl.ds(2, 2), tile, pl.ds(r, 8), :],
    )
    pu1_copy = wires.copy(pu1, PU1, wires.slots(), 1, 0)
    pu1_copy.start()
    sent.append(pu1_copy)
    for copy in got_start + got_total:
        copy.wait_recv()

    def both(op, *pairs):
        return [op(*xs) for xs in zip(*pairs)]

    u0, v0, u_all, v_all = [list(sides(F2, f)) for f in range(4)]
    open_u = [(x > 0.0).astype(jnp.float32) for x in cu]
    open_v = [(x > 0.0).astype(jnp.float32) for x in cv]
    depth_u = both(depth, cu)
    depth_v = both(depth, cv)
    pull_u = both(lambda o, d: o * d * (DB * GRAVITY), open_u, depth_u)
    pull_v = both(lambda o, d: o * d * (DB * GRAVITY), open_v, depth_v)
    push_u = both(lambda o, a, b: o * ((a - b) * (DB / DT)), open_u, u_all, u0)
    push_v = both(lambda o, a, b: o * ((a - b) * (DB / DT)), open_v, v_all, v0)
    trans_u = both(lambda o, a: o * a, open_u, u0)
    trans_v = both(lambda o, a: o * a, open_v, v0)
    ease = both(lambda o: jnp.where(o, DB, 0.0), ocean)
    level = level0
    run_u = [jnp.zeros((24, LANES), jnp.float32)] * 2
    run_v = run_u
    for _ in range(SUBSTEPS):
        trans_u = both(
            lambda t, p, q, e, h: t + (p - q * (e - h)), trans_u, push_u, pull_u, ring_east(*level), level
        )
        trans_v = both(
            lambda t, p, q, h: t + (p - q * (north24(h) - h)), trans_v, push_v, pull_v, level
        )
        level = both(
            lambda h, e, u, w, v: h - e * ((u - w) + (v - south24(v))),
            level,
            ease,
            trans_u,
            ring_west(*trans_u),
            trans_v,
        )
        run_u = both(jnp.add, run_u, trans_u)
        run_v = both(jnp.add, run_v, trans_v)

    HN[...] = level[0][8:16]
    h_copy = pltpu.make_async_copy(HN, h_out, out_sem.at[4])
    h_copy.start()
    shift_u = both(
        lambda r, a, d, o: (r * (1.0 / SUBSTEPS) - a) / (d + (1.0 - o)), run_u, u_all, depth_u, open_u
    )
    shift_v = (run_v[0] * (1.0 / SUBSTEPS) - v_all[0]) / (depth_v[0] + (1.0 - open_v[0]))
    DV[...] = shift_v
    du = shift_u[0][8:16]
    dv = shift_v[8:16]
    dvs = DV[7:15, :]
    du_west = jnp.broadcast_to(shift_u[1][8:16, LANES - 1 : LANES], (ROWS, LANES))

    a_slot = wires.slots(2 * NC)

    def a_copy(c, up):
        src, dst, dy = (14, 6, 1) if up else (8, 16, -1)
        levels = pl.ds(c * LC, LC)
        return wires.copy(
            AX.at[:, levels, pl.ds(src, 2), :],
            AX.at[:, levels, pl.ds(dst, 2), :],
            a_slot + 2 * c + int(up),
            0,
            dy,
        )

    pu1_copy.wait_recv()

    @pl.loop(0, NC)
    def _(c):
        v1_copy(c).wait_recv()
        base = (c * LC).astype(jnp.float32)
        packed_level = lane_group + base

        u_edge = jnp.where(packed_level < PC[1, 8:16, :], PU1[c] + du_west, 0.0) * (0.5 * DTT)
        edges = []
        for f in (2, 3):
            raw = jnp.where(low2, PW[f, c, 1:9, :], PE[f, c, 1:9, :])
            c_halo = jnp.where(packed_level < PC[0, 8:16, :], raw, 0.0)
            c_own = jnp.where(packed_level < col_own4, pack[f, c], 0.0)
            flux = u_edge * (c_halo + roll(c_own, LANES - 1))
            edges.append(jnp.where(at1, flux, c_halo))

        ccs, cc0, ccn = [CC[r : r + 8, :] - base for r in (7, 8, 9)]
        cu0 = CU[8:16, :] - base
        cvs, cv0 = CV[7:15, :] - base, CV[8:16, :] - base
        held = [zero, zero]
        for i in range(LC):
            k = c * LC + i
            u = jnp.where(cu0 > i, U1B[k] + du, 0.0)
            v = jnp.where(cv0 > i, V1X[k, 8:16, :] + dv, 0.0)
            vs = jnp.where(cvs > i, V1X[k, 7:15, :] + dvs, 0.0) * (0.5 * DTT)
            UN[k] = u
            VN[k] = v
            u = u * (0.5 * DTT)
            v = v * (0.5 * DTT)
            for f in range(2):
                here = jnp.where(cc0 > i, X[2 + f, k, 8:16, :], 0.0)
                north = jnp.where(ccn > i, X[2 + f, k, 9:17, :], 0.0)
                south = jnp.where(ccs > i, X[2 + f, k, 7:15, :], 0.0)
                edge = unpacked(edges[f], i)
                flux_e = u * (here + east(here, edge))
                a = here - (
                    (flux_e - west(flux_e, edge)) + (v * (here + north) - vs * (here + south))
                )
                a = jnp.where(cc0 > i, a, 0.0)
                AX[f, k, 8:16, :] = a
                held[f] = jnp.where(lane_group == i, roll(a, 4 * i + 2), held[f])
        packa[0, c] = held[0]
        packa[1, c] = held[1]

        @pl.when(has_north)
        def _():
            a_copy(c, True).start()

        @pl.when(has_south)
        def _():
            a_copy(c, False).start()

    u_copy = pltpu.make_async_copy(UN, u_out, out_sem.at[0])
    v_copy = pltpu.make_async_copy(VN, v_out, out_sem.at[1])
    got_a = side_packs(
        packa,
        QW.at[:, :, pl.ds(1, 8), :],
        QE.at[:, :, pl.ds(1, 8), :],
        corner_copies(packa, QW, QE),
    )
    u_copy.start()
    v_copy.start()
    for copy in got_a:
        copy.wait_recv()

    south_row = jnp.logical_and(row == 0, jnp.logical_not(has_south))
    north_row = jnp.logical_and(row == ROWS - 1, jnp.logical_not(has_north))

    @pl.loop(0, NC)
    def _(c):
        @pl.when(has_south)
        def _():
            a_copy(c, True).wait_recv()

        @pl.when(has_north)
        def _():
            a_copy(c, False).wait_recv()

        base = (c * LC).astype(jnp.float32)
        cc0 = CC[8:16, :] - base
        near, beyond = [], []
        for f in range(2):
            s, m, n = [
                jnp.where(low2, QW[f, c, r : r + 8, :], QE[f, c, r : r + 8, :]) for r in range(3)
            ]
            y = jnp.where(north_row, 0.0, n) + jnp.where(south_row, 0.0, s)
            near.append(m)
            beyond.append(edge_terms(m, y))
        for i in range(LC):
            k = c * LC + i
            for f, out in ((0, TN), (1, SN)):
                ss, s, a, n, nn = [AX[f, k, r + 6 : r + 14, :] for r in range(5)]
                y = n + s
                far = nn + ss + spread_terms(a, y, unpacked(near[f], i), unpacked(beyond[f], i))
                mixed = centre_ts * a + (8.0 * KAPPA) * y - KAPPA * far
                out[k] = jnp.where(cc0 > i, mixed, 0.0)

    t_copy = pltpu.make_async_copy(TN, t_out, out_sem.at[2])
    s_copy = pltpu.make_async_copy(SN, s_out, out_sem.at[3])
    t_copy.start()
    s_copy.start()

    for copy in sent:
        copy.wait_send()

    @pl.loop(0, NC)
    def _(c):
        v1_copy(c).wait_send()
        for up in (True, False):
            uv_copy(c, up).wait_send()
            ts_copy(c, up).wait_send()

        @pl.when(has_north)
        def _():
            a_copy(c, True).wait_send()

        @pl.when(has_south)
        def _():
            a_copy(c, False).wait_send()

    for copy in (h_copy, u_copy, v_copy, t_copy, s_copy):
        copy.wait()


def per_device(nx, ny, *args):
    tile3 = jax.ShapeDtypeStruct((K, ROWS, LANES), jnp.float32)
    tile2 = jax.ShapeDtypeStruct((ROWS, LANES), jnp.float32)

    def vmem(*shape, dtype=jnp.float32):
        return pltpu.VMEM(shape, dtype)

    return pl.pallas_call(
        functools.partial(kernel, nx, ny),
        out_shape=(tile3, tile3, tile3, tile3, tile2),
        in_specs=[pl.BlockSpec(memory_space=pl.ANY)] * 7,
        out_specs=[pl.BlockSpec(memory_space=pl.ANY)] * 5,
        scratch_shapes=[
            vmem(4, K, 24, LANES),
            vmem(2, 3, 24, LANES),
            vmem(ROWS, LANES, dtype=jnp.int32),
            vmem(ROWS, LANES, dtype=jnp.int32),
            vmem(24, LANES),
            vmem(24, LANES),
            vmem(24, LANES),
            vmem(3, 24, LANES),
            vmem(4, NC, ROWS, LANES),
            vmem(4, NC, 16, LANES),
            vmem(4, NC, 16, LANES),
            vmem(4, 3, 24, LANES),
            vmem(24, LANES),
            vmem(K, ROWS, LANES),
            vmem(K, 16, LANES),
            vmem(NC, ROWS, LANES),
            vmem(NC, ROWS, LANES),
            vmem(2, K, 24, LANES),
            vmem(2, NC, ROWS, LANES),
            vmem(2, NC, 16, LANES),
            vmem(2, NC, 16, LANES),
            vmem(K, ROWS, LANES),
            vmem(K, ROWS, LANES),
            vmem(K, ROWS, LANES),
            vmem(K, ROWS, LANES),
            vmem(ROWS, LANES),
            pltpu.SemaphoreType.DMA((7,)),
            pltpu.SemaphoreType.DMA((N_WIRES,)),
            pltpu.SemaphoreType.DMA((N_WIRES,)),
            pltpu.SemaphoreType.DMA((5,)),
        ],
        compiler_params=pltpu.CompilerParams(
            collective_id=0, has_side_effects=True, vmem_limit_bytes=48 * 1024 * 1024
        ),
    )(*args)


def solution(mesh):
    placed = (P(None, "gy", "gx"),) * 4 + (P("gy", "gx"),) * 3
    return jax.shard_map(
        functools.partial(per_device, mesh.shape["gx"], mesh.shape["gy"]),
        mesh=mesh,
        in_specs=placed,
        out_specs=(P(None, "gy", "gx"),) * 4 + (P("gy", "gx"),),
        check_vma=False,
    )
```

```python
import functools

import jax
import jax.numpy as jnp
from jax import lax
from jax.experimental import pallas as pl
from jax.experimental.pallas import tpu as pltpu
from jax.sharding import PartitionSpec as P

MESH = pl.DeviceIdType.MESH
K = 75
NC = 5
LC = K // NC
SUBSTEPS = 8
ROWS = 8
LANES = 128

DT = 0.4
NU = 0.025
KAPPA = 0.01
DTT = 0.2
GRAVITY = 4.0
DB = DT / SUBSTEPS

AROUND = [(dx, dy) for dy in (-1, 0, 1) for dx in (-1, 0, 1) if (dx, dy) != (0, 0)]
CORNERS = [(dx, dy) for dx, dy in AROUND if dx != 0 and dy != 0]


class Wires:
    def __init__(self, send, recv, gx, gy, nx, ny):
        self.send, self.recv = send, recv
        self.gx, self.gy, self.nx, self.ny = gx, gy, nx, ny
        self.used = 0

    def slots(self, count=1):
        first = self.used
        self.used += count
        return first

    def device(self, dx, dy):
        return (lax.rem(self.gx + dx + self.nx, self.nx), lax.rem(self.gy + dy + self.ny, self.ny))

    def copy(self, src, dst, slot, dx, dy):
        return pltpu.make_async_remote_copy(
            src_ref=src,
            dst_ref=dst,
            send_sem=self.send.at[slot],
            recv_sem=self.recv.at[slot],
            device_id=self.device(dx, dy),
            device_id_type=MESH,
        )


N_WIRES = 128


def kernel(
    nx,
    ny,
    t_in,
    s_in,
    u_in,
    v_in,
    h_in,
    flag_in,
    bottom_in,
    TN,
    SN,
    UN,
    VN,
    HN,
    X,
    D2,
    flag_v,
    bottom_v,
    CU,
    CV,
    CC,
    PC,
    pack,
    PE,
    PW,
    F2,
    DV,
    U1B,
    V1X,
    pu1,
    PU1,
    AX,
    packa,
    QE,
    QW,
    load_sem,
    send_sem,
    recv_sem,
):
    gx, gy = lax.axis_index("gx"), lax.axis_index("gy")
    wires = Wires(send_sem, recv_sem, gx, gy, nx, ny)
    sent = []

    loads = [
        pltpu.make_async_copy(h_in, D2.at[1, 1, pl.ds(8, 8), :], load_sem.at[4]),
        pltpu.make_async_copy(flag_in, flag_v, load_sem.at[5]),
        pltpu.make_async_copy(bottom_in, bottom_v, load_sem.at[6]),
        pltpu.make_async_copy(u_in, X.at[0, :, pl.ds(8, 8), :], load_sem.at[0]),
        pltpu.make_async_copy(v_in, X.at[1, :, pl.ds(8, 8), :], load_sem.at[1]),
        pltpu.make_async_copy(t_in, X.at[2, :, pl.ds(8, 8), :], load_sem.at[2]),
        pltpu.make_async_copy(s_in, X.at[3, :, pl.ds(8, 8), :], load_sem.at[3]),
    ]
    for load in loads:
        load.start()

    barrier = pltpu.get_barrier_semaphore()
    for dx, dy in AROUND:
        pl.semaphore_signal(barrier, inc=1, device_id=wires.device(dx, dy), device_id_type=MESH)

    lane = lax.broadcasted_iota(jnp.int32, (ROWS, LANES), 1)
    lane4 = lax.rem(lane, 4)
    lane_group = lax.div(lane, 4).astype(jnp.float32)
    row = lax.broadcasted_iota(jnp.int32, (ROWS, LANES), 0)
    first, last = lane == 0, lane == LANES - 1
    low2, at1, at2 = lane4 < 2, lane4 == 1, lane4 == 2
    has_south, has_north = gy > 0, gy < ny - 1

    def roll(x, shift):
        return pltpu.roll(x, shift % LANES, 1)

    def east(x, halo):
        return roll(jnp.where(first, halo, x), LANES - 1)

    def west(x, halo):
        return roll(jnp.where(last, halo, x), 1)

    def unpacked(packed, i):
        return roll(packed, LANES - 2 - 4 * i)

    @pl.when(jnp.logical_not(has_south))
    def _():
        AX[:, :, 6:8, :] = jnp.zeros((2, K, 2, LANES), jnp.float32)

    @pl.when(jnp.logical_not(has_north))
    def _():
        AX[:, :, 16:18, :] = jnp.zeros((2, K, 2, LANES), jnp.float32)

    for load in loads[:3]:
        load.wait()
    D2[0, 1, 8:16, :] = (flag_v[...] * bottom_v[...]).astype(jnp.float32)

    pl.semaphore_wait(barrier, len(AROUND))

    def spread(src, dst_of):
        copies = []
        for dx, dy in AROUND:
            copy = wires.copy(src, dst_of(1 - dx, 8 * (1 - dy)), wires.slots(), dx, dy)
            copy.start()
            copies.append(copy)
        sent.extend(copies)
        return copies

    got_d2 = spread(
        D2.at[:, 1, pl.ds(8, 8), :], lambda tile, r: D2.at[:, tile, pl.ds(r, 8), :]
    )

    for load in loads[3:]:
        load.wait()
    uv_slot = wires.slots(2 * NC)
    ts_slot = wires.slots(2 * NC)

    def uv_copy(c, up):
        src, dst, dy = (14, 6, 1) if up else (8, 16, -1)
        levels = pl.ds(c * LC, LC)
        return wires.copy(
            X.at[pl.ds(0, 2), levels, pl.ds(src, 2), :],
            X.at[pl.ds(0, 2), levels, pl.ds(dst, 2), :],
            uv_slot + 2 * c + int(up),
            0,
            dy,
        )

    def ts_copy(c, up):
        src, dst, dy = (15, 7, 1) if up else (8, 16, -1)
        levels = pl.ds(c * LC, LC)
        return wires.copy(
            X.at[pl.ds(2, 2), levels, pl.ds(src, 1), :],
            X.at[pl.ds(2, 2), levels, pl.ds(dst, 1), :],
            ts_slot + 2 * c + int(up),
            0,
            dy,
        )

    @pl.loop(0, NC)
    def _(c):
        for up in (True, False):
            uv_copy(c, up).start()
            ts_copy(c, up).start()

    @pl.loop(0, NC)
    def _(c):
        for f in range(4):
            held = jnp.zeros((ROWS, LANES), jnp.float32)
            for i in range(LC):
                edge = roll(X[f, c * LC + i, 8:16, :], 4 * i + 2)
                held = jnp.where(lane_group == i, edge, held)
            pack[f, c] = held

    got_packs = []

    def side_packs(src, to_east, to_west, corners):
        copies = [
            wires.copy(src, to_east, wires.slots(), 1, 0),
            wires.copy(src, to_west, wires.slots(), -1, 0),
        ]
        for dx, dy, corner_src, corner_dst in corners:
            copies.append(wires.copy(corner_src, corner_dst, wires.slots(), dx, dy))
        for copy in copies:
            copy.start()
        sent.extend(copies)
        return copies

    def corner_copies(src, west_side, east_side):
        out = []
        for dx, dy in CORNERS:
            side = west_side if dx > 0 else east_side
            r_src, r_dst = (7, 0) if dy > 0 else (0, 9)
            out.append(
                (dx, dy, src.at[:, :, pl.ds(r_src, 1), :], side.at[:, :, pl.ds(r_dst, 1), :])
            )
        return out

    uv_pack = pack.at[pl.ds(0, 2)]
    got_packs = side_packs(
        pack,
        PW.at[:, :, pl.ds(1, 8), :],
        PE.at[:, :, pl.ds(1, 8), :],
        corner_copies(uv_pack, PW.at[pl.ds(0, 2)], PE.at[pl.ds(0, 2)]),
    )

    for copy in got_d2:
        copy.wait_recv()
    row24 = lax.broadcasted_iota(jnp.int32, (24, LANES), 0)
    lane24 = lax.broadcasted_iota(jnp.int32, (24, LANES), 1)
    first24, last24 = lane24 == 0, lane24 == LANES - 1
    inside = jnp.logical_and(
        jnp.logical_or(row24 >= 8, has_south), jnp.logical_or(row24 < 16, has_north)
    )

    def ring_east(c, h):
        return (
            roll(jnp.where(first24, h, c), LANES - 1),
            roll(jnp.where(first24, c, h), LANES - 1),
        )

    def ring_west(c, h):
        return (
            roll(jnp.where(last24, h, c), 1),
            roll(jnp.where(last24, c, h), 1),
        )

    def north24(x):
        return pltpu.roll(x, 23, 0)

    def south24(x):
        return pltpu.roll(x, 1, 0)

    def sides(ref, f):
        return ref[f, 1], jnp.where(lane24 < 64, ref[f, 2], ref[f, 0])

    col = [jnp.where(inside, x, 0.0) for x in sides(D2, 0)]
    ocean = [x > 0.0 for x in col]
    level0 = [jnp.where(o, x, 0.0) for o, x in zip(ocean, sides(D2, 1))]
    cu = [jnp.minimum(a, b) for a, b in zip(col, ring_east(*col))]
    cv = [jnp.minimum(a, north24(a)) for a in col]

    def depth(c):
        return c * (0.5 / K + c * (0.5 / (K * K)))

    CC[...] = col[0]
    CU[...] = cu[0]
    CV[...] = cv[0]

    def four(x):
        edge = [jnp.broadcast_to(x[:, l : l + 1], x.shape) for l in (126, 127, 0, 1)]
        l4 = lax.rem(lax.broadcasted_iota(jnp.int32, x.shape, 1), 4)
        return jnp.where(l4 < 2, jnp.where(l4 == 0, edge[0], edge[1]), jnp.where(l4 == 2, edge[2], edge[3]))

    PC[0] = four(col[1])
    PC[1] = four(cu[1])
    PC[2] = four(cv[1])
    col_own4 = four(col[0][8:16])

    def start_sums(c, carry):
        su, sv = carry
        base = (c * LC).astype(jnp.float32)
        cu0, cv0 = CU[8:16, :] - base, CV[8:16, :] - base
        for i in range(LC):
            dz = 0.5 / K + (base + (i + 0.5)) * (1.0 / (K * K))
            su = su + jnp.where(cu0 > i, X[0, c * LC + i, 8:16, :], 0.0) * dz
            sv = sv + jnp.where(cv0 > i, X[1, c * LC + i, 8:16, :], 0.0) * dz
        return su, sv

    zero = jnp.zeros((ROWS, LANES), jnp.float32)
    start_u, start_v = lax.fori_loop(0, NC, start_sums, (zero, zero))
    F2[0, 1, 8:16, :] = start_u
    F2[1, 1, 8:16, :] = start_v
    got_start = spread(
        F2.at[pl.ds(0, 2), 1, pl.ds(8, 8), :],
        lambda tile, r: F2.at[pl.ds(0, 2), tile, pl.ds(r, 8), :],
    )

    for copy in got_packs:
        copy.wait_recv()
    at_wall = jnp.where(
        jnp.logical_or(
            jnp.logical_and(row == 0, jnp.logical_not(has_south)),
            jnp.logical_and(row == ROWS - 1, jnp.logical_not(has_north)),
        ),
        19.0,
        20.0,
    )
    latitude = (row + gy * ROWS).astype(jnp.float32)
    f4 = (0.25 * DT) * (0.2 + 0.3 * (latitude + 0.5) / (ROWS * ny))
    centre_uv = 1.0 - (DT * NU) * at_wall
    centre_ts = 1.0 - KAPPA * at_wall

    v1_slot = wires.slots(NC)

    def v1_copy(c):
        levels = pl.ds(c * LC, LC)
        return wires.copy(
            V1X.at[levels, pl.ds(15, 1), :], V1X.at[levels, pl.ds(7, 1), :], v1_slot + c, 0, 1
        )

    def edge_terms(a, y):
        return (
            2.0 * y
            - 8.0 * a
            + jnp.where(at2, roll(a, LANES - 1), roll(a, 1))
        )

    def spread_terms(a, y, halo_a, halo_q):
        z = 2.0 * y - 8.0 * a
        return east(z + east(a, halo_a), halo_q) + west(z + west(a, halo_a), halo_q)

    def weight(t, s, dz):
        return (0.8 * s - t * (0.2 + 0.05 * t)) * dz

    def momentum(c, carry):
        cum_e, cum_n, sum_u, sum_v = carry
        for up in (True, False):
            uv_copy(c, up).wait_recv()
            ts_copy(c, up).wait_recv()
        base = (c * LC).astype(jnp.float32)
        packed_level = lane_group + base
        dz_packed = DT * (0.5 / K + (packed_level + 0.5) * (1.0 / (K * K)))

        def halo(f, depths, r):
            raw = jnp.where(low2, PW[f, c, r : r + 8, :], PE[f, c, r : r + 8, :])
            return jnp.where(packed_level < PC[depths, r + 7 : r + 15, :], raw, 0.0)

        us, uc, un = [halo(0, 1, r) for r in range(3)]
        vs, vc, vn = [halo(1, 2, r) for r in range(3)]
        pack_uq = edge_terms(uc, un + us)
        pack_vq = edge_terms(vc, vn + vs)
        pack_cross = jnp.where(at1, uc + un, vc + vs)
        pack_w = weight(halo(2, 0, 1), halo(3, 0, 1), dz_packed)

        cu5 = [CU[r : r + 8, :] - base for r in range(6, 11)]
        cv5 = [CV[r : r + 8, :] - base for r in range(6, 11)]
        cc0, ccn = CC[8:16, :] - base, CC[9:17, :] - base
        held = zero
        for i in range(LC):
            k = c * LC + i
            dz = 0.5 / K + (base + (i + 0.5)) * (1.0 / (K * K))
            uss, us, u, un, unn = [
                jnp.where(cu5[r] > i, X[0, k, r + 6 : r + 14, :], 0.0) for r in range(5)
            ]
            vss, vs, v, vn, vnn = [
                jnp.where(cv5[r] > i, X[1, k, r + 6 : r + 14, :], 0.0) for r in range(5)
            ]
            w = weight(
                jnp.where(cc0 > i, X[2, k, 8:16, :], 0.0),
                jnp.where(cc0 > i, X[3, k, 8:16, :], 0.0),
                DT * dz,
            )
            wn = weight(
                jnp.where(ccn > i, X[2, k, 9:17, :], 0.0),
                jnp.where(ccn > i, X[3, k, 9:17, :], 0.0),
                DT * dz,
            )
            step_e = east(w, unpacked(pack_w, i)) - w
            step_n = wn - w
            cum_e = cum_e + step_e
            cum_n = cum_n + step_n
            cross = unpacked(pack_cross, i)
            uu = u + un
            vv = v + vs
            uu = uu + west(uu, cross)
            vv = vv + east(vv, cross)
            yu, yv = un + us, vn + vs
            far_u = unn + uss + spread_terms(u, yu, unpacked(uc, i), unpacked(pack_uq, i))
            far_v = vnn + vss + spread_terms(v, yv, unpacked(vc, i), unpacked(pack_vq, i))
            u1 = centre_uv * u + (8.0 * DT * NU) * yu + f4 * vv - (cum_e - 0.5 * step_e) - (DT * NU) * far_u
            v1 = centre_uv * v + (8.0 * DT * NU) * yv - f4 * uu - (cum_n - 0.5 * step_n) - (DT * NU) * far_v
            u1 = jnp.where(cu5[2] > i, u1, 0.0)
            v1 = jnp.where(cv5[2] > i, v1, 0.0)
            sum_u = sum_u + u1 * dz
            sum_v = sum_v + v1 * dz
            U1B[k] = u1
            V1X[k, 8:16, :] = v1
            held = jnp.where(lane_group == i, roll(u1, 4 * i + 2), held)
        pu1[c] = held
        v1_copy(c).start()
        return cum_e, cum_n, sum_u, sum_v

    _, _, total_u, total_v = lax.fori_loop(0, NC, momentum, (zero, zero, zero, zero))

    F2[2, 1, 8:16, :] = total_u
    F2[3, 1, 8:16, :] = total_v
    got_total = spread(
        F2.at[pl.ds(2, 2), 1, pl.ds(8, 8), :],
        lambda tile, r: F2.at[pl.ds(2, 2), tile, pl.ds(r, 8), :],
    )
    pu1_copy = wires.copy(pu1, PU1, wires.slots(), 1, 0)
    pu1_copy.start()
    sent.append(pu1_copy)
    for copy in got_start + got_total:
        copy.wait_recv()

    def both(op, *pairs):
        return [op(*xs) for xs in zip(*pairs)]

    u0, v0, u_all, v_all = [list(sides(F2, f)) for f in range(4)]
    open_u = [(x > 0.0).astype(jnp.float32) for x in cu]
    open_v = [(x > 0.0).astype(jnp.float32) for x in cv]
    depth_u = both(depth, cu)
    depth_v = both(depth, cv)
    pull_u = both(lambda o, d: o * d * (DB * GRAVITY), open_u, depth_u)
    pull_v = both(lambda o, d: o * d * (DB * GRAVITY), open_v, depth_v)
    push_u = both(lambda o, a, b: o * ((a - b) * (DB / DT)), open_u, u_all, u0)
    push_v = both(lambda o, a, b: o * ((a - b) * (DB / DT)), open_v, v_all, v0)
    trans_u = both(lambda o, a: o * a, open_u, u0)
    trans_v = both(lambda o, a: o * a, open_v, v0)
    ease = both(lambda o: jnp.where(o, DB, 0.0), ocean)
    level = level0
    run_u = [jnp.zeros((24, LANES), jnp.float32)] * 2
    run_v = run_u
    for _ in range(SUBSTEPS):
        trans_u = both(
            lambda t, p, q, e, h: t + (p - q * (e - h)), trans_u, push_u, pull_u, ring_east(*level), level
        )
        trans_v = both(
            lambda t, p, q, h: t + (p - q * (north24(h) - h)), trans_v, push_v, pull_v, level
        )
        level = both(
            lambda h, e, u, w, v: h - e * ((u - w) + (v - south24(v))),
            level,
            ease,
            trans_u,
            ring_west(*trans_u),
            trans_v,
        )
        run_u = both(jnp.add, run_u, trans_u)
        run_v = both(jnp.add, run_v, trans_v)

    HN[...] = level[0][8:16]
    shift_u = both(
        lambda r, a, d, o: (r * (1.0 / SUBSTEPS) - a) / (d + (1.0 - o)), run_u, u_all, depth_u, open_u
    )
    shift_v = (run_v[0] * (1.0 / SUBSTEPS) - v_all[0]) / (depth_v[0] + (1.0 - open_v[0]))
    DV[...] = shift_v
    du = shift_u[0][8:16]
    dv = shift_v[8:16]
    dvs = DV[7:15, :]
    du_west = jnp.broadcast_to(shift_u[1][8:16, LANES - 1 : LANES], (ROWS, LANES))

    a_slot = wires.slots(2 * NC)

    def a_copy(c, up):
        src, dst, dy = (14, 6, 1) if up else (8, 16, -1)
        levels = pl.ds(c * LC, LC)
        return wires.copy(
            AX.at[:, levels, pl.ds(src, 2), :],
            AX.at[:, levels, pl.ds(dst, 2), :],
            a_slot + 2 * c + int(up),
            0,
            dy,
        )

    pu1_copy.wait_recv()

    @pl.loop(0, NC)
    def _(c):
        v1_copy(c).wait_recv()
        base = (c * LC).astype(jnp.float32)
        packed_level = lane_group + base

        u_edge = jnp.where(packed_level < PC[1, 8:16, :], PU1[c] + du_west, 0.0) * (0.5 * DTT)
        edges = []
        for f in (2, 3):
            raw = jnp.where(low2, PW[f, c, 1:9, :], PE[f, c, 1:9, :])
            c_halo = jnp.where(packed_level < PC[0, 8:16, :], raw, 0.0)
            c_own = jnp.where(packed_level < col_own4, pack[f, c], 0.0)
            flux = u_edge * (c_halo + roll(c_own, LANES - 1))
            edges.append(jnp.where(at1, flux, c_halo))

        ccs, cc0, ccn = [CC[r : r + 8, :] - base for r in (7, 8, 9)]
        cu0 = CU[8:16, :] - base
        cvs, cv0 = CV[7:15, :] - base, CV[8:16, :] - base
        held = [zero, zero]
        for i in range(LC):
            k = c * LC + i
            u = jnp.where(cu0 > i, U1B[k] + du, 0.0)
            v = jnp.where(cv0 > i, V1X[k, 8:16, :] + dv, 0.0)
            vs = jnp.where(cvs > i, V1X[k, 7:15, :] + dvs, 0.0) * (0.5 * DTT)
            UN[k] = u
            VN[k] = v
            u = u * (0.5 * DTT)
            v = v * (0.5 * DTT)
            for f in range(2):
                here = jnp.where(cc0 > i, X[2 + f, k, 8:16, :], 0.0)
                north = jnp.where(ccn > i, X[2 + f, k, 9:17, :], 0.0)
                south = jnp.where(ccs > i, X[2 + f, k, 7:15, :], 0.0)
                edge = unpacked(edges[f], i)
                flux_e = u * (here + east(here, edge))
                a = here - (
                    (flux_e - west(flux_e, edge)) + (v * (here + north) - vs * (here + south))
                )
                a = jnp.where(cc0 > i, a, 0.0)
                AX[f, k, 8:16, :] = a
                held[f] = jnp.where(lane_group == i, roll(a, 4 * i + 2), held[f])
        packa[0, c] = held[0]
        packa[1, c] = held[1]

        @pl.when(has_north)
        def _():
            a_copy(c, True).start()

        @pl.when(has_south)
        def _():
            a_copy(c, False).start()

    got_a = side_packs(
        packa,
        QW.at[:, :, pl.ds(1, 8), :],
        QE.at[:, :, pl.ds(1, 8), :],
        corner_copies(packa, QW, QE),
    )
    for copy in got_a:
        copy.wait_recv()

    south_row = jnp.logical_and(row == 0, jnp.logical_not(has_south))
    north_row = jnp.logical_and(row == ROWS - 1, jnp.logical_not(has_north))

    @pl.loop(0, NC)
    def _(c):
        @pl.when(has_south)
        def _():
            a_copy(c, True).wait_recv()

        @pl.when(has_north)
        def _():
            a_copy(c, False).wait_recv()

        base = (c * LC).astype(jnp.float32)
        cc0 = CC[8:16, :] - base
        near, beyond = [], []
        for f in range(2):
            s, m, n = [
                jnp.where(low2, QW[f, c, r : r + 8, :], QE[f, c, r : r + 8, :]) for r in range(3)
            ]
            y = jnp.where(north_row, 0.0, n) + jnp.where(south_row, 0.0, s)
            near.append(m)
            beyond.append(edge_terms(m, y))
        for i in range(LC):
            k = c * LC + i
            for f, out in ((0, TN), (1, SN)):
                ss, s, a, n, nn = [AX[f, k, r + 6 : r + 14, :] for r in range(5)]
                y = n + s
                far = nn + ss + spread_terms(a, y, unpacked(near[f], i), unpacked(beyond[f], i))
                mixed = centre_ts * a + (8.0 * KAPPA) * y - KAPPA * far
                out[k] = jnp.where(cc0 > i, mixed, 0.0)

    for copy in sent:
        copy.wait_send()

    @pl.loop(0, NC)
    def _(c):
        v1_copy(c).wait_send()
        for up in (True, False):
            uv_copy(c, up).wait_send()
            ts_copy(c, up).wait_send()

        @pl.when(has_north)
        def _():
            a_copy(c, True).wait_send()

        @pl.when(has_south)
        def _():
            a_copy(c, False).wait_send()


def per_device(nx, ny, *args):
    tile3 = jax.ShapeDtypeStruct((K, ROWS, LANES), jnp.float32)
    tile2 = jax.ShapeDtypeStruct((ROWS, LANES), jnp.float32)

    def vmem(*shape, dtype=jnp.float32):
        return pltpu.VMEM(shape, dtype)

    args = [pltpu.with_memory_space_constraint(x, pltpu.HBM) for x in args]
    held = pl.pallas_call(
        functools.partial(kernel, nx, ny),
        out_shape=tuple(pltpu.VMEM(x.shape, x.dtype) for x in (tile3, tile3, tile3, tile3, tile2)),
        in_specs=[pl.BlockSpec(memory_space=pltpu.HBM)] * 7,
        out_specs=[pl.BlockSpec(memory_space=pltpu.VMEM)] * 5,
        scratch_shapes=[
            vmem(4, K, 24, LANES),
            vmem(2, 3, 24, LANES),
            vmem(ROWS, LANES, dtype=jnp.int32),
            vmem(ROWS, LANES, dtype=jnp.int32),
            vmem(24, LANES),
            vmem(24, LANES),
            vmem(24, LANES),
            vmem(3, 24, LANES),
            vmem(4, NC, ROWS, LANES),
            vmem(4, NC, 16, LANES),
            vmem(4, NC, 16, LANES),
            vmem(4, 3, 24, LANES),
            vmem(24, LANES),
            vmem(K, ROWS, LANES),
            vmem(K, 16, LANES),
            vmem(NC, ROWS, LANES),
            vmem(NC, ROWS, LANES),
            vmem(2, K, 24, LANES),
            vmem(2, NC, ROWS, LANES),
            vmem(2, NC, 16, LANES),
            vmem(2, NC, 16, LANES),
            pltpu.SemaphoreType.DMA((7,)),
            pltpu.SemaphoreType.DMA((N_WIRES,)),
            pltpu.SemaphoreType.DMA((N_WIRES,)),
        ],
        compiler_params=pltpu.CompilerParams(
            collective_id=0, has_side_effects=True, vmem_limit_bytes=24 * 1024 * 1024
        ),
    )(*args)
    return pl.pallas_call(
        write_out,
        out_shape=(tile3, tile3, tile3, tile3, tile2),
        in_specs=[pl.BlockSpec(memory_space=pltpu.VMEM)] * 5,
        out_specs=[pl.BlockSpec(memory_space=pltpu.HBM)] * 5,
        scratch_shapes=[pltpu.SemaphoreType.DMA((5,))],
        compiler_params=pltpu.CompilerParams(vmem_limit_bytes=8 * 1024 * 1024),
    )(*held)


def write_out(*refs):
    copies = [pltpu.make_async_copy(refs[i], refs[5 + i], refs[10].at[i]) for i in range(5)]
    for copy in copies:
        copy.start()
    for copy in copies:
        copy.wait()


def solution(mesh):
    placed = (P(None, "gy", "gx"),) * 4 + (P("gy", "gx"),) * 3
    return jax.shard_map(
        functools.partial(per_device, mesh.shape["gx"], mesh.shape["gy"]),
        mesh=mesh,
        in_specs=placed,
        out_specs=(P(None, "gy", "gx"),) * 4 + (P("gy", "gx"),),
        check_vma=False,
    )
```

```python
import functools

import jax
import jax.numpy as jnp
from jax import lax
from jax.experimental import pallas as pl
from jax.experimental.pallas import tpu as pltpu
from jax.sharding import PartitionSpec as P

MESH = pl.DeviceIdType.MESH
K = 75
NC = 5
LC = K // NC
SUBSTEPS = 8
ROWS = 8
LANES = 128

DT = 0.4
NU = 0.025
KAPPA = 0.01
DTT = 0.2
GRAVITY = 4.0
DB = DT / SUBSTEPS

AROUND = [(dx, dy) for dy in (-1, 0, 1) for dx in (-1, 0, 1) if (dx, dy) != (0, 0)]
(G_2D, G_UV, G_W, G_SIDE, G_CORNER, G_POLE, G_TS, G_SUM, G_SIDE1, G_CORNER1, G_V1, G_UP, G_DOWN, G_UP1, G_DOWN1) = range(15)
GROUPS = 15


def kernel(
    nx,
    ny,
    t_in,
    s_in,
    u_in,
    v_in,
    h_in,
    flag_in,
    bottom_in,
    TN,
    SN,
    UN,
    VN,
    HN,
    X,
    WX,
    D2,
    flag_v,
    bottom_v,
    CC,
    CU,
    CV,
    SC,
    SU,
    SV,
    pack,
    PE,
    PW,
    F2,
    DV,
    DP,
    U1B,
    V1X,
    pack1,
    P1E,
    P1W,
    AX,
    AD,
    load_sem,
    send_sem,
    recv_sem,
):
    gx, gy = lax.axis_index("gx"), lax.axis_index("gy")

    def device(dx, dy):
        return (lax.rem(gx + dx + nx, nx), lax.rem(gy + dy + ny, ny))

    def send(group, src, dst, dx, dy):
        pltpu.make_async_remote_copy(
            src_ref=src,
            dst_ref=dst,
            send_sem=send_sem.at[group],
            recv_sem=recv_sem.at[group],
            device_id=device(dx, dy),
            device_id_type=MESH,
        ).start()

    def received(group, size):
        pltpu.make_async_copy(size, size, recv_sem.at[group]).wait()

    def left(group, size):
        pltpu.make_async_copy(size, size, send_sem.at[group]).wait()

    loads = [
        pltpu.make_async_copy(flag_in, flag_v, load_sem.at[5]),
        pltpu.make_async_copy(bottom_in, bottom_v, load_sem.at[6]),
        pltpu.make_async_copy(h_in, D2.at[1, 1, pl.ds(8, 8), :], load_sem.at[4]),
        pltpu.make_async_copy(u_in, X.at[0, :, pl.ds(8, 8), :], load_sem.at[0]),
        pltpu.make_async_copy(v_in, X.at[1, :, pl.ds(8, 8), :], load_sem.at[1]),
        pltpu.make_async_copy(t_in, X.at[2, :, pl.ds(8, 8), :], load_sem.at[2]),
        pltpu.make_async_copy(s_in, X.at[3, :, pl.ds(8, 8), :], load_sem.at[3]),
    ]
    for load in loads:
        load.start()

    barrier = pltpu.get_barrier_semaphore()
    for dx, dy in AROUND:
        pl.semaphore_signal(barrier, inc=1, device_id=device(dx, dy), device_id_type=MESH)

    lane = lax.broadcasted_iota(jnp.int32, (ROWS, LANES), 1)
    lane8 = lax.rem(lane, 8)
    slot = lax.div(lane, 8).astype(jnp.float32)
    row = lax.broadcasted_iota(jnp.int32, (ROWS, LANES), 0)
    first, last = lane == 0, lane == LANES - 1
    edge4 = jnp.logical_or(lane < 2, lane >= LANES - 2)
    western, at3, at4 = lane8 < 4, lane8 == 3, lane8 == 4
    has_south, has_north = gy > 0, gy < ny - 1
    zero = jnp.zeros((ROWS, LANES), jnp.float32)

    def roll(x, shift):
        return pltpu.roll(x, shift % LANES, 1)

    def packed(x, i):
        return roll(x, 8 * i + 4)

    def unpacked(x, i):
        return roll(x, LANES - 4 - 8 * i)

    def in_slots(x, lanes):
        l8 = lax.rem(lax.broadcasted_iota(jnp.int32, x.shape, 1), 8)
        out = None
        for l in lanes:
            column = jnp.broadcast_to(x[:, l : l + 1], x.shape)
            out = column if out is None else jnp.where(l8 == (l + 4) % LANES, column, out)
        return out

    @pl.when(jnp.logical_not(has_south))
    def _():
        AD[:, :, 0:1, :] = jnp.zeros((2, NC, 1, LANES), jnp.float32)

        @pl.loop(0, K)
        def _(k):
            for f in range(2):
                AX[f, k, 6:8, :] = jnp.zeros((2, LANES), jnp.float32)

    @pl.when(jnp.logical_not(has_north))
    def _():
        AD[:, :, 9:10, :] = jnp.zeros((2, NC, 1, LANES), jnp.float32)

        @pl.loop(0, K)
        def _(k):
            for f in range(2):
                AX[f, k, 16:18, :] = jnp.zeros((2, LANES), jnp.float32)

    for load in loads[:3]:
        load.wait()
    own = (flag_v[...] * bottom_v[...]).astype(jnp.float32)
    D2[0, 1, 8:16, :] = own
    D2[2, 1, 8:16, :] = in_slots(own, (124, 125, 126, 127, 0, 1, 2, 3))

    pl.semaphore_wait(barrier, len(AROUND))

    for dx, dy in AROUND:
        send(
            G_2D,
            D2.at[:, 1, pl.ds(8, 8), :],
            D2.at[:, 1 - dx, pl.ds(8 * (1 - dy), 8), :],
            dx,
            dy,
        )

    def rows(group, fields, count, dy):
        src, dst = (16 - count, 8 - count) if dy > 0 else (8, 16)
        send(
            group,
            X.at[fields, :, pl.ds(src, count), :],
            X.at[fields, :, pl.ds(dst, count), :],
            0,
            dy,
        )

    for load in loads[3:]:
        load.wait()
    for dy in (1, -1):
        rows(G_UV, pl.ds(0, 2), 2, dy)

    def weight(t, s, dz):
        return (0.8 * s - t * (0.2 + 0.05 * t)) * dz

    def thickness(base, i):
        return 0.5 / K + (base + (i + 0.5)) * (1.0 / (K * K))

    @pl.loop(0, NC)
    def _(c):
        base = (c * LC).astype(jnp.float32)
        depth = D2[0, 1, 8:16, :] - base
        held = [zero] * 5
        for i in range(LC):
            k = c * LC + i
            u, v, t, s = [X[f, k, 8:16, :] for f in range(4)]
            w = jnp.where(depth > i, weight(t, s, DT * thickness(base, i)), 0.0)
            WX[k, 0:8, :] = w
            for n, x in enumerate((u, v, w, t, s)):
                held[n] = jnp.where(slot == i, packed(x, i), held[n])
        for n in range(5):
            pack[n, c, 1:9, :] = held[n]

    for dx in (1, -1):
        side = PW if dx > 0 else PE
        send(G_SIDE, pack.at[:, :, pl.ds(1, 8), :], side.at[:, :, pl.ds(1, 8), :], dx, 0)
    for dx in (1, -1):
        for dy in (1, -1):
            side = PW if dx > 0 else PE
            src, dst = (8, 0) if dy > 0 else (1, 9)
            send(
                G_CORNER, pack.at[:, :, pl.ds(src, 1), :], side.at[:, :, pl.ds(dst, 1), :], dx, dy
            )
    for dy in (1, -1):
        src, dst = (8, 0) if dy > 0 else (1, 9)
        uv = pl.ds(0, 2)
        send(G_POLE, pack.at[uv, :, pl.ds(src, 1), :], pack.at[uv, :, pl.ds(dst, 1), :], 0, dy)
    send(G_W, WX.at[:, pl.ds(0, 1), :], WX.at[:, pl.ds(8, 1), :], 0, -1)
    for dy in (1, -1):
        rows(G_TS, pl.ds(2, 2), 1, dy)

    size_2d = X.at[0, pl.ds(0, 24), pl.ds(0, 8), :]
    size_uv = X.at[pl.ds(0, 2), :, pl.ds(0, 4), :]
    size_w = X.at[0, :, pl.ds(0, 1), :]
    size_side = PE.at[:, :, pl.ds(0, 16), :]
    size_corner = PE.at[:, :, pl.ds(0, 4), :]
    size_pole = PE.at[pl.ds(0, 2), :, pl.ds(0, 2), :]
    size_ts = X.at[pl.ds(0, 2), :, pl.ds(0, 2), :]
    size_sum = X.at[0, pl.ds(0, 32), pl.ds(0, 8), :]
    size_side1 = P1E.at[:, :, pl.ds(0, 16), :]
    size_corner1 = P1E.at[0, :, pl.ds(0, 2), :]
    size_v1 = V1X.at[:, pl.ds(0, 1), :]
    size_a = X.at[pl.ds(0, 2), :, pl.ds(0, 2), :]
    size_ad = AD.at[:, :, pl.ds(0, 1), :]

    received(G_2D, size_2d)
    row24 = lax.broadcasted_iota(jnp.int32, (24, LANES), 0)
    lane24 = lax.broadcasted_iota(jnp.int32, (24, LANES), 1)
    slot24 = lax.rem(lane24, 8)
    first24, last24 = lane24 == 0, lane24 == LANES - 1
    inside = jnp.logical_and(
        jnp.logical_or(row24 >= 8, has_south), jnp.logical_or(row24 < 16, has_north)
    )

    def ring_east(c, h, seam=first24):
        return (
            roll(jnp.where(seam, h, c), LANES - 1),
            roll(jnp.where(seam, c, h), LANES - 1),
        )

    def ring_west(c, h):
        return (
            roll(jnp.where(last24, h, c), 1),
            roll(jnp.where(last24, c, h), 1),
        )

    def north24(x):
        return pltpu.roll(x, 23, 0)

    def south24(x):
        return pltpu.roll(x, 1, 0)

    def sides(ref, f):
        return ref[f, 1], jnp.where(lane24 < 64, ref[f, 2], ref[f, 0])

    col = [jnp.where(inside, x, 0.0) for x in sides(D2, 0)]
    ocean = [x > 0.0 for x in col]
    cu = [jnp.minimum(a, b) for a, b in zip(col, ring_east(*col))]
    cv = [jnp.minimum(a, north24(a)) for a in col]
    CC[...] = col[0]
    CU[...] = cu[0]
    CV[...] = cv[0]
    edge_col = [
        jnp.where(inside, x, 0.0)
        for x in (jnp.where(slot24 < 4, D2[2, 0], D2[2, 2]), D2[2, 1])
    ]
    edge_cu = [jnp.minimum(a, b) for a, b in zip(edge_col, ring_east(*edge_col, slot24 == 4))]
    for n in range(2):
        SC[n] = edge_col[n]
        SU[n] = edge_cu[n]
        SV[n] = jnp.minimum(edge_col[n], north24(edge_col[n]))

    at_wall = jnp.where(
        jnp.logical_or(
            jnp.logical_and(row == 0, jnp.logical_not(has_south)),
            jnp.logical_and(row == ROWS - 1, jnp.logical_not(has_north)),
        ),
        19.0,
        20.0,
    )
    latitude = (row + gy * ROWS).astype(jnp.float32)
    f4 = (0.25 * DT) * (0.2 + 0.3 * (latitude + 0.5) / (ROWS * ny))
    centre_uv = 1.0 - (DT * NU) * at_wall
    centre_ts = 1.0 - KAPPA * at_wall

    received(G_UV, size_uv)
    left(G_UV, size_uv)

    @pl.loop(0, NC)
    def _(c):
        base = (c * LC).astype(jnp.float32)
        for f, depths in ((0, CU), (1, CV)):
            low, high = depths[6:14, :] - base, depths[10:18, :] - base
            for i in range(LC):
                k = c * LC + i
                a = jnp.where(low > i, X[f, k, 6:14, :], 0.0)
                b = jnp.where(high > i, X[f, k, 10:18, :], 0.0)
                X[f, k, 6:14, :] = a
                X[f, k, 10:18, :] = b

    received(G_W, size_w)
    received(G_SIDE, size_side)
    received(G_CORNER, size_corner)
    received(G_POLE, size_pole)

    def edge_far(d, y):
        z = 2.0 * y - 8.0 * d
        return jnp.where(western, roll(d, -2), roll(d, 2)) + jnp.where(
            at3, roll(z, -1), jnp.where(at4, roll(z, 1), 0.0)
        )

    def far(a, y, yy):
        z = 2.0 * y - 8.0 * a
        return yy + roll(z + roll(a, -1), -1) + roll(z + roll(a, 1), 1)

    def momentum(c, carry):
        cum_e, cum_n, edge_cum, sum_u0, sum_v0, sum_u, sum_v = carry
        base = (c * LC).astype(jnp.float32)
        level = slot + base

        def excess(f, depths, r):
            beyond = jnp.where(western, PW[f, c, r : r + 8, :], PE[f, c, r : r + 8, :])
            beyond = jnp.where(level < depths[0, r + 7 : r + 15, :], beyond, 0.0)
            return beyond - jnp.where(
                level < depths[1, r + 7 : r + 15, :], pack[f, c, r : r + 8, :], 0.0
            )

        du_s, du, du_n = [excess(0, SU, r) for r in range(3)]
        dv_s, dv, dv_n = [excess(1, SV, r) for r in range(3)]
        dw = jnp.where(western, PW[2, c, 1:9, :], PE[2, c, 1:9, :]) - pack[2, c, 1:9, :]
        dw = jnp.where(at3, roll(dw, -1), 0.0)
        run = dw
        for shift in (8, 16, 32, 64):
            run = run + jnp.where(lane >= shift, roll(run, shift), 0.0)
        run = run + edge_cum
        edge_cum = jnp.broadcast_to(run[:, 8 * LC - 5 : 8 * LC - 4], run.shape)
        edge_u = (
            jnp.where(at3, f4 * roll(dv + dv_s, -1) - run + 0.5 * dw, 0.0)
            - (DT * NU) * edge_far(du, du_n + du_s)
        )
        edge_v = (
            jnp.where(at4, -f4 * roll(du + du_n, 1), 0.0)
            - (DT * NU) * edge_far(dv, dv_n + dv_s)
        )

        cu0, cv0 = CU[8:16, :] - base, CV[8:16, :] - base
        held_u = held_v = zero
        for i in range(LC):
            k = c * LC + i
            dz = thickness(base, i)
            uss, us, u, un, unn = [X[0, k, r : r + 8, :] for r in range(6, 11)]
            vss, vs, v, vn, vnn = [X[1, k, r : r + 8, :] for r in range(6, 11)]
            w, wn = WX[k, 0:8, :], WX[k, 1:9, :]
            step_e = roll(w, -1) - w
            step_n = wn - w
            cum_e = cum_e + step_e
            cum_n = cum_n + step_n
            uu = u + un
            vv = v + vs
            uu = uu + roll(uu, 1)
            vv = vv + roll(vv, -1)
            yu, yv = un + us, vn + vs
            u1 = (
                centre_uv * u
                + f4 * vv
                - (cum_e - 0.5 * step_e)
                - (DT * NU) * (far(u, yu, unn + uss) - 8.0 * yu)
                + jnp.where(edge4, unpacked(edge_u, i), 0.0)
            )
            v1 = (
                centre_uv * v
                - f4 * uu
                - (cum_n - 0.5 * step_n)
                - (DT * NU) * (far(v, yv, vnn + vss) - 8.0 * yv)
                + jnp.where(edge4, unpacked(edge_v, i), 0.0)
            )
            u1 = jnp.where(cu0 > i, u1, 0.0)
            v1 = jnp.where(cv0 > i, v1, 0.0)
            sum_u0 = sum_u0 + u * dz
            sum_v0 = sum_v0 + v * dz
            sum_u = sum_u + u1 * dz
            sum_v = sum_v + v1 * dz
            U1B[k] = u1
            V1X[k, 8:16, :] = v1
            held_u = jnp.where(slot == i, packed(u1, i), held_u)
            held_v = jnp.where(slot == i, packed(v1, i), held_v)
        pack1[0, c] = held_u
        pack1[1, c] = held_v
        return cum_e, cum_n, edge_cum, sum_u0, sum_v0, sum_u, sum_v

    sums = lax.fori_loop(0, NC, momentum, (zero,) * 7)[3:]

    for n in range(4):
        F2[n, 1, 8:16, :] = sums[n]
    for dx, dy in AROUND:
        send(
            G_SUM,
            F2.at[:, 1, pl.ds(8, 8), :],
            F2.at[:, 1 - dx, pl.ds(8 * (1 - dy), 8), :],
            dx,
            dy,
        )
    for dx in (1, -1):
        side = P1W if dx > 0 else P1E
        send(G_SIDE1, pack1, side.at[:, :, pl.ds(1, 8), :], dx, 0)
        send(G_CORNER1, pack1.at[1, :, pl.ds(7, 1), :], side.at[1, :, pl.ds(0, 1), :], dx, 1)
    send(G_V1, V1X.at[:, pl.ds(15, 1), :], V1X.at[:, pl.ds(7, 1), :], 0, 1)

    left(G_2D, size_2d)
    left(G_W, size_w)
    left(G_SIDE, size_side)
    left(G_CORNER, size_corner)
    left(G_POLE, size_pole)
    left(G_TS, size_ts)
    received(G_TS, size_ts)

    @pl.loop(0, NC)
    def _(c):
        base = (c * LC).astype(jnp.float32)
        low, high = CC[7:15, :] - base, CC[9:17, :] - base
        for f in (2, 3):
            for i in range(LC):
                k = c * LC + i
                a = jnp.where(low > i, X[f, k, 7:15, :], 0.0)
                b = jnp.where(high > i, X[f, k, 9:17, :], 0.0)
                X[f, k, 7:15, :] = a
                X[f, k, 9:17, :] = b

    def both(op, *pairs):
        return [op(*xs) for xs in zip(*pairs)]

    def depth_of(c):
        return c * (0.5 / K + c * (0.5 / (K * K)))

    open_u = [(x > 0.0).astype(jnp.float32) for x in cu]
    open_v = [(x > 0.0).astype(jnp.float32) for x in cv]
    depth_u = both(depth_of, cu)
    depth_v = both(depth_of, cv)
    pull_u = both(lambda o, d: o * d * (DB * GRAVITY), open_u, depth_u)
    pull_v = both(lambda o, d: o * d * (DB * GRAVITY), open_v, depth_v)
    ease = both(lambda o: jnp.where(o, DB, 0.0), ocean)
    level = [jnp.where(o, x, 0.0) for o, x in zip(ocean, sides(D2, 1))]

    received(G_SUM, size_sum)
    u0, v0, u_all, v_all = [list(sides(F2, f)) for f in range(4)]
    push_u = both(lambda o, a, b: o * ((a - b) * (DB / DT)), open_u, u_all, u0)
    push_v = both(lambda o, a, b: o * ((a - b) * (DB / DT)), open_v, v_all, v0)
    trans_u = both(lambda o, a: o * a, open_u, u0)
    trans_v = both(lambda o, a: o * a, open_v, v0)
    run_u = [jnp.zeros((24, LANES), jnp.float32)] * 2
    run_v = run_u

    def substep(_, state):
        level, trans_u, trans_v, run_u, run_v = state
        trans_u = both(
            lambda t, p, q, e, h: t + (p - q * (e - h)),
            trans_u,
            push_u,
            pull_u,
            ring_east(*level),
            level,
        )
        trans_v = both(
            lambda t, p, q, h: t + (p - q * (north24(h) - h)), trans_v, push_v, pull_v, level
        )
        level = both(
            lambda h, e, u, w, v: h - e * ((u - w) + (v - south24(v))),
            level,
            ease,
            trans_u,
            ring_west(*trans_u),
            trans_v,
        )
        return level, trans_u, trans_v, both(jnp.add, run_u, trans_u), both(jnp.add, run_v, trans_v)

    state = level, trans_u, trans_v, run_u, run_v
    for n in range(SUBSTEPS):
        state = substep(n, state)
    level, _, _, run_u, run_v = state

    HN[...] = level[0][8:16]

    def shift(r, a, d, o):
        return (r * (1.0 / SUBSTEPS) - a) / (d + (1.0 - o))

    shift_u = both(shift, run_u, u_all, depth_u, open_u)
    shift_v = both(shift, run_v, v_all, depth_v, open_v)
    DV[0] = shift_v[0]
    DV[1] = shift_v[1]
    du, dv, dvs = shift_u[0][8:16], shift_v[0][8:16], DV[0, 7:15, :]
    DP[0] = in_slots(shift_u[1][8:16], (125, 126, 127, 0, 1))
    DP[1] = in_slots(DV[1, 8:16, :], (126, 127, 0, 1))
    DP[2] = in_slots(DV[1, 7:15, :], (126, 127, 0, 1))
    DP[3] = jnp.broadcast_to(du[:, LANES - 1 :], du.shape)

    received(G_SIDE1, size_side1)
    received(G_CORNER1, size_corner1)
    received(G_V1, size_v1)
    half = 0.5 * DTT

    @pl.loop(0, NC)
    def _(c):
        base = (c * LC).astype(jnp.float32)
        level = slot + base

        def beyond(west, east, f, r):
            return jnp.where(western, west[f, c, r : r + 8, :], east[f, c, r : r + 8, :])

        edge_u = jnp.where(level < SU[0, 8:16, :], beyond(P1W, P1E, 0, 1) + DP[0], 0.0) * half
        edge_v = jnp.where(level < SV[0, 8:16, :], beyond(P1W, P1E, 1, 1) + DP[1], 0.0) * half
        edge_vs = jnp.where(level < SV[0, 7:15, :], beyond(P1W, P1E, 1, 0) + DP[2], 0.0) * half
        last_u = jnp.where(level < SU[1, 8:16, :], pack1[0, c] + DP[3], 0.0) * half
        edges, outer = [], []
        for f in (3, 4):
            south, here, north = [
                jnp.where(level < SC[0, r + 7 : r + 15, :], beyond(PW, PE, f, r), 0.0)
                for r in range(3)
            ]
            inner = jnp.where(level < SC[1, 8:16, :], pack[f, c, 1:9, :], 0.0)
            flux = edge_u * (here + roll(jnp.where(at4, inner, here), -1))
            flux_last = last_u * (inner + roll(here, -1))
            flux_west = roll(jnp.where(at3, flux_last, flux), 1)
            a = here - ((flux - flux_west) + (edge_v * (here + north) - edge_vs * (south + here)))
            outer.append(jnp.where(level < SC[0, 8:16, :], a, 0.0))
            edges.append(jnp.where(at3, flux, here))

        cc0, cu0, cv0 = CC[8:16, :] - base, CU[8:16, :] - base, CV[8:16, :] - base
        cvs = CV[7:15, :] - base
        held = [zero, zero]
        for i in range(LC):
            k = c * LC + i
            u = jnp.where(cu0 > i, U1B[k] + du, 0.0)
            v = jnp.where(cv0 > i, V1X[k, 8:16, :] + dv, 0.0)
            vs = jnp.where(cvs > i, V1X[k, 7:15, :] + dvs, 0.0) * half
            UN[k] = u
            VN[k] = v
            u = u * half
            v = v * half
            for f in range(2):
                south, here, north = [X[2 + f, k, r : r + 8, :] for r in (7, 8, 9)]
                edge = unpacked(edges[f], i)
                flux = u * (here + roll(jnp.where(first, edge, here), -1))
                a = here - (
                    (flux - roll(jnp.where(last, edge, flux), 1))
                    + (v * (here + north) - vs * (south + here))
                )
                a = jnp.where(cc0 > i, a, 0.0)
                AX[f, k, 8:16, :] = a
                held[f] = jnp.where(slot == i, packed(a, i), held[f])
        for f in range(2):
            AD[f, c, 1:9, :] = outer[f] - held[f]

    @pl.when(has_north)
    def _():
        send(G_UP, AX.at[:, :, pl.ds(14, 2), :], AX.at[:, :, pl.ds(6, 2), :], 0, 1)
        send(G_UP1, AD.at[:, :, pl.ds(8, 1), :], AD.at[:, :, pl.ds(0, 1), :], 0, 1)

    @pl.when(has_south)
    def _():
        send(G_DOWN, AX.at[:, :, pl.ds(8, 2), :], AX.at[:, :, pl.ds(16, 2), :], 0, -1)
        send(G_DOWN1, AD.at[:, :, pl.ds(1, 1), :], AD.at[:, :, pl.ds(9, 1), :], 0, -1)

    left(G_SUM, size_sum)
    left(G_SIDE1, size_side1)
    left(G_CORNER1, size_corner1)
    left(G_V1, size_v1)

    @pl.when(has_south)
    def _():
        received(G_UP, size_a)
        received(G_UP1, size_ad)

    @pl.when(has_north)
    def _():
        received(G_DOWN, size_a)
        received(G_DOWN1, size_ad)

    @pl.loop(0, NC)
    def _(c):
        base = (c * LC).astype(jnp.float32)
        cc0 = CC[8:16, :] - base
        edges = []
        for f in range(2):
            south, here, north = [AD[f, c, r : r + 8, :] for r in range(3)]
            edges.append(KAPPA * edge_far(here, south + north))
        for i in range(LC):
            k = c * LC + i
            for f, out in ((0, TN), (1, SN)):
                ss, s, a, n, nn = [AX[f, k, r : r + 8, :] for r in range(6, 11)]
                y = n + s
                mixed = (
                    centre_ts * a
                    - KAPPA * (far(a, y, nn + ss) - 8.0 * y)
                    - jnp.where(edge4, unpacked(edges[f], i), 0.0)
                )
                out[k] = jnp.where(cc0 > i, mixed, 0.0)

    @pl.when(has_north)
    def _():
        left(G_UP, size_a)
        left(G_UP1, size_ad)

    @pl.when(has_south)
    def _():
        left(G_DOWN, size_a)
        left(G_DOWN1, size_ad)


def write_out(*refs):
    copies = [pltpu.make_async_copy(refs[i], refs[5 + i], refs[10].at[i]) for i in range(5)]
    for copy in copies:
        copy.start()
    for copy in copies:
        copy.wait()


def per_device(nx, ny, *args):
    tile3 = jax.ShapeDtypeStruct((K, ROWS, LANES), jnp.float32)
    tile2 = jax.ShapeDtypeStruct((ROWS, LANES), jnp.float32)
    outs = (tile3, tile3, tile3, tile3, tile2)

    def vmem(*shape, dtype=jnp.float32):
        return pltpu.VMEM(shape, dtype)

    args = [pltpu.with_memory_space_constraint(x, pltpu.HBM) for x in args]
    held = pl.pallas_call(
        functools.partial(kernel, nx, ny),
        out_shape=tuple(pltpu.VMEM(x.shape, x.dtype) for x in outs),
        in_specs=[pl.BlockSpec(memory_space=pltpu.HBM)] * 7,
        out_specs=[pl.BlockSpec(memory_space=pltpu.VMEM)] * 5,
        scratch_shapes=[
            vmem(4, K, 24, LANES),
            vmem(K, 16, LANES),
            vmem(3, 3, 24, LANES),
            vmem(ROWS, LANES, dtype=jnp.int32),
            vmem(ROWS, LANES, dtype=jnp.int32),
            vmem(24, LANES),
            vmem(24, LANES),
            vmem(24, LANES),
            vmem(2, 24, LANES),
            vmem(2, 24, LANES),
            vmem(2, 24, LANES),
            vmem(5, NC, 16, LANES),
            vmem(5, NC, 16, LANES),
            vmem(5, NC, 16, LANES),
            vmem(4, 3, 24, LANES),
            vmem(2, 24, LANES),
            vmem(4, ROWS, LANES),
            vmem(K, ROWS, LANES),
            vmem(K, 16, LANES),
            vmem(2, NC, ROWS, LANES),
            vmem(2, NC, 16, LANES),
            vmem(2, NC, 16, LANES),
            vmem(2, K, 24, LANES),
            vmem(2, NC, 16, LANES),
            pltpu.SemaphoreType.DMA((7,)),
            pltpu.SemaphoreType.DMA((GROUPS,)),
            pltpu.SemaphoreType.DMA((GROUPS,)),
        ],
        compiler_params=pltpu.CompilerParams(
            collective_id=0, has_side_effects=True, vmem_limit_bytes=24 * 1024 * 1024
        ),
    )(*args)
    return pl.pallas_call(
        write_out,
        out_shape=outs,
        in_specs=[pl.BlockSpec(memory_space=pltpu.VMEM)] * 5,
        out_specs=[pl.BlockSpec(memory_space=pltpu.HBM)] * 5,
        scratch_shapes=[pltpu.SemaphoreType.DMA((5,))],
        compiler_params=pltpu.CompilerParams(vmem_limit_bytes=8 * 1024 * 1024),
    )(*held)


def solution(mesh):
    placed = (P(None, "gy", "gx"),) * 4 + (P("gy", "gx"),) * 3
    return jax.shard_map(
        functools.partial(per_device, mesh.shape["gx"], mesh.shape["gy"]),
        mesh=mesh,
        in_specs=placed,
        out_specs=(P(None, "gy", "gx"),) * 4 + (P("gy", "gx"),),
        check_vma=False,
    )
```

```python
import functools

import jax
import jax.numpy as jnp
from jax import lax
from jax.experimental import pallas as pl
from jax.experimental.pallas import tpu as pltpu
from jax.sharding import PartitionSpec as P

MESH = pl.DeviceIdType.MESH
K = 75
NC = 5
LC = K // NC
SUBSTEPS = 8
ROWS = 8
LANES = 128

DT = 0.4
NU = 0.025
KAPPA = 0.01
DTT = 0.2
GRAVITY = 4.0
DB = DT / SUBSTEPS

AROUND = [(-1, -1), (1, -1), (-1, 1), (1, 1), (-1, 0), (1, 0), (0, -1), (0, 1)]
(G_2D, G_UV, G_W, G_SIDE, G_CORNER, G_POLE, G_TS, G_SUM, G_SIDE1, G_CORNER1, G_V1, G_UP, G_DOWN, G_UP1, G_DOWN1) = range(15)
GROUPS = 15


def kernel(
    nx,
    ny,
    t_in,
    s_in,
    u_in,
    v_in,
    h_in,
    flag_in,
    bottom_in,
    TN,
    SN,
    UN,
    VN,
    HN,
    X,
    WX,
    D2,
    flag_v,
    bottom_v,
    CC,
    CU,
    CV,
    SC,
    SU,
    SV,
    pack,
    PE,
    PW,
    F2,
    DV,
    DP,
    U1B,
    V1X,
    pack1,
    P1E,
    P1W,
    AX,
    AD,
    EU,
    EV,
    HC,
    CE,
    FW,
    AO,
    EM,
    load_sem,
    send_sem,
    recv_sem,
):
    gx, gy = lax.axis_index("gx"), lax.axis_index("gy")

    def device(dx, dy):
        return (lax.rem(gx + dx + nx, nx), lax.rem(gy + dy + ny, ny))

    def send(group, src, dst, dx, dy):
        pltpu.make_async_remote_copy(
            src_ref=src,
            dst_ref=dst,
            send_sem=send_sem.at[group],
            recv_sem=recv_sem.at[group],
            device_id=device(dx, dy),
            device_id_type=MESH,
        ).start()

    def received(group, size):
        pltpu.make_async_copy(size, size, recv_sem.at[group]).wait()

    def left(group, size):
        pltpu.make_async_copy(size, size, send_sem.at[group]).wait()

    loads = [
        pltpu.make_async_copy(flag_in, flag_v, load_sem.at[5]),
        pltpu.make_async_copy(bottom_in, bottom_v, load_sem.at[6]),
        pltpu.make_async_copy(h_in, D2.at[1, 1, pl.ds(8, 8), :], load_sem.at[4]),
        pltpu.make_async_copy(u_in, X.at[0, :, pl.ds(8, 8), :], load_sem.at[0]),
        pltpu.make_async_copy(v_in, X.at[1, :, pl.ds(8, 8), :], load_sem.at[1]),
        pltpu.make_async_copy(t_in, X.at[2, :, pl.ds(8, 8), :], load_sem.at[2]),
        pltpu.make_async_copy(s_in, X.at[3, :, pl.ds(8, 8), :], load_sem.at[3]),
    ]
    for load in loads:
        load.start()

    barrier = pltpu.get_barrier_semaphore()
    for dx, dy in AROUND:
        pl.semaphore_signal(barrier, inc=1, device_id=device(dx, dy), device_id_type=MESH)

    lane = lax.broadcasted_iota(jnp.int32, (ROWS, LANES), 1)
    lane8 = lax.rem(lane, 8)
    slot = lax.div(lane, 8).astype(jnp.float32)
    row = lax.broadcasted_iota(jnp.int32, (ROWS, LANES), 0)
    first, last = lane == 0, lane == LANES - 1
    edge4 = jnp.logical_or(lane < 2, lane >= LANES - 2)
    western, at3, at4 = lane8 < 4, lane8 == 3, lane8 == 4
    has_south, has_north = gy > 0, gy < ny - 1
    zero = jnp.zeros((ROWS, LANES), jnp.float32)

    def roll(x, shift):
        return pltpu.roll(x, shift % LANES, x.ndim - 1)

    def packed(x, i):
        return roll(x, 8 * i + 4)

    def unpacked(x, i):
        return roll(x, LANES - 4 - 8 * i)

    def in_slots(x, lanes):
        l8 = lax.rem(lax.broadcasted_iota(jnp.int32, x.shape, 1), 8)
        out = None
        for l in lanes:
            column = jnp.broadcast_to(x[:, l : l + 1], x.shape)
            out = column if out is None else jnp.where(l8 == (l + 4) % LANES, column, out)
        return out

    @pl.when(jnp.logical_not(has_south))
    def _():
        AD[:, :, 0:1, :] = jnp.zeros((2, NC, 1, LANES), jnp.float32)

        @pl.loop(0, K)
        def _(k):
            for f in range(2):
                AX[f, k, 6:8, :] = jnp.zeros((2, LANES), jnp.float32)

    @pl.when(jnp.logical_not(has_north))
    def _():
        AD[:, :, 9:10, :] = jnp.zeros((2, NC, 1, LANES), jnp.float32)

        @pl.loop(0, K)
        def _(k):
            for f in range(2):
                AX[f, k, 16:18, :] = jnp.zeros((2, LANES), jnp.float32)

    for load in loads[:3]:
        load.wait()
    own = (flag_v[...] * bottom_v[...]).astype(jnp.float32)
    D2[0, 1, 8:16, :] = own
    D2[2, 1, 8:16, :] = in_slots(own, (124, 125, 126, 127, 0, 1, 2, 3))

    def rows(group, fields, count, dy):
        src, dst = (16 - count, 8 - count) if dy > 0 else (8, 16)
        send(
            group,
            X.at[fields, :, pl.ds(src, count), :],
            X.at[fields, :, pl.ds(dst, count), :],
            0,
            dy,
        )

    for load in loads[3:]:
        load.wait()
    def weight(t, s, dz):
        return (0.8 * s - t * (0.2 + 0.05 * t)) * dz

    def thickness(base, i):
        return 0.5 / K + (base + (i + 0.5)) * (1.0 / (K * K))

    @pl.loop(0, NC)
    def _(c):
        base = (c * LC).astype(jnp.float32)
        depth = D2[0, 1, 8:16, :] - base
        held = [zero] * 5
        for i in range(LC):
            k = c * LC + i
            u, v, t, s = [X[f, k, 8:16, :] for f in range(4)]
            w = jnp.where(depth > i, weight(t, s, DT * thickness(base, i)), 0.0)
            WX[k, 0:8, :] = w
            for n, x in enumerate((u, v, w, t, s)):
                held[n] = jnp.where(slot == i, packed(x, i), held[n])
        for n in range(5):
            pack[n, c, 1:9, :] = held[n]

    pl.semaphore_wait(barrier, len(AROUND))

    for dx, dy in AROUND:
        send(
            G_2D,
            D2.at[:, 1, pl.ds(8, 8), :],
            D2.at[:, 1 - dx, pl.ds(8 * (1 - dy), 8), :],
            dx,
            dy,
        )
    for dx in (1, -1):
        for dy in (1, -1):
            side = PW if dx > 0 else PE
            src, dst = (8, 0) if dy > 0 else (1, 9)
            send(
                G_CORNER, pack.at[:, :, pl.ds(src, 1), :], side.at[:, :, pl.ds(dst, 1), :], dx, dy
            )
    for dx in (1, -1):
        side = PW if dx > 0 else PE
        send(G_SIDE, pack.at[:, :, pl.ds(1, 8), :], side.at[:, :, pl.ds(1, 8), :], dx, 0)
    for dy in (1, -1):
        rows(G_UV, pl.ds(0, 2), 2, dy)
    for dy in (1, -1):
        src, dst = (8, 0) if dy > 0 else (1, 9)
        uv = pl.ds(0, 2)
        send(G_POLE, pack.at[uv, :, pl.ds(src, 1), :], pack.at[uv, :, pl.ds(dst, 1), :], 0, dy)
    send(G_W, WX.at[:, pl.ds(0, 1), :], WX.at[:, pl.ds(8, 1), :], 0, -1)
    for dy in (1, -1):
        rows(G_TS, pl.ds(2, 2), 1, dy)

    size_2d = X.at[0, pl.ds(0, 24), pl.ds(0, 8), :]
    size_uv = X.at[pl.ds(0, 2), :, pl.ds(0, 4), :]
    size_w = X.at[0, :, pl.ds(0, 1), :]
    size_side = PE.at[:, :, pl.ds(0, 16), :]
    size_corner = PE.at[:, :, pl.ds(0, 4), :]
    size_pole = PE.at[pl.ds(0, 2), :, pl.ds(0, 2), :]
    size_ts = X.at[pl.ds(0, 2), :, pl.ds(0, 2), :]
    size_sum = X.at[0, pl.ds(0, 32), pl.ds(0, 8), :]
    size_side1 = P1E.at[:, :, pl.ds(0, 16), :]
    size_corner1 = P1E.at[0, :, pl.ds(0, 2), :]
    size_v1 = V1X.at[:, pl.ds(0, 1), :]
    size_a = X.at[pl.ds(0, 2), :, pl.ds(0, 2), :]
    size_ad = AD.at[:, :, pl.ds(0, 1), :]

    received(G_2D, size_2d)
    row24 = lax.broadcasted_iota(jnp.int32, (24, LANES), 0)
    lane24 = lax.broadcasted_iota(jnp.int32, (24, LANES), 1)
    slot24 = lax.rem(lane24, 8)
    first24, last24 = lane24 == 0, lane24 == LANES - 1
    inside = jnp.logical_and(
        jnp.logical_or(row24 >= 8, has_south), jnp.logical_or(row24 < 16, has_north)
    )

    def ring_east(c, h, seam=first24):
        return (
            roll(jnp.where(seam, h, c), LANES - 1),
            roll(jnp.where(seam, c, h), LANES - 1),
        )

    def ring_west(c, h):
        return (
            roll(jnp.where(last24, h, c), 1),
            roll(jnp.where(last24, c, h), 1),
        )

    def north24(x):
        return pltpu.roll(x, 23, 0)

    def south24(x):
        return pltpu.roll(x, 1, 0)

    def sides(ref, f):
        return ref[f, 1], jnp.where(lane24 < 64, ref[f, 2], ref[f, 0])

    col = [jnp.where(inside, x, 0.0) for x in sides(D2, 0)]
    ocean = [x > 0.0 for x in col]
    cu = [jnp.minimum(a, b) for a, b in zip(col, ring_east(*col))]
    cv = [jnp.minimum(a, north24(a)) for a in col]
    CC[...] = col[0]
    CU[...] = cu[0]
    CV[...] = cv[0]
    edge_col = [
        jnp.where(inside, x, 0.0)
        for x in (jnp.where(slot24 < 4, D2[2, 0], D2[2, 2]), D2[2, 1])
    ]
    edge_cu = [jnp.minimum(a, b) for a, b in zip(edge_col, ring_east(*edge_col, slot24 == 4))]
    for n in range(2):
        SC[n] = edge_col[n]
        SU[n] = edge_cu[n]
        SV[n] = jnp.minimum(edge_col[n], north24(edge_col[n]))

    at_wall = jnp.where(
        jnp.logical_or(
            jnp.logical_and(row == 0, jnp.logical_not(has_south)),
            jnp.logical_and(row == ROWS - 1, jnp.logical_not(has_north)),
        ),
        19.0,
        20.0,
    )
    latitude = (row + gy * ROWS).astype(jnp.float32)
    f4 = (0.25 * DT) * (0.2 + 0.3 * (latitude + 0.5) / (ROWS * ny))
    centre_uv = 1.0 - (DT * NU) * at_wall
    centre_ts = 1.0 - KAPPA * at_wall

    received(G_UV, size_uv)
    left(G_UV, size_uv)

    @pl.loop(0, NC)
    def _(c):
        base = (c * LC).astype(jnp.float32)
        for f, depths in ((0, CU), (1, CV)):
            low, high = depths[6:14, :] - base, depths[10:18, :] - base
            for i in range(LC):
                k = c * LC + i
                a = jnp.where(low > i, X[f, k, 6:14, :], 0.0)
                b = jnp.where(high > i, X[f, k, 10:18, :], 0.0)
                X[f, k, 6:14, :] = a
                X[f, k, 10:18, :] = b

    received(G_W, size_w)
    received(G_SIDE, size_side)
    received(G_CORNER, size_corner)
    received(G_POLE, size_pole)

    def far(a, y, yy):
        z = 2.0 * y - 8.0 * a
        return yy + roll(z + roll(a, -1), -1) + roll(z + roll(a, 1), 1)

    group = lax.broadcasted_iota(jnp.int32, (NC, ROWS, LANES), 0).astype(jnp.float32)
    lanes = lax.broadcasted_iota(jnp.int32, (NC, ROWS, LANES), 2)
    level = lax.div(lanes, 8).astype(jnp.float32) + group * LC
    slots = lax.rem(lanes, 8)
    westerns, at3s, at4s = slots < 4, slots == 3, slots == 4

    def beyond(west, east, f, r):
        return jnp.where(westerns, west[f, :, r : r + 8, :], east[f, :, r : r + 8, :])

    def if_wet(depths, n, r, x):
        return jnp.where(level < depths[n, r + 7 : r + 15, :][None], x, 0.0)

    def excess(f, depths, r):
        return if_wet(depths, 0, r, beyond(PW, PE, f, r)) - if_wet(
            depths, 1, r, pack[f, :, r : r + 8, :]
        )

    def edge_far(d, y):
        z = 2.0 * y - 8.0 * d
        return jnp.where(westerns, roll(d, -2), roll(d, 2)) + jnp.where(
            at3s, roll(z, -1), jnp.where(at4s, roll(z, 1), 0.0)
        )

    du_s, du, du_n = [excess(0, SU, r) for r in range(3)]
    dv_s, dv, dv_n = [excess(1, SV, r) for r in range(3)]
    dw = beyond(PW, PE, 2, 1) - pack[2, :, 1:9, :]
    dw = jnp.where(at3s, roll(dw, -1), 0.0)
    run = dw
    for shift in (8, 16, 32, 64):
        run = run + jnp.where(lanes >= shift, roll(run, shift), 0.0)
    whole = jnp.broadcast_to(run[:, :, 8 * LC - 5 : 8 * LC - 4], run.shape)
    above = [zero]
    for c in range(NC - 1):
        above.append(above[-1] + whole[c])
    run = run + jnp.stack(above)
    EU[...] = jnp.where(at3s, f4[None] * roll(dv + dv_s, -1) - run + 0.5 * dw, 0.0) - (
        DT * NU
    ) * edge_far(du, du_n + du_s)
    EV[...] = jnp.where(at4s, -f4[None] * roll(du + du_n, 1), 0.0) - (DT * NU) * edge_far(
        dv, dv_n + dv_s
    )

    def momentum(c, carry):
        cum_e, cum_n, sum_u0, sum_v0, sum_u, sum_v = carry
        base = (c * LC).astype(jnp.float32)
        edge_u, edge_v = EU[c], EV[c]
        cu0, cv0 = CU[8:16, :] - base, CV[8:16, :] - base
        held_u = held_v = zero
        for i in range(LC):
            k = c * LC + i
            dz = thickness(base, i)
            uss, us, u, un, unn = [X[0, k, r : r + 8, :] for r in range(6, 11)]
            vss, vs, v, vn, vnn = [X[1, k, r : r + 8, :] for r in range(6, 11)]
            w, wn = WX[k, 0:8, :], WX[k, 1:9, :]
            step_e = roll(w, -1) - w
            step_n = wn - w
            cum_e = cum_e + step_e
            cum_n = cum_n + step_n
            uu = u + un
            vv = v + vs
            uu = uu + roll(uu, 1)
            vv = vv + roll(vv, -1)
            yu, yv = un + us, vn + vs
            u1 = (
                centre_uv * u
                + f4 * vv
                - (cum_e - 0.5 * step_e)
                - (DT * NU) * (far(u, yu, unn + uss) - 8.0 * yu)
                + jnp.where(edge4, unpacked(edge_u, i), 0.0)
            )
            v1 = (
                centre_uv * v
                - f4 * uu
                - (cum_n - 0.5 * step_n)
                - (DT * NU) * (far(v, yv, vnn + vss) - 8.0 * yv)
                + jnp.where(edge4, unpacked(edge_v, i), 0.0)
            )
            u1 = jnp.where(cu0 > i, u1, 0.0)
            v1 = jnp.where(cv0 > i, v1, 0.0)
            sum_u0 = sum_u0 + u * dz
            sum_v0 = sum_v0 + v * dz
            sum_u = sum_u + u1 * dz
            sum_v = sum_v + v1 * dz
            U1B[k] = u1
            V1X[k, 8:16, :] = v1
            held_u = jnp.where(slot == i, packed(u1, i), held_u)
            held_v = jnp.where(slot == i, packed(v1, i), held_v)
        pack1[0, c] = held_u
        pack1[1, c] = held_v
        return cum_e, cum_n, sum_u0, sum_v0, sum_u, sum_v

    sums = lax.fori_loop(0, NC, momentum, (zero,) * 6)[2:]

    for n in range(4):
        F2[n, 1, 8:16, :] = sums[n]
    for dx, dy in AROUND:
        send(
            G_SUM,
            F2.at[:, 1, pl.ds(8, 8), :],
            F2.at[:, 1 - dx, pl.ds(8 * (1 - dy), 8), :],
            dx,
            dy,
        )
    for dx in (1, -1):
        side = P1W if dx > 0 else P1E
        send(G_SIDE1, pack1, side.at[:, :, pl.ds(1, 8), :], dx, 0)
        send(G_CORNER1, pack1.at[1, :, pl.ds(7, 1), :], side.at[1, :, pl.ds(0, 1), :], dx, 1)
    send(G_V1, V1X.at[:, pl.ds(15, 1), :], V1X.at[:, pl.ds(7, 1), :], 0, 1)

    left(G_2D, size_2d)
    left(G_W, size_w)
    left(G_SIDE, size_side)
    left(G_CORNER, size_corner)
    left(G_POLE, size_pole)
    left(G_TS, size_ts)
    received(G_TS, size_ts)

    for f in range(2):
        HC[f] = if_wet(SC, 0, 1, beyond(PW, PE, 3 + f, 1))

    @pl.loop(0, NC)
    def _(c):
        base = (c * LC).astype(jnp.float32)
        low, mid, high = [CC[r : r + 8, :] - base for r in (7, 8, 9)]
        for f in range(2):
            edge = HC[f, c]
            for i in range(LC):
                k = c * LC + i
                south = jnp.where(low > i, X[2 + f, k, 7:15, :], 0.0)
                here = jnp.where(mid > i, X[2 + f, k, 8:16, :], 0.0)
                north = jnp.where(high > i, X[2 + f, k, 9:17, :], 0.0)
                X[2 + f, k, 7:15, :] = south
                X[2 + f, k, 9:17, :] = north
                CE[f, k] = here + roll(jnp.where(first, unpacked(edge, i), here), -1)

    def both(op, *pairs):
        return [op(*xs) for xs in zip(*pairs)]

    def depth_of(c):
        return c * (0.5 / K + c * (0.5 / (K * K)))

    open_u = [(x > 0.0).astype(jnp.float32) for x in cu]
    open_v = [(x > 0.0).astype(jnp.float32) for x in cv]
    depth_u = both(depth_of, cu)
    depth_v = both(depth_of, cv)
    pull_u = both(lambda o, d: o * d * (DB * GRAVITY), open_u, depth_u)
    pull_v = both(lambda o, d: o * d * (DB * GRAVITY), open_v, depth_v)
    pull_w = ring_west(*pull_u)
    ease = both(lambda o: jnp.where(o, DB, 0.0), ocean)
    height = [jnp.where(o, x, 0.0) for o, x in zip(ocean, sides(D2, 1))]

    received(G_SUM, size_sum)
    u0, v0, u_all, v_all = [list(sides(F2, f)) for f in range(4)]
    push_u = both(lambda o, a, b: o * ((a - b) * (DB / DT)), open_u, u_all, u0)
    push_v = both(lambda o, a, b: o * ((a - b) * (DB / DT)), open_v, v_all, v0)
    trans_u = both(lambda o, a: o * a, open_u, u0)
    trans_v = both(lambda o, a: o * a, open_v, v0)
    run_u = [jnp.zeros((24, LANES), jnp.float32)] * 2
    run_v = run_u

    def substep(_, state):
        level, trans_u, trans_w, trans_v, run_u, run_v = state
        level_w = ring_west(*level)
        trans_w = both(
            lambda t, p, q, h, w: t + (p - q * (h - w)), trans_w, push_w, pull_w, level, level_w
        )
        trans_u = both(
            lambda t, p, q, e, h: t + (p - q * (e - h)),
            trans_u,
            push_u,
            pull_u,
            ring_east(*level),
            level,
        )
        trans_v = both(
            lambda t, p, q, h: t + (p - q * (north24(h) - h)), trans_v, push_v, pull_v, level
        )
        level = both(
            lambda h, e, u, w, v: h - e * ((u - w) + (v - south24(v))),
            level,
            ease,
            trans_u,
            trans_w,
            trans_v,
        )
        return level, trans_u, trans_w, trans_v, both(jnp.add, run_u, trans_u), both(jnp.add, run_v, trans_v)

    trans_w, push_w = ring_west(*trans_u), ring_west(*push_u)
    state = height, trans_u, trans_w, trans_v, run_u, run_v
    for n in range(SUBSTEPS):
        state = substep(n, state)
    height, _, _, _, run_u, run_v = state

    HN[...] = height[0][8:16]

    def shift(r, a, d, o):
        return (r * (1.0 / SUBSTEPS) - a) / (d + (1.0 - o))

    shift_u = both(shift, run_u, u_all, depth_u, open_u)
    shift_v = both(shift, run_v, v_all, depth_v, open_v)
    DV[0] = shift_v[0]
    DV[1] = shift_v[1]
    du, dv, dvs = shift_u[0][8:16], shift_v[0][8:16], DV[0, 7:15, :]
    DP[0] = in_slots(shift_u[1][8:16], (125, 126, 127, 0, 1))
    DP[1] = in_slots(DV[1, 8:16, :], (126, 127, 0, 1))
    DP[2] = in_slots(DV[1, 7:15, :], (126, 127, 0, 1))
    DP[3] = jnp.broadcast_to(du[:, LANES - 1 :], du.shape)

    received(G_SIDE1, size_side1)
    received(G_CORNER1, size_corner1)
    received(G_V1, size_v1)
    half = 0.5 * DTT

    edge_u = if_wet(SU, 0, 1, beyond(P1W, P1E, 0, 1) + DP[0][None]) * half
    edge_v = if_wet(SV, 0, 1, beyond(P1W, P1E, 1, 1) + DP[1][None]) * half
    edge_vs = if_wet(SV, 0, 0, beyond(P1W, P1E, 1, 0) + DP[2][None]) * half
    last_u = if_wet(SU, 1, 1, pack1[0] + DP[3][None]) * half
    for f in range(2):
        south = if_wet(SC, 0, 0, beyond(PW, PE, 3 + f, 0))
        here = HC[f]
        north = if_wet(SC, 0, 2, beyond(PW, PE, 3 + f, 2))
        inner = if_wet(SC, 1, 1, pack[3 + f, :, 1:9, :])
        flux = edge_u * (here + roll(jnp.where(at4s, inner, here), -1))
        flux_last = last_u * (inner + roll(here, -1))
        flux_west = roll(jnp.where(at3s, flux_last, flux), 1)
        a = here - ((flux - flux_west) + (edge_v * (here + north) - edge_vs * (south + here)))
        FW[f] = flux
        AO[f] = if_wet(SC, 0, 1, a)

    def send_rows(c, up):
        src, dst, dy, group = (14, 6, 1, G_UP) if up else (8, 16, -1, G_DOWN)
        levels = pl.ds(c * LC, LC)
        send(
            group,
            AX.at[:, levels, pl.ds(src, 2), :],
            AX.at[:, levels, pl.ds(dst, 2), :],
            0,
            dy,
        )

    @pl.loop(0, NC)
    def _(c):
        base = (c * LC).astype(jnp.float32)
        edges = [FW[f, c] for f in range(2)]
        cc0, cu0, cv0 = CC[8:16, :] - base, CU[8:16, :] - base, CV[8:16, :] - base
        cvs = CV[7:15, :] - base
        held = [zero, zero]
        for i in range(LC):
            k = c * LC + i
            u = jnp.where(cu0 > i, U1B[k] + du, 0.0)
            v = jnp.where(cv0 > i, V1X[k, 8:16, :] + dv, 0.0)
            vs = jnp.where(cvs > i, V1X[k, 7:15, :] + dvs, 0.0) * half
            UN[k] = u
            VN[k] = v
            u = u * half
            v = v * half
            for f in range(2):
                south, here, north = [X[2 + f, k, r : r + 8, :] for r in (7, 8, 9)]
                edge = unpacked(edges[f], i)
                flux = u * CE[f, k]
                a = here - (
                    (flux - roll(jnp.where(last, edge, flux), 1))
                    + (v * (here + north) - vs * (south + here))
                )
                a = jnp.where(cc0 > i, a, 0.0)
                AX[f, k, 8:16, :] = a
                held[f] = jnp.where(slot == i, packed(a, i), held[f])
        for f in range(2):
            AD[f, c, 1:9, :] = AO[f, c] - held[f]

        @pl.when(has_north)
        def _():
            send_rows(c, True)

        @pl.when(has_south)
        def _():
            send_rows(c, False)

    @pl.when(has_north)
    def _():
        send(G_UP1, AD.at[:, :, pl.ds(8, 1), :], AD.at[:, :, pl.ds(0, 1), :], 0, 1)

    @pl.when(has_south)
    def _():
        send(G_DOWN1, AD.at[:, :, pl.ds(1, 1), :], AD.at[:, :, pl.ds(9, 1), :], 0, -1)

    left(G_SUM, size_sum)
    left(G_SIDE1, size_side1)
    left(G_CORNER1, size_corner1)
    left(G_V1, size_v1)

    @pl.when(has_south)
    def _():
        received(G_UP, size_a)
        received(G_UP1, size_ad)

    @pl.when(has_north)
    def _():
        received(G_DOWN, size_a)
        received(G_DOWN1, size_ad)

    for f in range(2):
        south, here, north = [AD[f, :, r : r + 8, :] for r in range(3)]
        EM[f] = KAPPA * edge_far(here, south + north)

    @pl.loop(0, NC)
    def _(c):
        base = (c * LC).astype(jnp.float32)
        cc0 = CC[8:16, :] - base
        edges = [EM[f, c] for f in range(2)]
        for i in range(LC):
            k = c * LC + i
            for f, out in ((0, TN), (1, SN)):
                ss, s, a, n, nn = [AX[f, k, r : r + 8, :] for r in range(6, 11)]
                y = n + s
                mixed = (
                    centre_ts * a
                    - KAPPA * (far(a, y, nn + ss) - 8.0 * y)
                    - jnp.where(edge4, unpacked(edges[f], i), 0.0)
                )
                out[k] = jnp.where(cc0 > i, mixed, 0.0)

    @pl.when(has_north)
    def _():
        left(G_UP, size_a)
        left(G_UP1, size_ad)

    @pl.when(has_south)
    def _():
        left(G_DOWN, size_a)
        left(G_DOWN1, size_ad)


def write_out(*refs):
    copies = [pltpu.make_async_copy(refs[i], refs[5 + i], refs[10].at[i]) for i in range(5)]
    for copy in copies:
        copy.start()
    for copy in copies:
        copy.wait()


def per_device(nx, ny, *args):
    tile3 = jax.ShapeDtypeStruct((K, ROWS, LANES), jnp.float32)
    tile2 = jax.ShapeDtypeStruct((ROWS, LANES), jnp.float32)
    outs = (tile3, tile3, tile3, tile3, tile2)

    def vmem(*shape, dtype=jnp.float32):
        return pltpu.VMEM(shape, dtype)

    args = [pltpu.with_memory_space_constraint(x, pltpu.HBM) for x in args]
    held = pl.pallas_call(
        functools.partial(kernel, nx, ny),
        out_shape=tuple(pltpu.VMEM(x.shape, x.dtype) for x in outs),
        in_specs=[pl.BlockSpec(memory_space=pltpu.HBM)] * 7,
        out_specs=[pl.BlockSpec(memory_space=pltpu.VMEM)] * 5,
        scratch_shapes=[
            vmem(4, K, 24, LANES),
            vmem(K, 16, LANES),
            vmem(3, 3, 24, LANES),
            vmem(ROWS, LANES, dtype=jnp.int32),
            vmem(ROWS, LANES, dtype=jnp.int32),
            vmem(24, LANES),
            vmem(24, LANES),
            vmem(24, LANES),
            vmem(2, 24, LANES),
            vmem(2, 24, LANES),
            vmem(2, 24, LANES),
            vmem(5, NC, 16, LANES),
            vmem(5, NC, 16, LANES),
            vmem(5, NC, 16, LANES),
            vmem(4, 3, 24, LANES),
            vmem(2, 24, LANES),
            vmem(4, ROWS, LANES),
            vmem(K, ROWS, LANES),
            vmem(K, 16, LANES),
            vmem(2, NC, ROWS, LANES),
            vmem(2, NC, 16, LANES),
            vmem(2, NC, 16, LANES),
            vmem(2, K, 24, LANES),
            vmem(2, NC, 16, LANES),
            vmem(NC, ROWS, LANES),
            vmem(NC, ROWS, LANES),
            vmem(2, NC, ROWS, LANES),
            vmem(2, K, ROWS, LANES),
            vmem(2, NC, ROWS, LANES),
            vmem(2, NC, ROWS, LANES),
            vmem(2, NC, ROWS, LANES),
            pltpu.SemaphoreType.DMA((7,)),
            pltpu.SemaphoreType.DMA((GROUPS,)),
            pltpu.SemaphoreType.DMA((GROUPS,)),
        ],
        compiler_params=pltpu.CompilerParams(
            collective_id=0, has_side_effects=True, vmem_limit_bytes=24 * 1024 * 1024
        ),
    )(*args)
    return pl.pallas_call(
        write_out,
        out_shape=outs,
        in_specs=[pl.BlockSpec(memory_space=pltpu.VMEM)] * 5,
        out_specs=[pl.BlockSpec(memory_space=pltpu.HBM)] * 5,
        scratch_shapes=[pltpu.SemaphoreType.DMA((5,))],
        compiler_params=pltpu.CompilerParams(vmem_limit_bytes=8 * 1024 * 1024),
    )(*held)


def solution(mesh):
    placed = (P(None, "gy", "gx"),) * 4 + (P("gy", "gx"),) * 3
    return jax.shard_map(
        functools.partial(per_device, mesh.shape["gx"], mesh.shape["gy"]),
        mesh=mesh,
        in_specs=placed,
        out_specs=(P(None, "gy", "gx"),) * 4 + (P("gy", "gx"),),
        check_vma=False,
    )
```

```python
import functools

import jax
import jax.numpy as jnp
from jax import lax
from jax.experimental import pallas as pl
from jax.experimental.pallas import tpu as pltpu
from jax.sharding import PartitionSpec as P

MESH = pl.DeviceIdType.MESH
K = 75
NC = 5
LC = K // NC
NM = 5
LM = K // NM
SUBSTEPS = 8
ROWS = 8
LANES = 128

DT = 0.4
NU = 0.025
KAPPA = 0.01
DTT = 0.2
GRAVITY = 4.0
DB = DT / SUBSTEPS

AROUND = [(-1, -1), (1, -1), (-1, 1), (1, 1), (-1, 0), (1, 0), (0, -1), (0, 1)]
GROUPS = 7
G_2D, G_A, G_TS, G_SUM, G_B, G_UP, G_DOWN = range(GROUPS)


def kernel(
    nx,
    ny,
    t_in,
    s_in,
    u_in,
    v_in,
    h_in,
    flag_in,
    bottom_in,
    TN,
    SN,
    UN,
    VN,
    HN,
    X,
    WX,
    D2,
    flag_v,
    bottom_v,
    CC,
    CU,
    CV,
    SC,
    SU,
    SV,
    SU4,
    SV4,
    pack,
    PE,
    PW,
    pack_ts,
    TE,
    TW,
    F2,
    DV,
    DP,
    U1B,
    V1X,
    pack1,
    P1E,
    P1W,
    AX,
    AD,
    EU,
    EV,
    HC,
    CE,
    FW,
    AO,
    EM,
    load_sem,
    send_sem,
    recv_sem,
):
    gx, gy = lax.axis_index("gx"), lax.axis_index("gy")

    def device(dx, dy):
        return (lax.rem(gx + dx + nx, nx), lax.rem(gy + dy + ny, ny))

    def send(group, src, dst, dx, dy):
        pltpu.make_async_remote_copy(
            src_ref=src,
            dst_ref=dst,
            send_sem=send_sem.at[group],
            recv_sem=recv_sem.at[group],
            device_id=device(dx, dy),
            device_id_type=MESH,
        ).start()

    def received(group, size):
        pltpu.make_async_copy(size, size, recv_sem.at[group]).wait()

    def left(group, size):
        pltpu.make_async_copy(size, size, send_sem.at[group]).wait()

    barrier = pltpu.get_barrier_semaphore()
    for dx, dy in AROUND:
        pl.semaphore_signal(barrier, inc=1, device_id=device(dx, dy), device_id_type=MESH)

    pltpu.make_async_copy(flag_in, flag_v, load_sem.at[0]).start()
    pltpu.make_async_copy(bottom_in, bottom_v, load_sem.at[0]).start()
    pltpu.make_async_copy(h_in, D2.at[1, 1, pl.ds(8, 8), :], load_sem.at[0]).start()
    for f, source in enumerate((u_in, v_in, t_in, s_in)):
        pltpu.make_async_copy(source, X.at[f, :, pl.ds(8, 8), :], load_sem.at[1]).start()

    def loaded(sem, size):
        pltpu.make_async_copy(size, size, load_sem.at[sem]).wait()

    lane = lax.broadcasted_iota(jnp.int32, (ROWS, LANES), 1)
    slot = lax.div(lane, 8).astype(jnp.float32)
    row = lax.broadcasted_iota(jnp.int32, (ROWS, LANES), 0)
    first, last = lane == 0, lane == LANES - 1
    edge4 = jnp.logical_or(lane < 2, lane >= LANES - 2)
    slot4 = lax.div(lane, 4).astype(jnp.float32)
    has_south, has_north = gy > 0, gy < ny - 1
    zero = jnp.zeros((ROWS, LANES), jnp.float32)

    def roll(x, shift):
        return pltpu.roll(x, shift % LANES, x.ndim - 1)

    def packed(x, i, width=8):
        return roll(x, width * i + width // 2)

    def unpacked(x, i, width=8):
        return roll(x, LANES - width // 2 - width * i)

    def in_slots(x, lanes, width=8):
        at = lax.rem(lax.broadcasted_iota(jnp.int32, x.shape, 1), width)
        out = None
        for l in lanes:
            column = jnp.broadcast_to(x[:, l : l + 1], x.shape)
            out = column if out is None else jnp.where(at == (l + width // 2) % LANES, column, out)
        return out

    @pl.when(jnp.logical_not(has_south))
    def _():
        AD[:, :, 0:1, :] = jnp.zeros((2, NC, 1, LANES), jnp.float32)

        @pl.loop(0, K)
        def _(k):
            for f in range(2):
                AX[f, k, 6:8, :] = jnp.zeros((2, LANES), jnp.float32)

    @pl.when(jnp.logical_not(has_north))
    def _():
        AD[:, :, 9:10, :] = jnp.zeros((2, NC, 1, LANES), jnp.float32)

        @pl.loop(0, K)
        def _(k):
            for f in range(2):
                AX[f, k, 16:18, :] = jnp.zeros((2, LANES), jnp.float32)

    loaded(0, AX.at[0, pl.ds(0, 3), pl.ds(8, 8), :])
    own = (flag_v[...] * bottom_v[...]).astype(jnp.float32)
    D2[0, 1, 8:16, :] = own
    D2[2, 1, 8:16, :] = in_slots(own, (124, 125, 126, 127, 0, 1, 2, 3))

    def rows(group, fields, count, dy):
        src, dst = (16 - count, 8 - count) if dy > 0 else (8, 16)
        send(
            group,
            X.at[fields, :, pl.ds(src, count), :],
            X.at[fields, :, pl.ds(dst, count), :],
            0,
            dy,
        )

    loaded(1, X.at[:, :, pl.ds(8, 8), :])
    def weight(t, s, dz):
        return (0.8 * s - t * (0.2 + 0.05 * t)) * dz

    def thickness(base, i):
        return 0.5 / K + (base + (i + 0.5)) * (1.0 / (K * K))

    @pl.loop(0, NM)
    def _(c):
        base = (c * LM).astype(jnp.float32)
        depth = D2[0, 1, 8:16, :] - base
        held = [zero] * 3
        for i in range(LM):
            k = c * LM + i
            u, v, t, s = [X[f, k, 8:16, :] for f in range(4)]
            w = jnp.where(depth > i, weight(t, s, DT * thickness(base, i)), 0.0)
            WX[k, 0:8, :] = w
            for n, x in enumerate((u, v, w)):
                held[n] = jnp.where(slot4 == i, packed(x, i, 4), held[n])
        for n in range(3):
            pack[n, c, 1:9, :] = held[n]

    pl.semaphore_wait(barrier, len(AROUND))

    def corners(group, src, west, east, fields):
        for dx in (1, -1):
            for dy in (1, -1):
                side = west if dx > 0 else east
                r_src, r_dst = (8, 0) if dy > 0 else (1, 9)
                send(
                    group,
                    src.at[fields, :, pl.ds(r_src, 1), :],
                    side.at[fields, :, pl.ds(r_dst, 1), :],
                    dx,
                    dy,
                )

    def spread(group, ref, around):
        for dx, dy in around:
            send(
                group,
                ref.at[:, 1, pl.ds(8, 8), :],
                ref.at[:, 1 - dx, pl.ds(8 * (1 - dy), 8), :],
                dx,
                dy,
            )

    uv = pl.ds(0, 2)
    spread(G_2D, D2, AROUND[:4])
    corners(G_A, pack, PW, PE, uv)
    spread(G_2D, D2, AROUND[4:6])
    for dx in (1, -1):
        side = PW if dx > 0 else PE
        send(G_A, pack.at[:, :, pl.ds(1, 8), :], side.at[:, :, pl.ds(1, 8), :], dx, 0)
    spread(G_2D, D2, AROUND[6:])
    for dy in (1, -1):
        rows(G_A, uv, 2, dy)
    for dy in (1, -1):
        src, dst = (8, 0) if dy > 0 else (1, 9)
        send(G_A, pack.at[uv, :, pl.ds(src, 1), :], pack.at[uv, :, pl.ds(dst, 1), :], 0, dy)
    send(G_A, WX.at[:, pl.ds(0, 1), :], WX.at[:, pl.ds(8, 1), :], 0, -1)

    @pl.loop(0, NC)
    def _(c):
        held = [zero] * 2
        for i in range(LC):
            for f in range(2):
                held[f] = jnp.where(slot == i, packed(X[2 + f, c * LC + i, 8:16, :], i), held[f])
        for f in range(2):
            pack_ts[f, c, 1:9, :] = held[f]

    for dx in (1, -1):
        side = TW if dx > 0 else TE
        send(G_TS, pack_ts.at[:, :, pl.ds(1, 8), :], side.at[:, :, pl.ds(1, 8), :], dx, 0)
    corners(G_TS, pack_ts, TW, TE, uv)
    for dy in (1, -1):
        rows(G_TS, pl.ds(2, 2), 1, dy)

    def size(levels, count):
        return X.at[0, pl.ds(0, levels), pl.ds(0, count), :]

    size_2d = size(24, 8)
    size_a = size(K, 13)
    size_ts = size(50, 10)
    size_sum = size(32, 8)
    size_b = size(49, 5)
    size_c = size(62, 5)

    received(G_2D, size_2d)
    row24 = lax.broadcasted_iota(jnp.int32, (24, LANES), 0)
    lane24 = lax.broadcasted_iota(jnp.int32, (24, LANES), 1)
    slot24 = lax.rem(lane24, 8)
    first24, last24 = lane24 == 0, lane24 == LANES - 1
    inside = jnp.logical_and(
        jnp.logical_or(row24 >= 8, has_south), jnp.logical_or(row24 < 16, has_north)
    )

    def ring_east(c, h, seam=first24):
        return (
            roll(jnp.where(seam, h, c), LANES - 1),
            roll(jnp.where(seam, c, h), LANES - 1),
        )

    def ring_west(c, h):
        return (
            roll(jnp.where(last24, h, c), 1),
            roll(jnp.where(last24, c, h), 1),
        )

    def north24(x):
        return pltpu.roll(x, 23, 0)

    def south24(x):
        return pltpu.roll(x, 1, 0)

    def sides(ref, f):
        return ref[f, 1], jnp.where(lane24 < 64, ref[f, 2], ref[f, 0])

    col = [jnp.where(inside, x, 0.0) for x in sides(D2, 0)]
    ocean = [x > 0.0 for x in col]
    cu = [jnp.minimum(a, b) for a, b in zip(col, ring_east(*col))]
    cv = [jnp.minimum(a, north24(a)) for a in col]
    CC[...] = col[0]
    CU[...] = cu[0]
    CV[...] = cv[0]
    edge_col = [
        jnp.where(inside, x, 0.0)
        for x in (jnp.where(slot24 < 4, D2[2, 0], D2[2, 2]), D2[2, 1])
    ]
    edge_cu = [jnp.minimum(a, b) for a, b in zip(edge_col, ring_east(*edge_col, slot24 == 4))]
    for n in range(2):
        SU4[n] = in_slots(cu[1 - n], (126, 127, 0, 1), 4)
        SV4[n] = in_slots(cv[1 - n], (126, 127, 0, 1), 4)
        SC[n] = edge_col[n]
        SU[n] = edge_cu[n]
        SV[n] = jnp.minimum(edge_col[n], north24(edge_col[n]))

    at_wall = jnp.where(
        jnp.logical_or(
            jnp.logical_and(row == 0, jnp.logical_not(has_south)),
            jnp.logical_and(row == ROWS - 1, jnp.logical_not(has_north)),
        ),
        19.0,
        20.0,
    )
    latitude = (row + gy * ROWS).astype(jnp.float32)
    f4 = (0.25 * DT) * (0.2 + 0.3 * (latitude + 0.5) / (ROWS * ny))
    centre_uv = 1.0 - (DT * NU) * at_wall
    centre_ts = 1.0 - KAPPA * at_wall

    received(G_A, size_a)
    left(G_A, size_a)

    @pl.loop(0, NC)
    def _(c):
        base = (c * LC).astype(jnp.float32)
        for f, depths in ((0, CU), (1, CV)):
            low, high = depths[6:14, :] - base, depths[10:18, :] - base
            for i in range(LC):
                k = c * LC + i
                a = jnp.where(low > i, X[f, k, 6:14, :], 0.0)
                b = jnp.where(high > i, X[f, k, 10:18, :], 0.0)
                X[f, k, 6:14, :] = a
                X[f, k, 10:18, :] = b

    def far(a, y, yy):
        z = 2.0 * y - 8.0 * a
        return yy + roll(z + roll(a, -1), -1) + roll(z + roll(a, 1), 1)

    class Slots:
        def __init__(self, count, width):
            shape = (count, ROWS, LANES)
            self.lanes = lax.broadcasted_iota(jnp.int32, shape, 2)
            self.place = lax.rem(self.lanes, width)
            tile = lax.broadcasted_iota(jnp.int32, shape, 0)
            self.level = (lax.div(self.lanes, width) + tile * (K // count)).astype(jnp.float32)
            self.west, self.east = self.place == width // 2 - 1, self.place == width // 2
            self.western = self.place < width // 2

        def beyond(self, west, east, f, r):
            return jnp.where(self.western, west[f, :, r : r + 8, :], east[f, :, r : r + 8, :])

        def if_wet(self, depths, n, r, x):
            return jnp.where(self.level < depths[n, r + 7 : r + 15, :][None], x, 0.0)

        def far(self, d, y):
            z = 2.0 * y - 8.0 * d
            return jnp.where(self.western, roll(d, -2), roll(d, 2)) + jnp.where(
                self.west, roll(z, -1), jnp.where(self.east, roll(z, 1), 0.0)
            )

    by4, by8 = Slots(NM, 4), Slots(NC, 8)

    def excess(f, depths, r):
        return by4.if_wet(depths, 0, r, by4.beyond(PW, PE, f, r)) - by4.if_wet(
            depths, 1, r, pack[f, :, r : r + 8, :]
        )

    du_s, du, du_n = [excess(0, SU4, r) for r in range(3)]
    dv_s, dv, dv_n = [excess(1, SV4, r) for r in range(3)]
    dw = by4.beyond(PW, PE, 2, 1) - pack[2, :, 1:9, :]
    dw = jnp.where(by4.west, roll(dw, -1), 0.0)
    run = dw
    for shift in (4, 8, 16, 32, 64):
        run = run + jnp.where(by4.lanes >= shift, roll(run, shift), 0.0)
    whole = jnp.broadcast_to(run[:, :, 4 * LM - 3 : 4 * LM - 2], run.shape)
    above = [zero]
    for c in range(NM - 1):
        above.append(above[-1] + whole[c])
    run = run + jnp.stack(above)
    EU[...] = jnp.where(by4.west, f4[None] * roll(dv + dv_s, -1) - run + 0.5 * dw, 0.0) - (
        DT * NU
    ) * by4.far(du, du_n + du_s)
    EV[...] = jnp.where(by4.east, -f4[None] * roll(du + du_n, 1), 0.0) - (DT * NU) * by4.far(
        dv, dv_n + dv_s
    )

    def momentum(c, carry):
        cum, cum_n, sum_u0, sum_v0, sum_u, sum_v = carry
        base = (c * LM).astype(jnp.float32)
        edge_u, edge_v = EU[c], EV[c]
        cu0, cv0 = CU[8:16, :] - base, CV[8:16, :] - base
        for i in range(LM):
            k = c * LM + i
            dz = thickness(base, i)
            uss, us, u, un, unn = [X[0, k, r : r + 8, :] for r in range(6, 11)]
            vss, vs, v, vn, vnn = [X[1, k, r : r + 8, :] for r in range(6, 11)]
            w, wn = WX[k, 0:8, :], WX[k, 1:9, :]
            cum = cum + w
            load = cum - 0.5 * w
            step_n = wn - w
            cum_n = cum_n + step_n
            cross_u = f4 * (v + vs)
            cross_v = f4 * (u + un)
            yu, yv = (DT * NU) * (un + us), (DT * NU) * (vn + vs)
            au, av = (DT * NU) * u, (DT * NU) * v
            zu, zv = 8.0 * au - 2.0 * yu, 8.0 * av - 2.0 * yv
            u1 = (
                centre_uv * u
                + 8.0 * yu
                - (DT * NU) * (unn + uss)
                + (cross_u + load)
                + roll((zu - roll(au, -1)) + (cross_u - load), -1)
                + roll(zu - roll(au, 1), 1)
                + jnp.where(edge4, unpacked(edge_u, i, 4), 0.0)
            )
            v1 = (
                centre_uv * v
                + 8.0 * yv
                - (DT * NU) * (vnn + vss)
                - cross_v
                - (cum_n - 0.5 * step_n)
                + roll(zv - roll(av, -1), -1)
                + roll((zv - roll(av, 1)) - cross_v, 1)
                + jnp.where(edge4, unpacked(edge_v, i, 4), 0.0)
            )
            u1 = jnp.where(cu0 > i, u1, 0.0)
            v1 = jnp.where(cv0 > i, v1, 0.0)
            sum_u0 = sum_u0 + u * dz
            sum_v0 = sum_v0 + v * dz
            sum_u = sum_u + u1 * dz
            sum_v = sum_v + v1 * dz
            U1B[k] = u1
            V1X[k, 8:16, :] = v1
        return cum, cum_n, sum_u0, sum_v0, sum_u, sum_v

    sums = lax.fori_loop(0, NM, momentum, (zero,) * 6)[2:]

    for n in range(4):
        F2[n, 1, 8:16, :] = sums[n]
    spread(G_SUM, F2, AROUND)

    @pl.loop(0, NC)
    def _(c):
        held_u = held_v = zero
        for i in range(LC):
            k = c * LC + i
            held_u = jnp.where(slot == i, packed(U1B[k], i), held_u)
            held_v = jnp.where(slot == i, packed(V1X[k, 8:16, :], i), held_v)
        pack1[0, c] = held_u
        pack1[1, c] = held_v

    for dx in (1, -1):
        side = P1W if dx > 0 else P1E
        send(G_B, pack1, side.at[:, :, pl.ds(1, 8), :], dx, 0)
        send(G_B, pack1.at[1, :, pl.ds(7, 1), :], side.at[1, :, pl.ds(0, 1), :], dx, 1)
    send(G_B, V1X.at[:, pl.ds(15, 1), :], V1X.at[:, pl.ds(7, 1), :], 0, 1)

    left(G_2D, size_2d)
    left(G_TS, size_ts)
    received(G_TS, size_ts)

    for f in range(2):
        HC[f] = by8.if_wet(SC, 0, 1, by8.beyond(TW, TE, f, 1))

    @pl.loop(0, NC)
    def _(c):
        base = (c * LC).astype(jnp.float32)
        low, mid, high = [CC[r : r + 8, :] - base for r in (7, 8, 9)]
        for f in range(2):
            edge = HC[f, c]
            for i in range(LC):
                k = c * LC + i
                south = jnp.where(low > i, X[2 + f, k, 7:15, :], 0.0)
                here = jnp.where(mid > i, X[2 + f, k, 8:16, :], 0.0)
                north = jnp.where(high > i, X[2 + f, k, 9:17, :], 0.0)
                X[2 + f, k, 7:15, :] = south
                X[2 + f, k, 9:17, :] = north
                CE[f, k] = here + roll(jnp.where(first, unpacked(edge, i), here), -1)

    def both(op, *pairs):
        return [op(*xs) for xs in zip(*pairs)]

    def depth_of(c):
        return c * (0.5 / K + c * (0.5 / (K * K)))

    open_u = [(x > 0.0).astype(jnp.float32) for x in cu]
    open_v = [(x > 0.0).astype(jnp.float32) for x in cv]
    depth_u = both(depth_of, cu)
    depth_v = both(depth_of, cv)
    pull_u = both(lambda o, d: o * d * (DB * GRAVITY), open_u, depth_u)
    pull_v = both(lambda o, d: o * d * (DB * GRAVITY), open_v, depth_v)
    pull_w = ring_west(*pull_u)
    ease = both(lambda o: jnp.where(o, DB, 0.0), ocean)
    height = [jnp.where(o, x, 0.0) for o, x in zip(ocean, sides(D2, 1))]

    received(G_SUM, size_sum)
    u0, v0, u_all, v_all = [list(sides(F2, f)) for f in range(4)]
    push_u = both(lambda o, a, b: o * ((a - b) * (DB / DT)), open_u, u_all, u0)
    push_v = both(lambda o, a, b: o * ((a - b) * (DB / DT)), open_v, v_all, v0)
    trans_u = both(lambda o, a: o * a, open_u, u0)
    trans_v = both(lambda o, a: o * a, open_v, v0)
    run_u = [jnp.zeros((24, LANES), jnp.float32)] * 2
    run_v = run_u

    def substep(_, state):
        level, trans_u, trans_w, trans_v, run_u, run_v = state
        level_w = ring_west(*level)
        trans_w = both(
            lambda t, p, q, h, w: t + (p - q * (h - w)), trans_w, push_w, pull_w, level, level_w
        )
        trans_u = both(
            lambda t, p, q, e, h: t + (p - q * (e - h)),
            trans_u,
            push_u,
            pull_u,
            ring_east(*level),
            level,
        )
        trans_v = both(
            lambda t, p, q, h: t + (p - q * (north24(h) - h)), trans_v, push_v, pull_v, level
        )
        level = both(
            lambda h, e, u, w, v: h - e * ((u - w) + (v - south24(v))),
            level,
            ease,
            trans_u,
            trans_w,
            trans_v,
        )
        return level, trans_u, trans_w, trans_v, both(jnp.add, run_u, trans_u), both(jnp.add, run_v, trans_v)

    trans_w, push_w = ring_west(*trans_u), ring_west(*push_u)
    state = height, trans_u, trans_w, trans_v, run_u, run_v
    for n in range(SUBSTEPS):
        state = substep(n, state)
    height, _, _, _, run_u, run_v = state

    HN[...] = height[0][8:16]

    def shift(r, a, d, o):
        return (r * (1.0 / SUBSTEPS) - a) / (d + (1.0 - o))

    shift_u = both(shift, run_u, u_all, depth_u, open_u)
    shift_v = both(shift, run_v, v_all, depth_v, open_v)
    DV[0] = shift_v[0]
    DV[1] = shift_v[1]
    du, dv, dvs = shift_u[0][8:16], shift_v[0][8:16], DV[0, 7:15, :]
    DP[0] = in_slots(shift_u[1][8:16], (125, 126, 127, 0, 1))
    DP[1] = in_slots(DV[1, 8:16, :], (126, 127, 0, 1))
    DP[2] = in_slots(DV[1, 7:15, :], (126, 127, 0, 1))
    DP[3] = jnp.broadcast_to(du[:, LANES - 1 :], du.shape)

    received(G_B, size_b)
    half = 0.5 * DTT

    edge_u = by8.if_wet(SU, 0, 1, by8.beyond(P1W, P1E, 0, 1) + DP[0][None]) * half
    edge_v = by8.if_wet(SV, 0, 1, by8.beyond(P1W, P1E, 1, 1) + DP[1][None]) * half
    edge_vs = by8.if_wet(SV, 0, 0, by8.beyond(P1W, P1E, 1, 0) + DP[2][None]) * half
    last_u = by8.if_wet(SU, 1, 1, pack1[0] + DP[3][None]) * half
    for f in range(2):
        south = by8.if_wet(SC, 0, 0, by8.beyond(TW, TE, f, 0))
        here = HC[f]
        north = by8.if_wet(SC, 0, 2, by8.beyond(TW, TE, f, 2))
        inner = by8.if_wet(SC, 1, 1, pack_ts[f, :, 1:9, :])
        flux = edge_u * (here + roll(jnp.where(by8.east, inner, here), -1))
        flux_last = last_u * (inner + roll(here, -1))
        flux_west = roll(jnp.where(by8.west, flux_last, flux), 1)
        a = here - ((flux - flux_west) + (edge_v * (here + north) - edge_vs * (south + here)))
        FW[f] = flux
        AO[f] = by8.if_wet(SC, 0, 1, a)

    def send_rows(c, up):
        src, dst, dy, group = (14, 6, 1, G_UP) if up else (8, 16, -1, G_DOWN)
        levels = pl.ds(c * LC, LC)
        send(
            group,
            AX.at[:, levels, pl.ds(src, 2), :],
            AX.at[:, levels, pl.ds(dst, 2), :],
            0,
            dy,
        )

    @pl.loop(0, NC)
    def _(c):
        base = (c * LC).astype(jnp.float32)
        edges = [FW[f, c] for f in range(2)]
        cc0, cu0, cv0 = CC[8:16, :] - base, CU[8:16, :] - base, CV[8:16, :] - base
        cvs = CV[7:15, :] - base
        held = [zero, zero]
        for i in range(LC):
            k = c * LC + i
            u = jnp.where(cu0 > i, U1B[k] + du, 0.0)
            v = jnp.where(cv0 > i, V1X[k, 8:16, :] + dv, 0.0)
            vs = jnp.where(cvs > i, V1X[k, 7:15, :] + dvs, 0.0) * half
            UN[k] = u
            VN[k] = v
            u = u * half
            v = v * half
            for f in range(2):
                south, here, north = [X[2 + f, k, r : r + 8, :] for r in (7, 8, 9)]
                edge = unpacked(edges[f], i)
                flux = u * CE[f, k]
                a = here - (
                    (flux - roll(jnp.where(last, edge, flux), 1))
                    + (v * (here + north) - vs * (south + here))
                )
                a = jnp.where(cc0 > i, a, 0.0)
                AX[f, k, 8:16, :] = a
                held[f] = jnp.where(slot == i, packed(a, i), held[f])
        for f in range(2):
            AD[f, c, 1:9, :] = AO[f, c] - held[f]

        @pl.when(has_north)
        def _():
            send_rows(c, True)

        @pl.when(has_south)
        def _():
            send_rows(c, False)

    @pl.when(has_north)
    def _():
        send(G_UP, AD.at[:, :, pl.ds(8, 1), :], AD.at[:, :, pl.ds(0, 1), :], 0, 1)

    @pl.when(has_south)
    def _():
        send(G_DOWN, AD.at[:, :, pl.ds(1, 1), :], AD.at[:, :, pl.ds(9, 1), :], 0, -1)

    left(G_SUM, size_sum)
    left(G_B, size_b)

    @pl.when(has_south)
    def _():
        received(G_UP, size_c)

    @pl.when(has_north)
    def _():
        received(G_DOWN, size_c)

    for f in range(2):
        south, here, north = [AD[f, :, r : r + 8, :] for r in range(3)]
        EM[f] = KAPPA * by8.far(here, south + north)

    @pl.loop(0, NC)
    def _(c):
        base = (c * LC).astype(jnp.float32)
        cc0 = CC[8:16, :] - base
        edges = [EM[f, c] for f in range(2)]
        for i in range(LC):
            k = c * LC + i
            for f, out in ((0, TN), (1, SN)):
                ss, s, a, n, nn = [AX[f, k, r : r + 8, :] for r in range(6, 11)]
                y = n + s
                mixed = (
                    centre_ts * a
                    - KAPPA * (far(a, y, nn + ss) - 8.0 * y)
                    - jnp.where(edge4, unpacked(edges[f], i), 0.0)
                )
                out[k] = jnp.where(cc0 > i, mixed, 0.0)

    @pl.when(has_north)
    def _():
        left(G_UP, size_c)

    @pl.when(has_south)
    def _():
        left(G_DOWN, size_c)


def write_out(*refs):
    copies = [pltpu.make_async_copy(refs[i], refs[5 + i], refs[10].at[i]) for i in range(5)]
    for copy in copies:
        copy.start()
    for copy in copies:
        copy.wait()


def per_device(nx, ny, *args):
    tile3 = jax.ShapeDtypeStruct((K, ROWS, LANES), jnp.float32)
    tile2 = jax.ShapeDtypeStruct((ROWS, LANES), jnp.float32)
    outs = (tile3, tile3, tile3, tile3, tile2)

    def vmem(*shape, dtype=jnp.float32):
        return pltpu.VMEM(shape, dtype)

    args = [pltpu.with_memory_space_constraint(x, pltpu.HBM) for x in args]
    held = pl.pallas_call(
        functools.partial(kernel, nx, ny),
        out_shape=tuple(pltpu.VMEM(x.shape, x.dtype) for x in outs),
        in_specs=[pl.BlockSpec(memory_space=pltpu.HBM)] * 7,
        out_specs=[pl.BlockSpec(memory_space=pltpu.VMEM)] * 5,
        scratch_shapes=[
            vmem(4, K, 24, LANES),
            vmem(K, 16, LANES),
            vmem(3, 3, 24, LANES),
            vmem(ROWS, LANES, dtype=jnp.int32),
            vmem(ROWS, LANES, dtype=jnp.int32),
            vmem(24, LANES),
            vmem(24, LANES),
            vmem(24, LANES),
            vmem(2, 24, LANES),
            vmem(2, 24, LANES),
            vmem(2, 24, LANES),
            vmem(2, 24, LANES),
            vmem(2, 24, LANES),
            vmem(3, NM, 16, LANES),
            vmem(3, NM, 16, LANES),
            vmem(3, NM, 16, LANES),
            vmem(2, NC, 16, LANES),
            vmem(2, NC, 16, LANES),
            vmem(2, NC, 16, LANES),
            vmem(4, 3, 24, LANES),
            vmem(2, 24, LANES),
            vmem(4, ROWS, LANES),
            vmem(K, ROWS, LANES),
            vmem(K, 16, LANES),
            vmem(2, NC, ROWS, LANES),
            vmem(2, NC, 16, LANES),
            vmem(2, NC, 16, LANES),
            vmem(2, K, 24, LANES),
            vmem(2, NC, 16, LANES),
            vmem(NM, ROWS, LANES),
            vmem(NM, ROWS, LANES),
            vmem(2, NC, ROWS, LANES),
            vmem(2, K, ROWS, LANES),
            vmem(2, NC, ROWS, LANES),
            vmem(2, NC, ROWS, LANES),
            vmem(2, NC, ROWS, LANES),
            pltpu.SemaphoreType.DMA((2,)),
            pltpu.SemaphoreType.DMA((GROUPS,)),
            pltpu.SemaphoreType.DMA((GROUPS,)),
        ],
        compiler_params=pltpu.CompilerParams(
            collective_id=0, has_side_effects=True, vmem_limit_bytes=24 * 1024 * 1024
        ),
    )(*args)
    return pl.pallas_call(
        write_out,
        out_shape=outs,
        in_specs=[pl.BlockSpec(memory_space=pltpu.VMEM)] * 5,
        out_specs=[pl.BlockSpec(memory_space=pltpu.HBM)] * 5,
        scratch_shapes=[pltpu.SemaphoreType.DMA((5,))],
        compiler_params=pltpu.CompilerParams(vmem_limit_bytes=8 * 1024 * 1024),
    )(*held)


def solution(mesh):
    placed = (P(None, "gy", "gx"),) * 4 + (P("gy", "gx"),) * 3
    return jax.shard_map(
        functools.partial(per_device, mesh.shape["gx"], mesh.shape["gy"]),
        mesh=mesh,
        in_specs=placed,
        out_specs=(P(None, "gy", "gx"),) * 4 + (P("gy", "gx"),),
        check_vma=False,
    )
```

```python
import functools

import jax
import jax.numpy as jnp
from jax import lax
from jax.experimental import pallas as pl
from jax.experimental.pallas import tpu as pltpu
from jax.sharding import PartitionSpec as P

MESH = pl.DeviceIdType.MESH
K = 75
NC = 5
LC = K // NC
NM = 5
LM = K // NM
SUBSTEPS = 8
ROWS = 8
LANES = 128

DT = 0.4
NU = 0.025
KAPPA = 0.01
DTT = 0.2
GRAVITY = 4.0
DB = DT / SUBSTEPS

AROUND = [(-1, -1), (1, -1), (-1, 1), (1, 1), (-1, 0), (1, 0), (0, -1), (0, 1)]
GROUPS = 7
G_2D, G_A, G_TS, G_SUM, G_B, G_UP, G_DOWN = range(GROUPS)


def kernel(
    nx,
    ny,
    t_in,
    s_in,
    u_in,
    v_in,
    h_in,
    flag_in,
    bottom_in,
    TN,
    SN,
    UN,
    VN,
    HN,
    X,
    PX,
    D2,
    flag_v,
    bottom_v,
    CC,
    CU,
    CV,
    SC,
    SU,
    SV,
    SU4,
    SV4,
    pack,
    PE,
    PW,
    pack_ts,
    TE,
    TW,
    F2,
    DV,
    DP,
    U1B,
    V1X,
    pack1,
    P1E,
    P1W,
    AX,
    AD,
    EU,
    EV,
    HC,
    CE,
    CN,
    FW,
    AO,
    EM,
    load_sem,
    send_sem,
    recv_sem,
):
    gx, gy = lax.axis_index("gx"), lax.axis_index("gy")

    def device(dx, dy):
        return (lax.rem(gx + dx + nx, nx), lax.rem(gy + dy + ny, ny))

    def send(group, src, dst, dx, dy):
        pltpu.make_async_remote_copy(
            src_ref=src,
            dst_ref=dst,
            send_sem=send_sem.at[group],
            recv_sem=recv_sem.at[group],
            device_id=device(dx, dy),
            device_id_type=MESH,
        ).start()

    def received(group, size):
        pltpu.make_async_copy(size, size, recv_sem.at[group]).wait()

    def left(group, size):
        pltpu.make_async_copy(size, size, send_sem.at[group]).wait()

    barrier = pltpu.get_barrier_semaphore()
    for dx, dy in AROUND:
        pl.semaphore_signal(barrier, inc=1, device_id=device(dx, dy), device_id_type=MESH)

    pltpu.make_async_copy(flag_in, flag_v, load_sem.at[0]).start()
    pltpu.make_async_copy(bottom_in, bottom_v, load_sem.at[0]).start()
    pltpu.make_async_copy(h_in, D2.at[1, 1, pl.ds(8, 8), :], load_sem.at[0]).start()
    for f, source in enumerate((u_in, v_in, t_in, s_in)):
        pltpu.make_async_copy(source, X.at[f, :, pl.ds(8, 8), :], load_sem.at[1]).start()

    def loaded(sem, size):
        pltpu.make_async_copy(size, size, load_sem.at[sem]).wait()

    lane = lax.broadcasted_iota(jnp.int32, (ROWS, LANES), 1)
    slot = lax.div(lane, 8).astype(jnp.float32)
    row = lax.broadcasted_iota(jnp.int32, (ROWS, LANES), 0)
    first, last = lane == 0, lane == LANES - 1
    half = 0.5 * DTT
    edge4 = jnp.logical_or(lane < 2, lane >= LANES - 2)
    slot4 = lax.div(lane, 4).astype(jnp.float32)
    has_south, has_north = gy > 0, gy < ny - 1
    zero = jnp.zeros((ROWS, LANES), jnp.float32)

    def roll(x, shift):
        return pltpu.roll(x, shift % LANES, x.ndim - 1)

    def packed(x, i, width=8):
        return roll(x, width * i + width // 2)

    def unpacked(x, i, width=8):
        return roll(x, LANES - width // 2 - width * i)

    def in_slots(x, lanes, width=8):
        at = lax.rem(lax.broadcasted_iota(jnp.int32, x.shape, 1), width)
        out = None
        for l in lanes:
            column = jnp.broadcast_to(x[:, l : l + 1], x.shape)
            out = column if out is None else jnp.where(at == (l + width // 2) % LANES, column, out)
        return out

    @pl.when(jnp.logical_not(has_south))
    def _():
        AD[:, :, 0:1, :] = jnp.zeros((2, NC, 1, LANES), jnp.float32)

        @pl.loop(0, K)
        def _(k):
            for f in range(2):
                AX[f, k, 6:8, :] = jnp.zeros((2, LANES), jnp.float32)

    @pl.when(jnp.logical_not(has_north))
    def _():
        AD[:, :, 9:10, :] = jnp.zeros((2, NC, 1, LANES), jnp.float32)

        @pl.loop(0, K)
        def _(k):
            for f in range(2):
                AX[f, k, 16:18, :] = jnp.zeros((2, LANES), jnp.float32)

    loaded(0, AX.at[0, pl.ds(0, 3), pl.ds(8, 8), :])
    own = (flag_v[...] * bottom_v[...]).astype(jnp.float32)
    D2[0, 1, 8:16, :] = own
    D2[2, 1, 8:16, :] = in_slots(own, (124, 125, 126, 127, 0, 1, 2, 3))

    def rows(group, fields, count, dy):
        src, dst = (16 - count, 8 - count) if dy > 0 else (8, 16)
        send(
            group,
            X.at[fields, :, pl.ds(src, count), :],
            X.at[fields, :, pl.ds(dst, count), :],
            0,
            dy,
        )

    loaded(1, X.at[:, :, pl.ds(8, 8), :])
    def weight(t, s, dz):
        return (0.8 * s - t * (0.2 + 0.05 * t)) * dz

    def thickness(base, i):
        return 0.5 / K + (base + (i + 0.5)) * (1.0 / (K * K))

    def press(c, cum):
        base = (c * LM).astype(jnp.float32)
        depth = D2[0, 1, 8:16, :] - base
        held = [zero] * 3
        for i in range(LM):
            k = c * LM + i
            u, v, t, s = [X[f, k, 8:16, :] for f in range(4)]
            w = jnp.where(depth > i, weight(t, s, DT * thickness(base, i)), 0.0)
            cum = cum + w
            load = cum - 0.5 * w
            PX[k, 0:8, :] = load
            for n, x in enumerate((u, v, load)):
                held[n] = jnp.where(slot4 == i, packed(x, i, 4), held[n])
        for n in range(3):
            pack[n, c, 1:9, :] = held[n]
        return cum

    lax.fori_loop(0, NM, press, zero)

    pl.semaphore_wait(barrier, len(AROUND))

    def corners(group, src, west, east, fields):
        for dx in (1, -1):
            for dy in (1, -1):
                side = west if dx > 0 else east
                r_src, r_dst = (8, 0) if dy > 0 else (1, 9)
                send(
                    group,
                    src.at[fields, :, pl.ds(r_src, 1), :],
                    side.at[fields, :, pl.ds(r_dst, 1), :],
                    dx,
                    dy,
                )

    def spread(group, ref, around):
        for dx, dy in around:
            send(
                group,
                ref.at[:, 1, pl.ds(8, 8), :],
                ref.at[:, 1 - dx, pl.ds(8 * (1 - dy), 8), :],
                dx,
                dy,
            )

    uv = pl.ds(0, 2)
    spread(G_2D, D2, AROUND[:4])
    corners(G_A, pack, PW, PE, uv)
    spread(G_2D, D2, AROUND[4:6])
    for dx in (1, -1):
        side = PW if dx > 0 else PE
        send(G_A, pack.at[:, :, pl.ds(1, 8), :], side.at[:, :, pl.ds(1, 8), :], dx, 0)
    spread(G_2D, D2, AROUND[6:])
    for dy in (1, -1):
        rows(G_A, uv, 2, dy)
    for dy in (1, -1):
        src, dst = (8, 0) if dy > 0 else (1, 9)
        send(G_A, pack.at[uv, :, pl.ds(src, 1), :], pack.at[uv, :, pl.ds(dst, 1), :], 0, dy)
    send(G_A, PX.at[:, pl.ds(0, 1), :], PX.at[:, pl.ds(8, 1), :], 0, -1)

    @pl.loop(0, NC)
    def _(c):
        held = [zero] * 2
        for i in range(LC):
            for f in range(2):
                held[f] = jnp.where(slot == i, packed(X[2 + f, c * LC + i, 8:16, :], i), held[f])
        for f in range(2):
            pack_ts[f, c, 1:9, :] = held[f]

    for dx in (1, -1):
        side = TW if dx > 0 else TE
        send(G_TS, pack_ts.at[:, :, pl.ds(1, 8), :], side.at[:, :, pl.ds(1, 8), :], dx, 0)
    corners(G_TS, pack_ts, TW, TE, uv)
    for dy in (1, -1):
        rows(G_TS, pl.ds(2, 2), 1, dy)

    def size(levels, count):
        return X.at[0, pl.ds(0, levels), pl.ds(0, count), :]

    size_2d = size(24, 8)
    size_a = size(K, 13)
    size_ts = size(50, 10)
    size_sum = size(32, 8)
    size_b = size(49, 5)
    size_c = size(62, 5)

    received(G_2D, size_2d)
    row24 = lax.broadcasted_iota(jnp.int32, (24, LANES), 0)
    lane24 = lax.broadcasted_iota(jnp.int32, (24, LANES), 1)
    slot24 = lax.rem(lane24, 8)
    first24, last24 = lane24 == 0, lane24 == LANES - 1
    inside = jnp.logical_and(
        jnp.logical_or(row24 >= 8, has_south), jnp.logical_or(row24 < 16, has_north)
    )

    def ring_east(c, h, seam=first24):
        return (
            roll(jnp.where(seam, h, c), LANES - 1),
            roll(jnp.where(seam, c, h), LANES - 1),
        )

    def ring_west(c, h):
        return (
            roll(jnp.where(last24, h, c), 1),
            roll(jnp.where(last24, c, h), 1),
        )

    def north24(x):
        return pltpu.roll(x, 23, 0)

    def south24(x):
        return pltpu.roll(x, 1, 0)

    def sides(ref, f):
        return ref[f, 1], jnp.where(lane24 < 64, ref[f, 2], ref[f, 0])

    col = [jnp.where(inside, x, 0.0) for x in sides(D2, 0)]
    ocean = [x > 0.0 for x in col]
    cu = [jnp.minimum(a, b) for a, b in zip(col, ring_east(*col))]
    cv = [jnp.minimum(a, north24(a)) for a in col]
    CC[...] = col[0]
    CU[...] = cu[0]
    CV[...] = cv[0]
    for n in range(2):
        SU4[n] = in_slots(cu[1 - n], (126, 127, 0, 1), 4)
        SV4[n] = in_slots(cv[1 - n], (126, 127, 0, 1), 4)

    at_wall = jnp.where(
        jnp.logical_or(
            jnp.logical_and(row == 0, jnp.logical_not(has_south)),
            jnp.logical_and(row == ROWS - 1, jnp.logical_not(has_north)),
        ),
        19.0,
        20.0,
    )
    latitude = (row + gy * ROWS).astype(jnp.float32)
    f4 = (0.25 * DT) * (0.2 + 0.3 * (latitude + 0.5) / (ROWS * ny))
    centre_uv = 1.0 - (DT * NU) * at_wall
    centre_ts = 1.0 - KAPPA * at_wall

    received(G_A, size_a)
    left(G_A, size_a)

    @pl.loop(0, NC)
    def _(c):
        base = (c * LC).astype(jnp.float32)
        for f, depths in ((0, CU), (1, CV)):
            low, high = depths[6:14, :] - base, depths[10:18, :] - base
            for i in range(LC):
                k = c * LC + i
                a = jnp.where(low > i, X[f, k, 6:14, :], 0.0)
                b = jnp.where(high > i, X[f, k, 10:18, :], 0.0)
                X[f, k, 6:14, :] = a
                X[f, k, 10:18, :] = b

    class Slots:
        def __init__(self, count, width):
            shape = (count, ROWS, LANES)
            self.lanes = lax.broadcasted_iota(jnp.int32, shape, 2)
            self.place = lax.rem(self.lanes, width)
            tile = lax.broadcasted_iota(jnp.int32, shape, 0)
            self.level = (lax.div(self.lanes, width) + tile * (K // count)).astype(jnp.float32)
            self.west, self.east = self.place == width // 2 - 1, self.place == width // 2
            self.western = self.place < width // 2

        def beyond(self, west, east, f, r):
            return jnp.where(self.western, west[f, :, r : r + 8, :], east[f, :, r : r + 8, :])

        def if_wet(self, depths, n, r, x):
            return jnp.where(self.level < depths[n, r + 7 : r + 15, :][None], x, 0.0)

        def far(self, d, y):
            z = 2.0 * y - 8.0 * d
            return jnp.where(self.western, roll(d, -2), roll(d, 2)) + jnp.where(
                self.west, roll(z, -1), jnp.where(self.east, roll(z, 1), 0.0)
            )

    by4, by8 = Slots(NM, 4), Slots(NC, 8)

    def excess(f, depths, r):
        return by4.if_wet(depths, 0, r, by4.beyond(PW, PE, f, r)) - by4.if_wet(
            depths, 1, r, pack[f, :, r : r + 8, :]
        )

    du_s, du, du_n = [excess(0, SU4, r) for r in range(3)]
    dv_s, dv, dv_n = [excess(1, SV4, r) for r in range(3)]
    dp = by4.beyond(PW, PE, 2, 1) - pack[2, :, 1:9, :]
    EU[...] = jnp.where(by4.west, roll(f4[None] * (dv + dv_s) - dp, -1), 0.0) - (
        DT * NU
    ) * by4.far(du, du_n + du_s)
    EV[...] = jnp.where(by4.east, -f4[None] * roll(du + du_n, 1), 0.0) - (DT * NU) * by4.far(
        dv, dv_n + dv_s
    )

    def momentum(c, carry):
        sum_u0, sum_v0, sum_u, sum_v = carry
        base = (c * LM).astype(jnp.float32)
        edge_u, edge_v = EU[c], EV[c]
        cu0, cv0 = CU[8:16, :] - base, CV[8:16, :] - base
        for i in range(LM):
            k = c * LM + i
            dz = thickness(base, i)
            uss, us, u, un, unn = [X[0, k, r : r + 8, :] for r in range(6, 11)]
            vss, vs, v, vn, vnn = [X[1, k, r : r + 8, :] for r in range(6, 11)]
            load, load_n = PX[k, 0:8, :], PX[k, 1:9, :]
            cross_u = f4 * (v + vs)
            cross_v = f4 * (u + un)
            yu, yv = (DT * NU) * (un + us), (DT * NU) * (vn + vs)
            au, av = (DT * NU) * u, (DT * NU) * v
            zu, zv = 8.0 * au - 2.0 * yu, 8.0 * av - 2.0 * yv
            u1 = (
                centre_uv * u
                + 8.0 * yu
                - (DT * NU) * (unn + uss)
                + (cross_u + load)
                + (roll(zu + (cross_u - load), -1) + roll(zu, 1))
                - (roll(au, -2) + roll(au, 2))
                + jnp.where(edge4, unpacked(edge_u, i, 4), 0.0)
            )
            v1 = (
                centre_uv * v
                + 8.0 * yv
                - (DT * NU) * (vnn + vss)
                - cross_v
                - (load_n - load)
                + (roll(zv, -1) + roll(zv - cross_v, 1))
                - (roll(av, -2) + roll(av, 2))
                + jnp.where(edge4, unpacked(edge_v, i, 4), 0.0)
            )
            u1 = jnp.where(cu0 > i, u1, 0.0)
            v1 = jnp.where(cv0 > i, v1, 0.0)
            sum_u0 = sum_u0 + u * dz
            sum_v0 = sum_v0 + v * dz
            sum_u = sum_u + u1 * dz
            sum_v = sum_v + v1 * dz
            U1B[k] = u1
            V1X[k, 8:16, :] = v1
        return sum_u0, sum_v0, sum_u, sum_v

    sums = lax.fori_loop(0, NM, momentum, (zero,) * 4)

    for n in range(4):
        F2[n, 1, 8:16, :] = sums[n]
    spread(G_SUM, F2, AROUND)

    @pl.loop(0, NC)
    def _(c):
        held_u = held_v = zero
        for i in range(LC):
            k = c * LC + i
            held_u = jnp.where(slot == i, packed(U1B[k], i), held_u)
            held_v = jnp.where(slot == i, packed(V1X[k, 8:16, :], i), held_v)
        pack1[0, c] = held_u
        pack1[1, c] = held_v

    for dx in (1, -1):
        side = P1W if dx > 0 else P1E
        send(G_B, pack1, side.at[:, :, pl.ds(1, 8), :], dx, 0)
        send(G_B, pack1.at[1, :, pl.ds(7, 1), :], side.at[1, :, pl.ds(0, 1), :], dx, 1)
    send(G_B, V1X.at[:, pl.ds(15, 1), :], V1X.at[:, pl.ds(7, 1), :], 0, 1)

    left(G_2D, size_2d)
    left(G_TS, size_ts)
    received(G_TS, size_ts)

    edge_col = [
        jnp.where(inside, x, 0.0)
        for x in (jnp.where(slot24 < 4, D2[2, 0], D2[2, 2]), D2[2, 1])
    ]
    edge_cu = [jnp.minimum(a, b) for a, b in zip(edge_col, ring_east(*edge_col, slot24 == 4))]
    for n in range(2):
        SC[n] = edge_col[n]
        SU[n] = edge_cu[n]
        SV[n] = jnp.minimum(edge_col[n], north24(edge_col[n]))

    for f in range(2):
        HC[f] = by8.if_wet(SC, 0, 1, by8.beyond(TW, TE, f, 1))

    @pl.loop(0, NC)
    def _(c):
        base = (c * LC).astype(jnp.float32)
        low, mid, high = [CC[r : r + 8, :] - base for r in (7, 8, 9)]
        for f in range(2):
            edge = HC[f, c]
            for i in range(LC):
                k = c * LC + i
                south = jnp.where(low > i, X[2 + f, k, 7:15, :], 0.0)
                here = jnp.where(mid > i, X[2 + f, k, 8:16, :], 0.0)
                north = jnp.where(high > i, X[2 + f, k, 9:17, :], 0.0)
                X[2 + f, k, 7:15, :] = south
                X[2 + f, k, 9:17, :] = north
                east = jnp.where(last, roll(edge, LANES - 5 - 8 * i), roll(here, -1))
                CE[f, k] = half * (here + east)
                CN[f, k, 7:15, :] = half * (south + here)
                CN[f, k, 8:16, :] = half * (here + north)

    def both(op, *pairs):
        return [op(*xs) for xs in zip(*pairs)]

    def depth_of(c):
        return c * (0.5 / K + c * (0.5 / (K * K)))

    open_u = [(x > 0.0).astype(jnp.float32) for x in cu]
    open_v = [(x > 0.0).astype(jnp.float32) for x in cv]
    depth_u = both(depth_of, cu)
    depth_v = both(depth_of, cv)
    pull_u = both(lambda o, d: o * d * (DB * GRAVITY), open_u, depth_u)
    pull_v = both(lambda o, d: o * d * (DB * GRAVITY), open_v, depth_v)
    pull_w = ring_west(*pull_u)
    ease = both(lambda o: jnp.where(o, DB, 0.0), ocean)
    height = [jnp.where(o, x, 0.0) for o, x in zip(ocean, sides(D2, 1))]

    received(G_SUM, size_sum)
    u0, v0, u_all, v_all = [list(sides(F2, f)) for f in range(4)]
    push_u = both(lambda o, a, b: o * ((a - b) * (DB / DT)), open_u, u_all, u0)
    push_v = both(lambda o, a, b: o * ((a - b) * (DB / DT)), open_v, v_all, v0)
    trans_u = both(lambda o, a: o * a, open_u, u0)
    trans_v = both(lambda o, a: o * a, open_v, v0)
    run_u = [jnp.zeros((24, LANES), jnp.float32)] * 2
    run_v = run_u

    def substep(_, state):
        level, trans_u, trans_w, trans_v, run_u, run_v = state
        level_w = ring_west(*level)
        trans_w = both(
            lambda t, p, q, h, w: t + (p - q * (h - w)), trans_w, push_w, pull_w, level, level_w
        )
        trans_u = both(
            lambda t, p, q, e, h: t + (p - q * (e - h)),
            trans_u,
            push_u,
            pull_u,
            ring_east(*level),
            level,
        )
        trans_v = both(
            lambda t, p, q, h: t + (p - q * (north24(h) - h)), trans_v, push_v, pull_v, level
        )
        level = both(
            lambda h, e, u, w, v: h - e * ((u - w) + (v - south24(v))),
            level,
            ease,
            trans_u,
            trans_w,
            trans_v,
        )
        return level, trans_u, trans_w, trans_v, both(jnp.add, run_u, trans_u), both(jnp.add, run_v, trans_v)

    trans_w, push_w = ring_west(*trans_u), ring_west(*push_u)
    state = height, trans_u, trans_w, trans_v, run_u, run_v
    for n in range(SUBSTEPS):
        state = substep(n, state)
    height, _, _, _, run_u, run_v = state

    HN[...] = height[0][8:16]

    def shift(r, a, d, o):
        return (r * (1.0 / SUBSTEPS) - a) / (d + (1.0 - o))

    shift_u = both(shift, run_u, u_all, depth_u, open_u)
    shift_v = both(shift, run_v, v_all, depth_v, open_v)
    DV[0] = shift_v[0]
    DV[1] = shift_v[1]
    du, dv, dvs = shift_u[0][8:16], shift_v[0][8:16], DV[0, 7:15, :]
    DP[0] = in_slots(shift_u[1][8:16], (125, 126, 127, 0, 1))
    DP[1] = in_slots(DV[1, 8:16, :], (126, 127, 0, 1))
    DP[2] = in_slots(DV[1, 7:15, :], (126, 127, 0, 1))
    DP[3] = jnp.broadcast_to(du[:, LANES - 1 :], du.shape)

    received(G_B, size_b)
    edge_u = by8.if_wet(SU, 0, 1, by8.beyond(P1W, P1E, 0, 1) + DP[0][None]) * half
    edge_v = by8.if_wet(SV, 0, 1, by8.beyond(P1W, P1E, 1, 1) + DP[1][None]) * half
    edge_vs = by8.if_wet(SV, 0, 0, by8.beyond(P1W, P1E, 1, 0) + DP[2][None]) * half
    last_u = by8.if_wet(SU, 1, 1, pack1[0] + DP[3][None]) * half
    for f in range(2):
        south = by8.if_wet(SC, 0, 0, by8.beyond(TW, TE, f, 0))
        here = HC[f]
        north = by8.if_wet(SC, 0, 2, by8.beyond(TW, TE, f, 2))
        inner = by8.if_wet(SC, 1, 1, pack_ts[f, :, 1:9, :])
        flux = edge_u * (here + roll(jnp.where(by8.east, inner, here), -1))
        flux_last = last_u * (inner + roll(here, -1))
        flux_west = roll(jnp.where(by8.west, flux_last, flux), 1)
        a = here - ((flux - flux_west) + (edge_v * (here + north) - edge_vs * (south + here)))
        FW[f] = flux
        AO[f] = by8.if_wet(SC, 0, 1, a)

    def send_rows(c, up):
        src, dst, dy, group = (14, 6, 1, G_UP) if up else (8, 16, -1, G_DOWN)
        levels = pl.ds(c * LC, LC)
        send(
            group,
            AX.at[:, levels, pl.ds(src, 2), :],
            AX.at[:, levels, pl.ds(dst, 2), :],
            0,
            dy,
        )

    @pl.loop(0, NC)
    def _(c):
        base = (c * LC).astype(jnp.float32)
        edges = [FW[f, c] for f in range(2)]
        cc0, cu0, cv0 = CC[8:16, :] - base, CU[8:16, :] - base, CV[8:16, :] - base
        cvs = CV[7:15, :] - base
        held = [zero, zero]
        for i in range(LC):
            k = c * LC + i
            u = jnp.where(cu0 > i, U1B[k] + du, 0.0)
            v = jnp.where(cv0 > i, V1X[k, 8:16, :] + dv, 0.0)
            vs = jnp.where(cvs > i, V1X[k, 7:15, :] + dvs, 0.0)
            UN[k] = u
            VN[k] = v
            for f in range(2):
                flux = u * CE[f, k]
                flux_west = jnp.where(first, roll(edges[f], LANES - 3 - 8 * i), roll(flux, 1))
                a = X[2 + f, k, 8:16, :] - (
                    (flux - flux_west) + (v * CN[f, k, 8:16, :] - vs * CN[f, k, 7:15, :])
                )
                a = jnp.where(cc0 > i, a, 0.0)
                AX[f, k, 8:16, :] = a
                held[f] = jnp.where(slot == i, packed(a, i), held[f])
        for f in range(2):
            AD[f, c, 1:9, :] = AO[f, c] - held[f]

        @pl.when(has_north)
        def _():
            send_rows(c, True)

        @pl.when(has_south)
        def _():
            send_rows(c, False)

    @pl.when(has_north)
    def _():
        send(G_UP, AD.at[:, :, pl.ds(8, 1), :], AD.at[:, :, pl.ds(0, 1), :], 0, 1)

    @pl.when(has_south)
    def _():
        send(G_DOWN, AD.at[:, :, pl.ds(1, 1), :], AD.at[:, :, pl.ds(9, 1), :], 0, -1)

    left(G_SUM, size_sum)
    left(G_B, size_b)

    @pl.loop(0, NC)
    def _(c):
        for i in range(LC):
            k = c * LC + i
            for f, out in ((0, TN), (1, SN)):
                a = AX[f, k, 8:16, :]
                b = KAPPA * a
                out[k] = (
                    centre_ts * a
                    + 8.0 * (roll(b, -1) + roll(b, 1))
                    - (roll(b, -2) + roll(b, 2))
                )

    @pl.when(has_south)
    def _():
        received(G_UP, size_c)

    @pl.when(has_north)
    def _():
        received(G_DOWN, size_c)

    for f in range(2):
        south, here, north = [AD[f, :, r : r + 8, :] for r in range(3)]
        EM[f] = KAPPA * by8.far(here, south + north)

    @pl.loop(0, NC)
    def _(c):
        base = (c * LC).astype(jnp.float32)
        cc0 = CC[8:16, :] - base
        edges = [EM[f, c] for f in range(2)]
        for i in range(LC):
            k = c * LC + i
            for f, out in ((0, TN), (1, SN)):
                ss, s, n, nn = [AX[f, k, r : r + 8, :] for r in (6, 7, 9, 10)]
                y = KAPPA * (n + s)
                mixed = (
                    out[k]
                    + 8.0 * y
                    - 2.0 * (roll(y, -1) + roll(y, 1))
                    - KAPPA * (nn + ss)
                    - jnp.where(edge4, unpacked(edges[f], i), 0.0)
                )
                out[k] = jnp.where(cc0 > i, mixed, 0.0)

    @pl.when(has_north)
    def _():
        left(G_UP, size_c)

    @pl.when(has_south)
    def _():
        left(G_DOWN, size_c)


def write_out(*refs):
    copies = [pltpu.make_async_copy(refs[i], refs[5 + i], refs[10].at[i]) for i in range(5)]
    for copy in copies:
        copy.start()
    for copy in copies:
        copy.wait()


def per_device(nx, ny, *args):
    tile3 = jax.ShapeDtypeStruct((K, ROWS, LANES), jnp.float32)
    tile2 = jax.ShapeDtypeStruct((ROWS, LANES), jnp.float32)
    outs = (tile3, tile3, tile3, tile3, tile2)

    def vmem(*shape, dtype=jnp.float32):
        return pltpu.VMEM(shape, dtype)

    args = [pltpu.with_memory_space_constraint(x, pltpu.HBM) for x in args]
    held = pl.pallas_call(
        functools.partial(kernel, nx, ny),
        out_shape=tuple(pltpu.VMEM(x.shape, x.dtype) for x in outs),
        in_specs=[pl.BlockSpec(memory_space=pltpu.HBM)] * 7,
        out_specs=[pl.BlockSpec(memory_space=pltpu.VMEM)] * 5,
        scratch_shapes=[
            vmem(4, K, 24, LANES),
            vmem(K, 16, LANES),
            vmem(3, 3, 24, LANES),
            vmem(ROWS, LANES, dtype=jnp.int32),
            vmem(ROWS, LANES, dtype=jnp.int32),
            vmem(24, LANES),
            vmem(24, LANES),
            vmem(24, LANES),
            vmem(2, 24, LANES),
            vmem(2, 24, LANES),
            vmem(2, 24, LANES),
            vmem(2, 24, LANES),
            vmem(2, 24, LANES),
            vmem(3, NM, 16, LANES),
            vmem(3, NM, 16, LANES),
            vmem(3, NM, 16, LANES),
            vmem(2, NC, 16, LANES),
            vmem(2, NC, 16, LANES),
            vmem(2, NC, 16, LANES),
            vmem(4, 3, 24, LANES),
            vmem(2, 24, LANES),
            vmem(4, ROWS, LANES),
            vmem(K, ROWS, LANES),
            vmem(K, 16, LANES),
            vmem(2, NC, ROWS, LANES),
            vmem(2, NC, 16, LANES),
            vmem(2, NC, 16, LANES),
            vmem(2, K, 24, LANES),
            vmem(2, NC, 16, LANES),
            vmem(NM, ROWS, LANES),
            vmem(NM, ROWS, LANES),
            vmem(2, NC, ROWS, LANES),
            vmem(2, K, ROWS, LANES),
            vmem(2, K, 16, LANES),
            vmem(2, NC, ROWS, LANES),
            vmem(2, NC, ROWS, LANES),
            vmem(2, NC, ROWS, LANES),
            pltpu.SemaphoreType.DMA((2,)),
            pltpu.SemaphoreType.DMA((GROUPS,)),
            pltpu.SemaphoreType.DMA((GROUPS,)),
        ],
        compiler_params=pltpu.CompilerParams(
            collective_id=0, has_side_effects=True, vmem_limit_bytes=24 * 1024 * 1024
        ),
    )(*args)
    return pl.pallas_call(
        write_out,
        out_shape=outs,
        in_specs=[pl.BlockSpec(memory_space=pltpu.VMEM)] * 5,
        out_specs=[pl.BlockSpec(memory_space=pltpu.HBM)] * 5,
        scratch_shapes=[pltpu.SemaphoreType.DMA((5,))],
        compiler_params=pltpu.CompilerParams(vmem_limit_bytes=8 * 1024 * 1024),
    )(*held)


def solution(mesh):
    placed = (P(None, "gy", "gx"),) * 4 + (P("gy", "gx"),) * 3
    return jax.shard_map(
        functools.partial(per_device, mesh.shape["gx"], mesh.shape["gy"]),
        mesh=mesh,
        in_specs=placed,
        out_specs=(P(None, "gy", "gx"),) * 4 + (P("gy", "gx"),),
        check_vma=False,
    )
```

```python
import functools

import jax
import jax.numpy as jnp
from jax import lax
from jax.experimental import pallas as pl
from jax.experimental.pallas import tpu as pltpu
from jax.sharding import PartitionSpec as P

MESH = pl.DeviceIdType.MESH
K = 75
NC = 5
LC = K // NC
NM = 5
LM = K // NM
SUBSTEPS = 8
ROWS = 8
LANES = 128

DT = 0.4
NU = 0.025
KAPPA = 0.01
DTT = 0.2
GRAVITY = 4.0
DB = DT / SUBSTEPS

AROUND = [(-1, -1), (1, -1), (-1, 1), (1, 1), (-1, 0), (1, 0), (0, -1), (0, 1)]
GROUPS = 7
G_2D, G_A, G_TS, G_SUM, G_B, G_UP, G_DOWN = range(GROUPS)


def kernel(
    nx,
    ny,
    t_in,
    s_in,
    u_in,
    v_in,
    h_in,
    flag_in,
    bottom_in,
    TN,
    SN,
    UN,
    VN,
    HN,
    AX,
    EM,
    CC,
    X,
    PX,
    D2,
    flag_v,
    bottom_v,
    CU,
    CV,
    SC,
    SU,
    SV,
    SU4,
    SV4,
    pack,
    PE,
    PW,
    pack_ts,
    TE,
    TW,
    F2,
    DV,
    DP,
    U1B,
    V1X,
    pack1,
    P1E,
    P1W,
    AD,
    EU,
    EV,
    HC,
    CE,
    CN,
    FW,
    AO,
    HS,
    load_sem,
    send_sem,
    recv_sem,
):
    gx, gy = lax.axis_index("gx"), lax.axis_index("gy")

    def device(dx, dy):
        return (lax.rem(gx + dx + nx, nx), lax.rem(gy + dy + ny, ny))

    def send(group, src, dst, dx, dy):
        pltpu.make_async_remote_copy(
            src_ref=src,
            dst_ref=dst,
            send_sem=send_sem.at[group],
            recv_sem=recv_sem.at[group],
            device_id=device(dx, dy),
            device_id_type=MESH,
        ).start()

    def received(group, size):
        pltpu.make_async_copy(size, size, recv_sem.at[group]).wait()

    def left(group, size):
        pltpu.make_async_copy(size, size, send_sem.at[group]).wait()

    barrier = pltpu.get_barrier_semaphore()
    for dx, dy in AROUND:
        pl.semaphore_signal(barrier, inc=1, device_id=device(dx, dy), device_id_type=MESH)

    pltpu.make_async_copy(flag_in, flag_v, load_sem.at[0]).start()
    pltpu.make_async_copy(bottom_in, bottom_v, load_sem.at[0]).start()
    pltpu.make_async_copy(h_in, D2.at[1, 1, pl.ds(8, 8), :], load_sem.at[0]).start()
    for f, source in enumerate((u_in, v_in, t_in, s_in)):
        pltpu.make_async_copy(source, X.at[f, :, pl.ds(8, 8), :], load_sem.at[1]).start()

    def loaded(sem, size):
        pltpu.make_async_copy(size, size, load_sem.at[sem]).wait()

    lane = lax.broadcasted_iota(jnp.int32, (ROWS, LANES), 1)
    slot = lax.div(lane, 8).astype(jnp.float32)
    row = lax.broadcasted_iota(jnp.int32, (ROWS, LANES), 0)
    first, last = lane == 0, lane == LANES - 1
    half = 0.5 * DTT
    edge4 = jnp.logical_or(lane < 2, lane >= LANES - 2)
    slot4 = lax.div(lane, 4).astype(jnp.float32)
    has_south, has_north = gy > 0, gy < ny - 1
    zero = jnp.zeros((ROWS, LANES), jnp.float32)

    def roll(x, shift):
        return pltpu.roll(x, shift % LANES, x.ndim - 1)

    def packed(x, i, width=8):
        return roll(x, width * i + width // 2)

    def unpacked(x, i, width=8):
        return roll(x, LANES - width // 2 - width * i)

    def in_slots(x, lanes, width=8):
        at = lax.rem(lax.broadcasted_iota(jnp.int32, x.shape, 1), width)
        out = None
        for l in lanes:
            column = jnp.broadcast_to(x[:, l : l + 1], x.shape)
            out = column if out is None else jnp.where(at == (l + width // 2) % LANES, column, out)
        return out

    @pl.when(jnp.logical_not(has_south))
    def _():
        AD[:, :, 0:1, :] = jnp.zeros((2, NC, 1, LANES), jnp.float32)

        @pl.loop(0, K)
        def _(k):
            for f in range(2):
                AX[f, k, 6:8, :] = jnp.zeros((2, LANES), jnp.float32)

    @pl.when(jnp.logical_not(has_north))
    def _():
        AD[:, :, 9:10, :] = jnp.zeros((2, NC, 1, LANES), jnp.float32)

        @pl.loop(0, K)
        def _(k):
            for f in range(2):
                AX[f, k, 16:18, :] = jnp.zeros((2, LANES), jnp.float32)

    loaded(0, AX.at[0, pl.ds(0, 3), pl.ds(8, 8), :])
    own = (flag_v[...] * bottom_v[...]).astype(jnp.float32)
    D2[0, 1, 8:16, :] = own
    D2[2, 1, 8:16, :] = in_slots(own, (124, 125, 126, 127, 0, 1, 2, 3))

    def rows(group, fields, count, dy):
        src, dst = (16 - count, 8 - count) if dy > 0 else (8, 16)
        send(
            group,
            X.at[fields, :, pl.ds(src, count), :],
            X.at[fields, :, pl.ds(dst, count), :],
            0,
            dy,
        )

    loaded(1, X.at[:, :, pl.ds(8, 8), :])
    def weight(t, s, dz):
        return (0.8 * s - t * (0.2 + 0.05 * t)) * dz

    def thickness(base, i):
        return 0.5 / K + (base + (i + 0.5)) * (1.0 / (K * K))

    def press(c, cum):
        base = (c * LM).astype(jnp.float32)
        depth = D2[0, 1, 8:16, :] - base
        held = [zero] * 3
        for i in range(LM):
            k = c * LM + i
            u, v, t, s = [X[f, k, 8:16, :] for f in range(4)]
            w = jnp.where(depth > i, weight(t, s, DT * thickness(base, i)), 0.0)
            cum = cum + w
            load = cum - 0.5 * w
            PX[k, 0:8, :] = load
            for n, x in enumerate((u, v, load)):
                held[n] = jnp.where(slot4 == i, packed(x, i, 4), held[n])
        for n in range(3):
            pack[n, c, 1:9, :] = held[n]
        return cum

    lax.fori_loop(0, NM, press, zero)

    pl.semaphore_wait(barrier, len(AROUND))

    def corners(group, src, west, east, fields):
        for dx in (1, -1):
            for dy in (1, -1):
                side = west if dx > 0 else east
                r_src, r_dst = (8, 0) if dy > 0 else (1, 9)
                send(
                    group,
                    src.at[fields, :, pl.ds(r_src, 1), :],
                    side.at[fields, :, pl.ds(r_dst, 1), :],
                    dx,
                    dy,
                )

    def spread(group, ref, around):
        for dx, dy in around:
            send(
                group,
                ref.at[:, 1, pl.ds(8, 8), :],
                ref.at[:, 1 - dx, pl.ds(8 * (1 - dy), 8), :],
                dx,
                dy,
            )

    uv = pl.ds(0, 2)
    spread(G_2D, D2, AROUND[:4])
    corners(G_A, pack, PW, PE, uv)
    spread(G_2D, D2, AROUND[4:6])
    for dx in (1, -1):
        side = PW if dx > 0 else PE
        send(G_A, pack.at[:, :, pl.ds(1, 8), :], side.at[:, :, pl.ds(1, 8), :], dx, 0)
    spread(G_2D, D2, AROUND[6:])
    for dy in (1, -1):
        rows(G_A, uv, 2, dy)
    for dy in (1, -1):
        src, dst = (8, 0) if dy > 0 else (1, 9)
        send(G_A, pack.at[uv, :, pl.ds(src, 1), :], pack.at[uv, :, pl.ds(dst, 1), :], 0, dy)
    send(G_A, PX.at[:, pl.ds(0, 1), :], PX.at[:, pl.ds(8, 1), :], 0, -1)

    @pl.loop(0, NC)
    def _(c):
        held = [zero] * 2
        for i in range(LC):
            for f in range(2):
                held[f] = jnp.where(slot == i, packed(X[2 + f, c * LC + i, 8:16, :], i), held[f])
        for f in range(2):
            pack_ts[f, c, 1:9, :] = held[f]

    for dx in (1, -1):
        side = TW if dx > 0 else TE
        send(G_TS, pack_ts.at[:, :, pl.ds(1, 8), :], side.at[:, :, pl.ds(1, 8), :], dx, 0)
    corners(G_TS, pack_ts, TW, TE, uv)
    for dy in (1, -1):
        rows(G_TS, pl.ds(2, 2), 1, dy)

    def size(levels, count):
        return X.at[0, pl.ds(0, levels), pl.ds(0, count), :]

    size_2d = size(24, 8)
    size_a = size(K, 13)
    size_ts = size(50, 10)
    size_sum = size(32, 8)
    size_b = size(49, 5)
    size_c = size(62, 5)

    received(G_2D, size_2d)
    row24 = lax.broadcasted_iota(jnp.int32, (24, LANES), 0)
    lane24 = lax.broadcasted_iota(jnp.int32, (24, LANES), 1)
    slot24 = lax.rem(lane24, 8)
    first24, last24 = lane24 == 0, lane24 == LANES - 1
    inside = jnp.logical_and(
        jnp.logical_or(row24 >= 8, has_south), jnp.logical_or(row24 < 16, has_north)
    )

    def ring_east(c, h, seam=first24):
        return (
            roll(jnp.where(seam, h, c), LANES - 1),
            roll(jnp.where(seam, c, h), LANES - 1),
        )

    def ring_west(c, h):
        return (
            roll(jnp.where(last24, h, c), 1),
            roll(jnp.where(last24, c, h), 1),
        )

    def north24(x):
        return pltpu.roll(x, 23, 0)

    def south24(x):
        return pltpu.roll(x, 1, 0)

    def sides(ref, f):
        return ref[f, 1], jnp.where(lane24 < 64, ref[f, 2], ref[f, 0])

    col = [jnp.where(inside, x, 0.0) for x in sides(D2, 0)]
    ocean = [x > 0.0 for x in col]
    cu = [jnp.minimum(a, b) for a, b in zip(col, ring_east(*col))]
    cv = [jnp.minimum(a, north24(a)) for a in col]
    CC[...] = col[0]
    CU[...] = cu[0]
    CV[...] = cv[0]
    for n in range(2):
        SU4[n] = in_slots(cu[1 - n], (126, 127, 0, 1), 4)
        SV4[n] = in_slots(cv[1 - n], (126, 127, 0, 1), 4)

    at_wall = jnp.where(
        jnp.logical_or(
            jnp.logical_and(row == 0, jnp.logical_not(has_south)),
            jnp.logical_and(row == ROWS - 1, jnp.logical_not(has_north)),
        ),
        19.0,
        20.0,
    )
    latitude = (row + gy * ROWS).astype(jnp.float32)
    f4 = (0.25 * DT) * (0.2 + 0.3 * (latitude + 0.5) / (ROWS * ny))
    centre_uv = 1.0 - (DT * NU) * at_wall
    centre_ts = 1.0 - KAPPA * at_wall

    received(G_A, size_a)
    left(G_A, size_a)

    @pl.loop(0, NC)
    def _(c):
        base = (c * LC).astype(jnp.float32)
        for f, depths in ((0, CU), (1, CV)):
            low, high = depths[6:14, :] - base, depths[10:18, :] - base
            for i in range(LC):
                k = c * LC + i
                a = jnp.where(low > i, X[f, k, 6:14, :], 0.0)
                b = jnp.where(high > i, X[f, k, 10:18, :], 0.0)
                X[f, k, 6:14, :] = a
                X[f, k, 10:18, :] = b

    class Slots:
        def __init__(self, count, width):
            shape = (count, ROWS, LANES)
            self.lanes = lax.broadcasted_iota(jnp.int32, shape, 2)
            self.place = lax.rem(self.lanes, width)
            tile = lax.broadcasted_iota(jnp.int32, shape, 0)
            self.level = (lax.div(self.lanes, width) + tile * (K // count)).astype(jnp.float32)
            self.west, self.east = self.place == width // 2 - 1, self.place == width // 2
            self.western = self.place < width // 2

        def beyond(self, west, east, f, r):
            return jnp.where(self.western, west[f, :, r : r + 8, :], east[f, :, r : r + 8, :])

        def if_wet(self, depths, n, r, x):
            return jnp.where(self.level < depths[n, r + 7 : r + 15, :][None], x, 0.0)

        def far(self, d, y):
            z = 2.0 * y - 8.0 * d
            return jnp.where(self.western, roll(d, -2), roll(d, 2)) + jnp.where(
                self.west, roll(z, -1), jnp.where(self.east, roll(z, 1), 0.0)
            )

    by4, by8 = Slots(NM, 4), Slots(NC, 8)

    def excess(f, depths, r):
        return by4.if_wet(depths, 0, r, by4.beyond(PW, PE, f, r)) - by4.if_wet(
            depths, 1, r, pack[f, :, r : r + 8, :]
        )

    du_s, du, du_n = [excess(0, SU4, r) for r in range(3)]
    dv_s, dv, dv_n = [excess(1, SV4, r) for r in range(3)]
    dp = by4.beyond(PW, PE, 2, 1) - pack[2, :, 1:9, :]
    EU[...] = jnp.where(by4.west, roll(f4[None] * (dv + dv_s) - dp, -1), 0.0) - (
        DT * NU
    ) * by4.far(du, du_n + du_s)
    EV[...] = jnp.where(by4.east, -f4[None] * roll(du + du_n, 1), 0.0) - (DT * NU) * by4.far(
        dv, dv_n + dv_s
    )

    def momentum(c, carry):
        sum_u0, sum_v0, sum_u, sum_v = carry
        base = (c * LM).astype(jnp.float32)
        edge_u, edge_v = EU[c], EV[c]
        cu0, cv0 = CU[8:16, :] - base, CV[8:16, :] - base
        for i in range(LM):
            k = c * LM + i
            dz = thickness(base, i)
            uss, us, u, un, unn = [X[0, k, r : r + 8, :] for r in range(6, 11)]
            vss, vs, v, vn, vnn = [X[1, k, r : r + 8, :] for r in range(6, 11)]
            load, load_n = PX[k, 0:8, :], PX[k, 1:9, :]
            cross_u = f4 * (v + vs)
            cross_v = f4 * (u + un)
            yu, yv = (DT * NU) * (un + us), (DT * NU) * (vn + vs)
            au, av = (DT * NU) * u, (DT * NU) * v
            zu, zv = 8.0 * au - 2.0 * yu, 8.0 * av - 2.0 * yv
            u1 = (
                centre_uv * u
                + 8.0 * yu
                - (DT * NU) * (unn + uss)
                + (cross_u + load)
                + (roll(zu + (cross_u - load), -1) + roll(zu, 1))
                - (roll(au, -2) + roll(au, 2))
                + jnp.where(edge4, unpacked(edge_u, i, 4), 0.0)
            )
            v1 = (
                centre_uv * v
                + 8.0 * yv
                - (DT * NU) * (vnn + vss)
                - cross_v
                - (load_n - load)
                + (roll(zv, -1) + roll(zv - cross_v, 1))
                - (roll(av, -2) + roll(av, 2))
                + jnp.where(edge4, unpacked(edge_v, i, 4), 0.0)
            )
            u1 = jnp.where(cu0 > i, u1, 0.0)
            v1 = jnp.where(cv0 > i, v1, 0.0)
            sum_u0 = sum_u0 + u * dz
            sum_v0 = sum_v0 + v * dz
            sum_u = sum_u + u1 * dz
            sum_v = sum_v + v1 * dz
            U1B[k] = u1
            V1X[k, 8:16, :] = v1
        return sum_u0, sum_v0, sum_u, sum_v

    sums = lax.fori_loop(0, NM, momentum, (zero,) * 4)

    for n in range(4):
        F2[n, 1, 8:16, :] = sums[n]
    spread(G_SUM, F2, AROUND)

    @pl.loop(0, NC)
    def _(c):
        held_u = held_v = zero
        for i in range(LC):
            k = c * LC + i
            held_u = jnp.where(slot == i, packed(U1B[k], i), held_u)
            held_v = jnp.where(slot == i, packed(V1X[k, 8:16, :], i), held_v)
        pack1[0, c] = held_u
        pack1[1, c] = held_v

    for dx in (1, -1):
        side = P1W if dx > 0 else P1E
        send(G_B, pack1, side.at[:, :, pl.ds(1, 8), :], dx, 0)
        send(G_B, pack1.at[1, :, pl.ds(7, 1), :], side.at[1, :, pl.ds(0, 1), :], dx, 1)
    send(G_B, V1X.at[:, pl.ds(15, 1), :], V1X.at[:, pl.ds(7, 1), :], 0, 1)

    left(G_2D, size_2d)
    left(G_TS, size_ts)
    received(G_TS, size_ts)

    edge_col = [
        jnp.where(inside, x, 0.0)
        for x in (jnp.where(slot24 < 4, D2[2, 0], D2[2, 2]), D2[2, 1])
    ]
    edge_cu = [jnp.minimum(a, b) for a, b in zip(edge_col, ring_east(*edge_col, slot24 == 4))]
    for n in range(2):
        SC[n] = edge_col[n]
        SU[n] = edge_cu[n]
        SV[n] = jnp.minimum(edge_col[n], north24(edge_col[n]))

    for f in range(2):
        south, here, north = [
            by8.if_wet(SC, 0, r, by8.beyond(TW, TE, f, r)) for r in range(3)
        ]
        inner = by8.if_wet(SC, 1, 1, pack_ts[f, :, 1:9, :])
        HC[f] = here
        HS[f, 0] = half * (here + roll(jnp.where(by8.east, inner, here), -1))
        HS[f, 1] = half * (inner + roll(here, -1))
        HS[f, 2] = half * (here + north)
        HS[f, 3] = half * (south + here)

    @pl.loop(0, NC)
    def _(c):
        base = (c * LC).astype(jnp.float32)
        low, mid, high = [CC[r : r + 8, :] - base for r in (7, 8, 9)]
        for f in range(2):
            edge = HC[f, c]
            for i in range(LC):
                k = c * LC + i
                south = jnp.where(low > i, X[2 + f, k, 7:15, :], 0.0)
                here = jnp.where(mid > i, X[2 + f, k, 8:16, :], 0.0)
                north = jnp.where(high > i, X[2 + f, k, 9:17, :], 0.0)
                X[2 + f, k, 7:15, :] = south
                X[2 + f, k, 9:17, :] = north
                east = jnp.where(last, roll(edge, LANES - 5 - 8 * i), roll(here, -1))
                CE[f, k] = half * (here + east)
                CN[f, k, 7:15, :] = half * (south + here)
                CN[f, k, 8:16, :] = half * (here + north)

    def both(op, *pairs):
        return [op(*xs) for xs in zip(*pairs)]

    def depth_of(c):
        return c * (0.5 / K + c * (0.5 / (K * K)))

    open_u = [(x > 0.0).astype(jnp.float32) for x in cu]
    open_v = [(x > 0.0).astype(jnp.float32) for x in cv]
    depth_u = both(depth_of, cu)
    depth_v = both(depth_of, cv)
    pull_u = both(lambda o, d: o * d * (DB * GRAVITY), open_u, depth_u)
    pull_v = both(lambda o, d: o * d * (DB * GRAVITY), open_v, depth_v)
    pull_w = ring_west(*pull_u)
    ease = both(lambda o: jnp.where(o, DB, 0.0), ocean)
    height = [jnp.where(o, x, 0.0) for o, x in zip(ocean, sides(D2, 1))]

    inverse_u = both(lambda d, o: 1.0 / (d + (1.0 - o)), depth_u, open_u)
    inverse_v = both(lambda d, o: 1.0 / (d + (1.0 - o)), depth_v, open_v)
    received(G_SUM, size_sum)
    u0, v0, u_all, v_all = [list(sides(F2, f)) for f in range(4)]
    push_u = both(lambda o, a, b: o * ((a - b) * (DB / DT)), open_u, u_all, u0)
    push_v = both(lambda o, a, b: o * ((a - b) * (DB / DT)), open_v, v_all, v0)
    trans_u = both(lambda o, a: o * a, open_u, u0)
    trans_v = both(lambda o, a: o * a, open_v, v0)
    run_u = [jnp.zeros((24, LANES), jnp.float32)] * 2
    run_v = run_u

    def substep(_, state):
        level, trans_u, trans_w, trans_v, run_u, run_v = state
        level_w = ring_west(*level)
        trans_w = both(
            lambda t, p, q, h, w: t + (p - q * (h - w)), trans_w, push_w, pull_w, level, level_w
        )
        trans_u = both(
            lambda t, p, q, e, h: t + (p - q * (e - h)),
            trans_u,
            push_u,
            pull_u,
            ring_east(*level),
            level,
        )
        trans_v = both(
            lambda t, p, q, h: t + (p - q * (north24(h) - h)), trans_v, push_v, pull_v, level
        )
        level = both(
            lambda h, e, u, w, v: h - e * ((u - w) + (v - south24(v))),
            level,
            ease,
            trans_u,
            trans_w,
            trans_v,
        )
        return level, trans_u, trans_w, trans_v, both(jnp.add, run_u, trans_u), both(jnp.add, run_v, trans_v)

    trans_w, push_w = ring_west(*trans_u), ring_west(*push_u)
    state = height, trans_u, trans_w, trans_v, run_u, run_v
    for n in range(SUBSTEPS):
        state = substep(n, state)
    height, _, _, _, run_u, run_v = state

    HN[...] = height[0][8:16]

    def shift(r, a, inverse):
        return (r * (1.0 / SUBSTEPS) - a) * inverse

    shift_u = both(shift, run_u, u_all, inverse_u)
    shift_v = both(shift, run_v, v_all, inverse_v)
    DV[0] = shift_v[0]
    DV[1] = shift_v[1]
    du, dv, dvs = shift_u[0][8:16], shift_v[0][8:16], DV[0, 7:15, :]
    DP[0] = in_slots(shift_u[1][8:16], (125, 126, 127, 0, 1))
    DP[1] = in_slots(DV[1, 8:16, :], (126, 127, 0, 1))
    DP[2] = in_slots(DV[1, 7:15, :], (126, 127, 0, 1))
    DP[3] = jnp.broadcast_to(du[:, LANES - 1 :], du.shape)

    received(G_B, size_b)
    edge_u = by8.if_wet(SU, 0, 1, by8.beyond(P1W, P1E, 0, 1) + DP[0][None])
    edge_v = by8.if_wet(SV, 0, 1, by8.beyond(P1W, P1E, 1, 1) + DP[1][None])
    edge_vs = by8.if_wet(SV, 0, 0, by8.beyond(P1W, P1E, 1, 0) + DP[2][None])
    last_u = by8.if_wet(SU, 1, 1, pack1[0] + DP[3][None])
    for f in range(2):
        flux = edge_u * HS[f, 0]
        flux_west = roll(jnp.where(by8.west, last_u * HS[f, 1], flux), 1)
        a = HC[f] - ((flux - flux_west) + (edge_v * HS[f, 2] - edge_vs * HS[f, 3]))
        FW[f] = flux
        AO[f] = by8.if_wet(SC, 0, 1, a)

    def send_rows(c, up):
        src, dst, dy, group = (14, 6, 1, G_UP) if up else (8, 16, -1, G_DOWN)
        levels = pl.ds(c * LC, LC)
        send(
            group,
            AX.at[:, levels, pl.ds(src, 2), :],
            AX.at[:, levels, pl.ds(dst, 2), :],
            0,
            dy,
        )

    @pl.loop(0, NC)
    def _(c):
        base = (c * LC).astype(jnp.float32)
        edges = [FW[f, c] for f in range(2)]
        cc0, cu0, cv0 = CC[8:16, :] - base, CU[8:16, :] - base, CV[8:16, :] - base
        cvs = CV[7:15, :] - base
        held = [zero, zero]
        for i in range(LC):
            k = c * LC + i
            u = jnp.where(cu0 > i, U1B[k] + du, 0.0)
            v = jnp.where(cv0 > i, V1X[k, 8:16, :] + dv, 0.0)
            vs = jnp.where(cvs > i, V1X[k, 7:15, :] + dvs, 0.0)
            UN[k] = u
            VN[k] = v
            for f in range(2):
                flux = u * CE[f, k]
                flux_west = jnp.where(first, roll(edges[f], LANES - 3 - 8 * i), roll(flux, 1))
                a = X[2 + f, k, 8:16, :] - (
                    (flux - flux_west) + (v * CN[f, k, 8:16, :] - vs * CN[f, k, 7:15, :])
                )
                a = jnp.where(cc0 > i, a, 0.0)
                AX[f, k, 8:16, :] = a
                held[f] = jnp.where(slot == i, packed(a, i), held[f])
        for f in range(2):
            AD[f, c, 1:9, :] = AO[f, c] - held[f]

        @pl.when(has_north)
        def _():
            send_rows(c, True)

        @pl.when(has_south)
        def _():
            send_rows(c, False)

    @pl.when(has_north)
    def _():
        send(G_UP, AD.at[:, :, pl.ds(8, 1), :], AD.at[:, :, pl.ds(0, 1), :], 0, 1)

    @pl.when(has_south)
    def _():
        send(G_DOWN, AD.at[:, :, pl.ds(1, 1), :], AD.at[:, :, pl.ds(9, 1), :], 0, -1)

    left(G_SUM, size_sum)
    left(G_B, size_b)

    @pl.loop(0, NC)
    def _(c):
        for i in range(LC):
            k = c * LC + i
            for f, out in ((0, TN), (1, SN)):
                a = AX[f, k, 8:16, :]
                b = KAPPA * a
                out[k] = (
                    centre_ts * a
                    + 8.0 * (roll(b, -1) + roll(b, 1))
                    - (roll(b, -2) + roll(b, 2))
                )

    @pl.when(has_south)
    def _():
        received(G_UP, size_c)

    @pl.when(has_north)
    def _():
        received(G_DOWN, size_c)

    for f in range(2):
        south, here, north = [AD[f, :, r : r + 8, :] for r in range(3)]
        EM[f] = KAPPA * by8.far(here, south + north)

    @pl.when(has_north)
    def _():
        left(G_UP, size_c)

    @pl.when(has_south)
    def _():
        left(G_DOWN, size_c)


def finish(TN, SN, UN, VN, HN, AX, EM, CC, t_out, s_out, u_out, v_out, h_out, TO, SO, sem):
    copies = [
        pltpu.make_async_copy(src, dst, sem.at[n])
        for n, (src, dst) in enumerate(((UN, u_out), (VN, v_out), (HN, h_out)))
    ]
    for copy in copies:
        copy.start()
    lane = lax.broadcasted_iota(jnp.int32, (ROWS, LANES), 1)
    edge4 = jnp.logical_or(lane < 2, lane >= LANES - 2)

    def roll(x, shift):
        return pltpu.roll(x, shift % LANES, 1)

    @pl.loop(0, NC)
    def _(c):
        cc0 = CC[8:16, :] - (c * LC).astype(jnp.float32)
        edges = [EM[f, c] for f in range(2)]
        for i in range(LC):
            k = c * LC + i
            for f, part, out in ((0, TN, TO), (1, SN, SO)):
                ss, s, n, nn = [AX[f, k, r : r + 8, :] for r in (6, 7, 9, 10)]
                y = KAPPA * (n + s)
                mixed = (
                    part[k]
                    + 8.0 * y
                    - 2.0 * (roll(y, -1) + roll(y, 1))
                    - KAPPA * (nn + ss)
                    - jnp.where(edge4, roll(edges[f], LANES - 4 - 8 * i), 0.0)
                )
                out[k] = jnp.where(cc0 > i, mixed, 0.0)
        levels = pl.ds(c * LC, LC)
        pltpu.make_async_copy(TO.at[levels], t_out.at[levels], sem.at[3]).start()
        pltpu.make_async_copy(SO.at[levels], s_out.at[levels], sem.at[4]).start()

    for copy in copies:
        copy.wait()
    pltpu.make_async_copy(TO, t_out, sem.at[3]).wait()
    pltpu.make_async_copy(SO, s_out, sem.at[4]).wait()


def per_device(nx, ny, *args):
    tile3 = jax.ShapeDtypeStruct((K, ROWS, LANES), jnp.float32)
    tile2 = jax.ShapeDtypeStruct((ROWS, LANES), jnp.float32)
    outs = (tile3, tile3, tile3, tile3, tile2)

    def vmem(*shape, dtype=jnp.float32):
        return pltpu.VMEM(shape, dtype)

    args = [pltpu.with_memory_space_constraint(x, pltpu.HBM) for x in args]
    held = pl.pallas_call(
        functools.partial(kernel, nx, ny),
        out_shape=tuple(
            pltpu.VMEM(shape, jnp.float32)
            for shape in [x.shape for x in outs]
            + [(2, K, 24, LANES), (2, NC, ROWS, LANES), (24, LANES)]
        ),
        in_specs=[pl.BlockSpec(memory_space=pltpu.HBM)] * 7,
        out_specs=[pl.BlockSpec(memory_space=pltpu.VMEM)] * 8,
        scratch_shapes=[
            vmem(4, K, 24, LANES),
            vmem(K, 16, LANES),
            vmem(3, 3, 24, LANES),
            vmem(ROWS, LANES, dtype=jnp.int32),
            vmem(ROWS, LANES, dtype=jnp.int32),
            vmem(24, LANES),
            vmem(24, LANES),
            vmem(2, 24, LANES),
            vmem(2, 24, LANES),
            vmem(2, 24, LANES),
            vmem(2, 24, LANES),
            vmem(2, 24, LANES),
            vmem(3, NM, 16, LANES),
            vmem(3, NM, 16, LANES),
            vmem(3, NM, 16, LANES),
            vmem(2, NC, 16, LANES),
            vmem(2, NC, 16, LANES),
            vmem(2, NC, 16, LANES),
            vmem(4, 3, 24, LANES),
            vmem(2, 24, LANES),
            vmem(4, ROWS, LANES),
            vmem(K, ROWS, LANES),
            vmem(K, 16, LANES),
            vmem(2, NC, ROWS, LANES),
            vmem(2, NC, 16, LANES),
            vmem(2, NC, 16, LANES),
            vmem(2, NC, 16, LANES),
            vmem(NM, ROWS, LANES),
            vmem(NM, ROWS, LANES),
            vmem(2, NC, ROWS, LANES),
            vmem(2, K, ROWS, LANES),
            vmem(2, K, 16, LANES),
            vmem(2, NC, ROWS, LANES),
            vmem(2, NC, ROWS, LANES),
            vmem(2, 4, NC, ROWS, LANES),
            pltpu.SemaphoreType.DMA((2,)),
            pltpu.SemaphoreType.DMA((GROUPS,)),
            pltpu.SemaphoreType.DMA((GROUPS,)),
        ],
        compiler_params=pltpu.CompilerParams(
            collective_id=0, has_side_effects=True, vmem_limit_bytes=24 * 1024 * 1024
        ),
    )(*args)
    return pl.pallas_call(
        finish,
        out_shape=outs,
        in_specs=[pl.BlockSpec(memory_space=pltpu.VMEM)] * 8,
        out_specs=[pl.BlockSpec(memory_space=pltpu.HBM)] * 5,
        scratch_shapes=[
            vmem(K, ROWS, LANES),
            vmem(K, ROWS, LANES),
            pltpu.SemaphoreType.DMA((5,)),
        ],
        compiler_params=pltpu.CompilerParams(vmem_limit_bytes=8 * 1024 * 1024),
    )(*held)


def solution(mesh):
    placed = (P(None, "gy", "gx"),) * 4 + (P("gy", "gx"),) * 3
    return jax.shard_map(
        functools.partial(per_device, mesh.shape["gx"], mesh.shape["gy"]),
        mesh=mesh,
        in_specs=placed,
        out_specs=(P(None, "gy", "gx"),) * 4 + (P("gy", "gx"),),
        check_vma=False,
    )
```

```python
import functools

import jax
import jax.numpy as jnp
from jax import lax
from jax.experimental import pallas as pl
from jax.experimental.pallas import tpu as pltpu
from jax.sharding import PartitionSpec as P

MESH = pl.DeviceIdType.MESH
K = 75
NC = 5
LC = K // NC
NM = 5
LM = K // NM
SUBSTEPS = 8
ROWS = 8
LANES = 128

DT = 0.4
NU = 0.025
KAPPA = 0.01
DTT = 0.2
GRAVITY = 4.0
DB = DT / SUBSTEPS

GROUPS = 7
G_2D, G_A, G_TS, G_SUM, G_B, G_UP, G_DOWN = range(GROUPS)


def kernel(
    nx,
    ny,
    t_in,
    s_in,
    u_in,
    v_in,
    h_in,
    flag_in,
    bottom_in,
    TN,
    SN,
    UN,
    VN,
    HN,
    AX,
    EM,
    CC,
    X,
    PX,
    D2,
    ET,
    flag_v,
    bottom_v,
    CU,
    CV,
    SC,
    SU,
    SV,
    S4,
    pack,
    PE,
    PW,
    packp,
    PP,
    pack_ts,
    TE,
    TW,
    F2,
    FT,
    FE,
    DV,
    DP,
    U1B,
    V1X,
    pack1,
    P1E,
    P1W,
    AD,
    EUV,
    HC,
    CE,
    CN,
    FW,
    AO,
    HS,
    load_sem,
    send_sem,
    recv_sem,
):
    gx, gy = lax.axis_index("gx"), lax.axis_index("gy")

    def device(dx, dy):
        return (lax.rem(gx + dx + nx, nx), lax.rem(gy + dy + ny, ny))

    def send(group, src, dst, dx, dy):
        pltpu.make_async_remote_copy(
            src_ref=src,
            dst_ref=dst,
            send_sem=send_sem.at[group],
            recv_sem=recv_sem.at[group],
            device_id=device(dx, dy),
            device_id_type=MESH,
        ).start()

    def received(group, size):
        pltpu.make_async_copy(size, size, recv_sem.at[group]).wait()

    def left(group, size):
        pltpu.make_async_copy(size, size, send_sem.at[group]).wait()

    has_south, has_north = gy > 0, gy < ny - 1

    def beside(dy):
        return pl.when(has_north if dy > 0 else has_south)

    barrier = pltpu.get_barrier_semaphore()

    def greet(dx, dy):
        pl.semaphore_signal(barrier, inc=1, device_id=device(dx, dy), device_id_type=MESH)

    for dy in (-1, 1):

        @beside(dy)
        def _():
            for dx in (-1, 1, 0):
                greet(dx, dy)

    for dx in (-1, 1):
        greet(dx, 0)

    pltpu.make_async_copy(flag_in, flag_v, load_sem.at[0]).start()
    pltpu.make_async_copy(bottom_in, bottom_v, load_sem.at[0]).start()
    pltpu.make_async_copy(h_in, D2.at[1, 1, pl.ds(8, 8), :], load_sem.at[0]).start()
    for f, source in enumerate((u_in, v_in, t_in, s_in)):
        pltpu.make_async_copy(source, X.at[f, :, pl.ds(8, 8), :], load_sem.at[1]).start()

    def loaded(sem, size):
        pltpu.make_async_copy(size, size, load_sem.at[sem]).wait()

    lane = lax.broadcasted_iota(jnp.int32, (ROWS, LANES), 1)
    slot = lax.div(lane, 8).astype(jnp.float32)
    row = lax.broadcasted_iota(jnp.int32, (ROWS, LANES), 0)
    first, last = lane == 0, lane == LANES - 1
    half = 0.5 * DTT
    edge4 = jnp.logical_or(lane < 2, lane >= LANES - 2)
    slot4 = lax.div(lane, 4).astype(jnp.float32)
    zero = jnp.zeros((ROWS, LANES), jnp.float32)

    def roll(x, shift):
        return pltpu.roll(x, shift % LANES, x.ndim - 1)

    def packed(x, i, width=8):
        return roll(x, width * i + width // 2)

    def unpacked(x, i, width=8):
        return roll(x, LANES - width // 2 - width * i)

    def in_slots(x, lanes, width=8):
        at = lax.rem(lax.broadcasted_iota(jnp.int32, x.shape, 1), width)
        out = None
        for l in lanes:
            column = jnp.broadcast_to(x[:, l : l + 1], x.shape)
            out = column if out is None else jnp.where(at == (l + width // 2) % LANES, column, out)
        return out

    @pl.when(jnp.logical_not(has_south))
    def _():
        AD[:, :, 0:1, :] = jnp.zeros((2, NC, 1, LANES), jnp.float32)

        @pl.loop(0, K)
        def _(k):
            for f in range(2):
                AX[f, k, 6:8, :] = jnp.zeros((2, LANES), jnp.float32)

    @pl.when(jnp.logical_not(has_north))
    def _():
        AD[:, :, 9:10, :] = jnp.zeros((2, NC, 1, LANES), jnp.float32)

        @pl.loop(0, K)
        def _(k):
            for f in range(2):
                AX[f, k, 16:18, :] = jnp.zeros((2, LANES), jnp.float32)

    loaded(0, AX.at[0, pl.ds(0, 3), pl.ds(8, 8), :])
    own = (flag_v[...] * bottom_v[...]).astype(jnp.float32)
    D2[0, 1, 8:16, :] = own
    ET[...] = jnp.where(jnp.logical_and(lane >= 32, lane < 96), roll(D2[1, 1, 8:16, :], 64), own)

    def rows(group, fields, count, dy):
        src, dst = (16 - count, 8 - count) if dy > 0 else (8, 16)
        send(
            group,
            X.at[fields, :, pl.ds(src, count), :],
            X.at[fields, :, pl.ds(dst, count), :],
            0,
            dy,
        )

    loaded(1, X.at[:, :, pl.ds(8, 8), :])
    def weight(t, s, dz):
        return (0.8 * s - t * (0.2 + 0.05 * t)) * dz

    def thickness(base, i):
        return 0.5 / K + (base + (i + 0.5)) * (1.0 / (K * K))

    def press(c, cum):
        base = (c * LM).astype(jnp.float32)
        depth = D2[0, 1, 8:16, :] - base
        held = held_p = zero
        for i in range(LM):
            k = c * LM + i
            u, v, t, s = [X[f, k, 8:16, :] for f in range(4)]
            w = jnp.where(depth > i, weight(t, s, DT * thickness(base, i)), 0.0)
            cum = cum + w
            load = cum - 0.5 * w
            PX[k, 0:8, :] = load
            held = jnp.where(slot4 == i, packed(u, i, 4), held)
            held = jnp.where(slot4 == i + 16, packed(v, i + 16, 4), held)
            held_p = jnp.where(slot4 == i, packed(load, i, 4), held_p)
        pack[0, c, 1:9, :] = held
        packp[c] = held_p
        return cum

    lax.fori_loop(0, NM, press, zero)

    pl.semaphore_wait(
        barrier, 2 + 3 * (has_south.astype(jnp.int32) + has_north.astype(jnp.int32))
    )

    def corners(group, src, west, east, dy):
        for dx in (1, -1):
            side = west if dx > 0 else east
            r_src, r_dst = (8, 0) if dy > 0 else (1, 9)
            send(
                group,
                src.at[:, :, pl.ds(r_src, 1), :],
                side.at[:, :, pl.ds(r_dst, 1), :],
                dx,
                dy,
            )

    def edge_tiles(group, edge, aside, dy):
        for dx in (-1, 1):
            send(group, edge, aside(1 - dx).at[pl.ds(8 * (1 - dy), 8), :], dx, dy)

    def whole_tiles(group, whole, dy):
        send(group, whole.at[:, pl.ds(8, 8), :], whole.at[:, pl.ds(8 * (1 - dy), 8), :], 0, dy)

    def edges_2d(dy):
        edge_tiles(G_2D, ET, lambda n: D2.at[0, n], dy)

    for dy in (-1, 1):

        @beside(dy)
        def _():
            edges_2d(dy)
            corners(G_A, pack, PW, PE, dy)

    edges_2d(0)
    for dx in (1, -1):
        side = PW if dx > 0 else PE
        send(G_A, pack.at[:, :, pl.ds(1, 8), :], side.at[:, :, pl.ds(1, 8), :], dx, 0)
    send(G_A, packp, PP, -1, 0)
    for dy in (-1, 1):

        @beside(dy)
        def _():
            whole_tiles(G_2D, D2.at[:, 1], dy)
            rows(G_A, pl.ds(0, 2), 2, dy)
            src, dst = (8, 0) if dy > 0 else (1, 9)
            send(G_A, pack.at[:, :, pl.ds(src, 1), :], pack.at[:, :, pl.ds(dst, 1), :], 0, dy)
            if dy < 0:
                send(G_A, PX.at[:, pl.ds(0, 1), :], PX.at[:, pl.ds(8, 1), :], 0, dy)

    @pl.loop(0, NC)
    def _(c):
        held = [zero] * 2
        for i in range(LC):
            for f in range(2):
                held[f] = jnp.where(slot == i, packed(X[2 + f, c * LC + i, 8:16, :], i), held[f])
        for f in range(2):
            pack_ts[f, c, 1:9, :] = held[f]

    for dx in (1, -1):
        side = TW if dx > 0 else TE
        send(G_TS, pack_ts.at[:, :, pl.ds(1, 8), :], side.at[:, :, pl.ds(1, 8), :], dx, 0)
    for dy in (-1, 1):

        @beside(dy)
        def _():
            corners(G_TS, pack_ts, TW, TE, dy)
            rows(G_TS, pl.ds(2, 2), 1, dy)

    def size(levels, count):
        return X.at[0, pl.ds(0, levels), pl.ds(0, count), :]

    def by_walls(wait, group, inner, southmost, northmost):
        @pl.when(jnp.logical_and(has_south, has_north))
        def _():
            wait(group, size(*inner))

        @pl.when(jnp.logical_not(has_south))
        def _():
            wait(group, size(*southmost))

        @pl.when(jnp.logical_not(has_north))
        def _():
            wait(group, size(*northmost))

    size_c = size(62, 5)

    by_walls(received, G_2D, (10, 8), (6, 8), (6, 8))
    row24 = lax.broadcasted_iota(jnp.int32, (24, LANES), 0)
    lane24 = lax.broadcasted_iota(jnp.int32, (24, LANES), 1)
    slot24 = lax.rem(lane24, 8)
    first24, last24 = lane24 == 0, lane24 == LANES - 1
    inside = jnp.logical_and(
        jnp.logical_or(row24 >= 8, has_south), jnp.logical_or(row24 < 16, has_north)
    )

    def ring_east(c, h, seam=first24):
        return (
            roll(jnp.where(seam, h, c), LANES - 1),
            roll(jnp.where(seam, c, h), LANES - 1),
        )

    def ring_west(c, h):
        return (
            roll(jnp.where(last24, h, c), 1),
            roll(jnp.where(last24, c, h), 1),
        )

    def north24(x):
        return pltpu.roll(x, 23, 0)

    def south24(x):
        return pltpu.roll(x, 1, 0)

    edges = jnp.where(lax.rem(lane24, 64) < 32, D2[0, 2], D2[0, 0])
    col = [jnp.where(inside, x, 0.0) for x in (D2[0, 1], edges)]
    ocean = [x > 0.0 for x in col]
    cu = [jnp.minimum(a, b) for a, b in zip(col, ring_east(*col))]
    cv = [jnp.minimum(a, north24(a)) for a in col]
    CC[...] = col[0]
    CU[...] = cu[0]
    CV[...] = cv[0]
    for n in range(2):
        S4[n] = jnp.where(
            lane24 < 64,
            in_slots(cu[1 - n], (126, 127, 0, 1), 4),
            in_slots(cv[1 - n], (126, 127, 0, 1), 4),
        )

    at_wall = jnp.where(
        jnp.logical_or(
            jnp.logical_and(row == 0, jnp.logical_not(has_south)),
            jnp.logical_and(row == ROWS - 1, jnp.logical_not(has_north)),
        ),
        19.0,
        20.0,
    )
    latitude = (row + gy * ROWS).astype(jnp.float32)
    f4 = (0.25 * DT) * (0.2 + 0.3 * (latitude + 0.5) / (ROWS * ny))
    centre_uv = 1.0 - (DT * NU) * at_wall
    centre_ts = 1.0 - KAPPA * at_wall

    by_walls(received, G_A, (K, 11), (51, 10), (29, 15))
    by_walls(left, G_A, (K, 11), (29, 15), (51, 10))

    @pl.loop(0, NC)
    def _(c):
        base = (c * LC).astype(jnp.float32)
        for f, depths in ((0, CU), (1, CV)):
            low, high = depths[6:14, :] - base, depths[10:18, :] - base
            for i in range(LC):
                k = c * LC + i
                a = jnp.where(low > i, X[f, k, 6:14, :], 0.0)
                b = jnp.where(high > i, X[f, k, 10:18, :], 0.0)
                X[f, k, 6:14, :] = a
                X[f, k, 10:18, :] = b

    class Slots:
        def __init__(self, count, width, span):
            shape = (count, ROWS, LANES)
            self.lanes = lax.broadcasted_iota(jnp.int32, shape, 2)
            self.place = lax.rem(self.lanes, width)
            tile = lax.broadcasted_iota(jnp.int32, shape, 0)
            self.level = (lax.div(lax.rem(self.lanes, span), width) + tile * (K // count)).astype(
                jnp.float32
            )
            self.west, self.east = self.place == width // 2 - 1, self.place == width // 2
            self.western = self.place < width // 2

        def beyond(self, west, east, f, r):
            return jnp.where(self.western, west[f, :, r : r + 8, :], east[f, :, r : r + 8, :])

        def if_wet(self, depths, n, r, x):
            return jnp.where(self.level < depths[n, r + 7 : r + 15, :][None], x, 0.0)

        def far(self, d, y):
            z = 2.0 * y - 8.0 * d
            return jnp.where(self.western, roll(d, -2), roll(d, 2)) + jnp.where(
                self.west, roll(z, -1), jnp.where(self.east, roll(z, 1), 0.0)
            )

    by4, by8 = Slots(NM, 4, 64), Slots(NC, 8, LANES)

    def excess(r):
        return by4.if_wet(S4, 0, r, by4.beyond(PW, PE, 0, r)) - by4.if_wet(
            S4, 1, r, pack[0, :, r : r + 8, :]
        )

    d_s, d, d_n = [excess(r) for r in range(3)]
    dp = PP[...] - packp[...]
    u_half = by4.lanes < 64
    EUV[...] = (
        jnp.where(
            jnp.logical_and(by4.west, u_half),
            f4[None] * roll(d + d_s, -65) - roll(dp, -1),
            jnp.where(
                jnp.logical_and(by4.east, jnp.logical_not(u_half)),
                -f4[None] * roll(d + d_n, 65),
                0.0,
            ),
        )
        - (DT * NU) * by4.far(d, d_n + d_s)
    )

    def momentum(c, carry):
        sum_u0, sum_v0, sum_u, sum_v = carry
        base = (c * LM).astype(jnp.float32)
        edge = EUV[c]
        cu0, cv0 = CU[8:16, :] - base, CV[8:16, :] - base
        for i in range(LM):
            k = c * LM + i
            dz = thickness(base, i)
            uss, us, u, un, unn = [X[0, k, r : r + 8, :] for r in range(6, 11)]
            vss, vs, v, vn, vnn = [X[1, k, r : r + 8, :] for r in range(6, 11)]
            load, load_n = PX[k, 0:8, :], PX[k, 1:9, :]
            cross_u = f4 * (v + vs)
            cross_v = f4 * (u + un)
            yu, yv = (DT * NU) * (un + us), (DT * NU) * (vn + vs)
            au, av = (DT * NU) * u, (DT * NU) * v
            zu, zv = 8.0 * au - 2.0 * yu, 8.0 * av - 2.0 * yv
            u1 = (
                centre_uv * u
                + 8.0 * yu
                - (DT * NU) * (unn + uss)
                + (cross_u + load)
                + (roll(zu + (cross_u - load), -1) + roll(zu, 1))
                - (roll(au, -2) + roll(au, 2))
                + jnp.where(edge4, unpacked(edge, i, 4), 0.0)
            )
            v1 = (
                centre_uv * v
                + 8.0 * yv
                - (DT * NU) * (vnn + vss)
                - cross_v
                - (load_n - load)
                + (roll(zv, -1) + roll(zv - cross_v, 1))
                - (roll(av, -2) + roll(av, 2))
                + jnp.where(edge4, unpacked(edge, i + 16, 4), 0.0)
            )
            u1 = jnp.where(cu0 > i, u1, 0.0)
            v1 = jnp.where(cv0 > i, v1, 0.0)
            sum_u0 = sum_u0 + u * dz
            sum_v0 = sum_v0 + v * dz
            sum_u = sum_u + u1 * dz
            sum_v = sum_v + v1 * dz
            U1B[k] = u1
            V1X[k, 8:16, :] = v1
        return sum_u0, sum_v0, sum_u, sum_v

    sums = lax.fori_loop(0, NM, momentum, (zero,) * 4)

    edge = sums[0]
    for n in range(4):
        F2[n, 8:16, :] = sums[n]
        near = jnp.logical_and(lane >= 32 * n - 16, lane < 32 * n + 16)
        edge = jnp.where(near, roll(sums[n], 32 * n), edge)
    FT[...] = edge
    for dy in (-1, 1):

        @beside(dy)
        def _():
            edge_tiles(G_SUM, FT, lambda n: FE.at[n], dy)

    edge_tiles(G_SUM, FT, lambda n: FE.at[n], 0)
    for dy in (-1, 1):

        @beside(dy)
        def _():
            whole_tiles(G_SUM, F2, dy)


    @pl.loop(0, NC)
    def _(c):
        held_u = held_v = zero
        for i in range(LC):
            k = c * LC + i
            held_u = jnp.where(slot == i, packed(U1B[k], i), held_u)
            held_v = jnp.where(slot == i, packed(V1X[k, 8:16, :], i), held_v)
        pack1[0, c] = held_u
        pack1[1, c] = held_v

    for dx in (1, -1):
        side = P1W if dx > 0 else P1E
        send(G_B, pack1, side.at[:, :, pl.ds(1, 8), :], dx, 0)

    @beside(1)
    def _():
        for dx in (1, -1):
            side = P1W if dx > 0 else P1E
            send(G_B, pack1.at[1, :, pl.ds(7, 1), :], side.at[1, :, pl.ds(0, 1), :], dx, 1)
        send(G_B, V1X.at[:, pl.ds(15, 1), :], V1X.at[:, pl.ds(7, 1), :], 0, 1)

    by_walls(left, G_2D, (10, 8), (6, 8), (6, 8))
    by_walls(left, G_TS, (50, 10), (33, 10), (33, 10))
    by_walls(received, G_TS, (50, 10), (33, 10), (33, 10))

    edge_col = [in_slots(x, (124, 125, 126, 127, 0, 1, 2, 3)) for x in (col[1], col[0])]
    edge_cu = [jnp.minimum(a, b) for a, b in zip(edge_col, ring_east(*edge_col, slot24 == 4))]
    for n in range(2):
        SC[n] = edge_col[n]
        SU[n] = edge_cu[n]
        SV[n] = jnp.minimum(edge_col[n], north24(edge_col[n]))

    for f in range(2):
        south, here, north = [
            by8.if_wet(SC, 0, r, by8.beyond(TW, TE, f, r)) for r in range(3)
        ]
        inner = by8.if_wet(SC, 1, 1, pack_ts[f, :, 1:9, :])
        HC[f] = here
        HS[f, 0] = half * (here + roll(jnp.where(by8.east, inner, here), -1))
        HS[f, 1] = half * (inner + roll(here, -1))
        HS[f, 2] = half * (here + north)
        HS[f, 3] = half * (south + here)

    @pl.loop(0, NC)
    def _(c):
        base = (c * LC).astype(jnp.float32)
        low, mid, high = [CC[r : r + 8, :] - base for r in (7, 8, 9)]
        for f in range(2):
            edge = HC[f, c]
            for i in range(LC):
                k = c * LC + i
                south = jnp.where(low > i, X[2 + f, k, 7:15, :], 0.0)
                here = jnp.where(mid > i, X[2 + f, k, 8:16, :], 0.0)
                north = jnp.where(high > i, X[2 + f, k, 9:17, :], 0.0)
                X[2 + f, k, 7:15, :] = south
                X[2 + f, k, 9:17, :] = north
                east = jnp.where(last, roll(edge, LANES - 5 - 8 * i), roll(here, -1))
                CE[f, k] = half * (here + east)
                CN[f, k, 7:15, :] = half * (south + here)
                CN[f, k, 8:16, :] = half * (here + north)

    def both(op, *pairs):
        return [op(*xs) for xs in zip(*pairs)]

    def depth_of(c):
        return c * (0.5 / K + c * (0.5 / (K * K)))

    open_u = [(x > 0.0).astype(jnp.float32) for x in cu]
    open_v = [(x > 0.0).astype(jnp.float32) for x in cv]
    depth_u = both(depth_of, cu)
    depth_v = both(depth_of, cv)
    pull_u = both(lambda o, d: o * d * (DB * GRAVITY), open_u, depth_u)
    pull_v = both(lambda o, d: o * d * (DB * GRAVITY), open_v, depth_v)
    pull_w = ring_west(*pull_u)
    ease = both(lambda o: jnp.where(o, DB, 0.0), ocean)
    height = [jnp.where(o, x, 0.0) for o, x in zip(ocean, (D2[1, 1], roll(edges, 64)))]

    inverse_u = both(lambda d, o: 1.0 / (d + (1.0 - o)), depth_u, open_u)
    inverse_v = both(lambda d, o: 1.0 / (d + (1.0 - o)), depth_v, open_v)
    by_walls(received, G_SUM, (14, 8), (8, 8), (8, 8))
    edges = jnp.where(lax.rem(lane24, 32) < 16, FE[2], FE[0])
    u0, v0, u_all, v_all = [[F2[n], roll(edges, -32 * n)] for n in range(4)]
    push_u = both(lambda o, a, b: jnp.where(o > 0.0, (a - b) * (DB / DT), 0.0), open_u, u_all, u0)
    push_v = both(lambda o, a, b: jnp.where(o > 0.0, (a - b) * (DB / DT), 0.0), open_v, v_all, v0)
    trans_u = both(lambda o, a: jnp.where(o > 0.0, a, 0.0), open_u, u0)
    trans_v = both(lambda o, a: jnp.where(o > 0.0, a, 0.0), open_v, v0)
    run_u = [jnp.zeros((24, LANES), jnp.float32)] * 2
    run_v = run_u

    def substep(_, state):
        level, trans_u, trans_w, trans_v, run_u, run_v = state
        level_w = ring_west(*level)
        trans_w = both(
            lambda t, p, q, h, w: t + (p - q * (h - w)), trans_w, push_w, pull_w, level, level_w
        )
        trans_u = both(
            lambda t, p, q, e, h: t + (p - q * (e - h)),
            trans_u,
            push_u,
            pull_u,
            ring_east(*level),
            level,
        )
        trans_v = both(
            lambda t, p, q, h: t + (p - q * (north24(h) - h)), trans_v, push_v, pull_v, level
        )
        level = both(
            lambda h, e, u, w, v: h - e * ((u - w) + (v - south24(v))),
            level,
            ease,
            trans_u,
            trans_w,
            trans_v,
        )
        return level, trans_u, trans_w, trans_v, both(jnp.add, run_u, trans_u), both(jnp.add, run_v, trans_v)

    trans_w, push_w = ring_west(*trans_u), ring_west(*push_u)
    state = height, trans_u, trans_w, trans_v, run_u, run_v
    for n in range(SUBSTEPS):
        state = substep(n, state)
    height, _, _, _, run_u, run_v = state

    HN[...] = height[0][8:16]

    def shift(r, a, inverse):
        return (r * (1.0 / SUBSTEPS) - a) * inverse

    shift_u = both(shift, run_u, u_all, inverse_u)
    shift_v = both(shift, run_v, v_all, inverse_v)
    DV[0] = shift_v[0]
    DV[1] = shift_v[1]
    du, dv, dvs = shift_u[0][8:16], shift_v[0][8:16], DV[0, 7:15, :]
    DP[0] = in_slots(shift_u[1][8:16], (125, 126, 127, 0, 1))
    DP[1] = in_slots(DV[1, 8:16, :], (126, 127, 0, 1))
    DP[2] = in_slots(DV[1, 7:15, :], (126, 127, 0, 1))
    DP[3] = jnp.broadcast_to(du[:, LANES - 1 :], du.shape)

    by_walls(received, G_B, (49, 5), (20, 8), (49, 5))
    edge_u = by8.if_wet(SU, 0, 1, by8.beyond(P1W, P1E, 0, 1) + DP[0][None])
    edge_v = by8.if_wet(SV, 0, 1, by8.beyond(P1W, P1E, 1, 1) + DP[1][None])
    edge_vs = by8.if_wet(SV, 0, 0, by8.beyond(P1W, P1E, 1, 0) + DP[2][None])
    last_u = by8.if_wet(SU, 1, 1, pack1[0] + DP[3][None])
    for f in range(2):
        flux = edge_u * HS[f, 0]
        flux_west = roll(jnp.where(by8.west, last_u * HS[f, 1], flux), 1)
        a = HC[f] - ((flux - flux_west) + (edge_v * HS[f, 2] - edge_vs * HS[f, 3]))
        FW[f] = flux
        AO[f] = by8.if_wet(SC, 0, 1, a)

    def send_rows(c, up):
        src, dst, dy, group = (14, 6, 1, G_UP) if up else (8, 16, -1, G_DOWN)
        levels = pl.ds(c * LC, LC)
        send(
            group,
            AX.at[:, levels, pl.ds(src, 2), :],
            AX.at[:, levels, pl.ds(dst, 2), :],
            0,
            dy,
        )

    @pl.loop(0, NC)
    def _(c):
        base = (c * LC).astype(jnp.float32)
        edges = [FW[f, c] for f in range(2)]
        cc0, cu0, cv0 = CC[8:16, :] - base, CU[8:16, :] - base, CV[8:16, :] - base
        cvs = CV[7:15, :] - base
        held = [zero, zero]
        for i in range(LC):
            k = c * LC + i
            u = jnp.where(cu0 > i, U1B[k] + du, 0.0)
            v = jnp.where(cv0 > i, V1X[k, 8:16, :] + dv, 0.0)
            vs = jnp.where(cvs > i, V1X[k, 7:15, :] + dvs, 0.0)
            UN[k] = u
            VN[k] = v
            for f in range(2):
                flux = u * CE[f, k]
                flux_west = jnp.where(first, roll(edges[f], LANES - 3 - 8 * i), roll(flux, 1))
                a = X[2 + f, k, 8:16, :] - (
                    (flux - flux_west) + (v * CN[f, k, 8:16, :] - vs * CN[f, k, 7:15, :])
                )
                a = jnp.where(cc0 > i, a, 0.0)
                AX[f, k, 8:16, :] = a
                held[f] = jnp.where(slot == i, packed(a, i), held[f])
        for f in range(2):
            AD[f, c, 1:9, :] = AO[f, c] - held[f]

        @pl.when(has_north)
        def _():
            send_rows(c, True)

        @pl.when(has_south)
        def _():
            send_rows(c, False)

    @pl.when(has_north)
    def _():
        send(G_UP, AD.at[:, :, pl.ds(8, 1), :], AD.at[:, :, pl.ds(0, 1), :], 0, 1)

    @pl.when(has_south)
    def _():
        send(G_DOWN, AD.at[:, :, pl.ds(1, 1), :], AD.at[:, :, pl.ds(9, 1), :], 0, -1)

    by_walls(left, G_SUM, (14, 8), (8, 8), (8, 8))
    by_walls(left, G_B, (49, 5), (49, 5), (20, 8))

    @pl.loop(0, NC)
    def _(c):
        for i in range(LC):
            k = c * LC + i
            for f, out in ((0, TN), (1, SN)):
                a = AX[f, k, 8:16, :]
                b = KAPPA * a
                out[k] = (
                    centre_ts * a
                    + 8.0 * (roll(b, -1) + roll(b, 1))
                    - (roll(b, -2) + roll(b, 2))
                )

    @pl.when(has_south)
    def _():
        received(G_UP, size_c)

    @pl.when(has_north)
    def _():
        received(G_DOWN, size_c)

    for f in range(2):
        south, here, north = [AD[f, :, r : r + 8, :] for r in range(3)]
        EM[f] = KAPPA * by8.far(here, south + north)

    @pl.when(has_north)
    def _():
        left(G_UP, size_c)

    @pl.when(has_south)
    def _():
        left(G_DOWN, size_c)


def finish(TN, SN, UN, VN, HN, AX, EM, CC, t_out, s_out, u_out, v_out, h_out, TO, SO, sem):
    copies = [
        pltpu.make_async_copy(src, dst, sem.at[n])
        for n, (src, dst) in enumerate(((UN, u_out), (VN, v_out), (HN, h_out)))
    ]
    for copy in copies:
        copy.start()
    lane = lax.broadcasted_iota(jnp.int32, (ROWS, LANES), 1)
    edge4 = jnp.logical_or(lane < 2, lane >= LANES - 2)

    def roll(x, shift):
        return pltpu.roll(x, shift % LANES, 1)

    @pl.loop(0, NC)
    def _(c):
        cc0 = CC[8:16, :] - (c * LC).astype(jnp.float32)
        edges = [EM[f, c] for f in range(2)]
        for i in range(LC):
            k = c * LC + i
            for f, part, out in ((0, TN, TO), (1, SN, SO)):
                ss, s, n, nn = [AX[f, k, r : r + 8, :] for r in (6, 7, 9, 10)]
                y = KAPPA * (n + s)
                mixed = (
                    part[k]
                    + 8.0 * y
                    - 2.0 * (roll(y, -1) + roll(y, 1))
                    - KAPPA * (nn + ss)
                    - jnp.where(edge4, roll(edges[f], LANES - 4 - 8 * i), 0.0)
                )
                out[k] = jnp.where(cc0 > i, mixed, 0.0)
        levels = pl.ds(c * LC, LC)
        pltpu.make_async_copy(TO.at[levels], t_out.at[levels], sem.at[3]).start()
        pltpu.make_async_copy(SO.at[levels], s_out.at[levels], sem.at[4]).start()

    for copy in copies:
        copy.wait()
    pltpu.make_async_copy(TO, t_out, sem.at[3]).wait()
    pltpu.make_async_copy(SO, s_out, sem.at[4]).wait()


def per_device(nx, ny, *args):
    tile3 = jax.ShapeDtypeStruct((K, ROWS, LANES), jnp.float32)
    tile2 = jax.ShapeDtypeStruct((ROWS, LANES), jnp.float32)
    outs = (tile3, tile3, tile3, tile3, tile2)

    def vmem(*shape, dtype=jnp.float32):
        return pltpu.VMEM(shape, dtype)

    args = [pltpu.with_memory_space_constraint(x, pltpu.HBM) for x in args]
    held = pl.pallas_call(
        functools.partial(kernel, nx, ny),
        out_shape=tuple(
            pltpu.VMEM(shape, jnp.float32)
            for shape in [x.shape for x in outs]
            + [(2, K, 24, LANES), (2, NC, ROWS, LANES), (24, LANES)]
        ),
        in_specs=[pl.BlockSpec(memory_space=pltpu.HBM)] * 7,
        out_specs=[pl.BlockSpec(memory_space=pltpu.VMEM)] * 8,
        scratch_shapes=[
            vmem(4, K, 24, LANES),
            vmem(K, 16, LANES),
            vmem(2, 3, 24, LANES),
            vmem(ROWS, LANES),
            vmem(ROWS, LANES, dtype=jnp.int32),
            vmem(ROWS, LANES, dtype=jnp.int32),
            vmem(24, LANES),
            vmem(24, LANES),
            vmem(2, 24, LANES),
            vmem(2, 24, LANES),
            vmem(2, 24, LANES),
            vmem(2, 24, LANES),
            vmem(1, NM, 16, LANES),
            vmem(1, NM, 16, LANES),
            vmem(1, NM, 16, LANES),
            vmem(NM, ROWS, LANES),
            vmem(NM, ROWS, LANES),
            vmem(2, NC, 16, LANES),
            vmem(2, NC, 16, LANES),
            vmem(2, NC, 16, LANES),
            vmem(4, 24, LANES),
            vmem(ROWS, LANES),
            vmem(3, 24, LANES),
            vmem(2, 24, LANES),
            vmem(4, ROWS, LANES),
            vmem(K, ROWS, LANES),
            vmem(K, 16, LANES),
            vmem(2, NC, ROWS, LANES),
            vmem(2, NC, 16, LANES),
            vmem(2, NC, 16, LANES),
            vmem(2, NC, 16, LANES),
            vmem(NM, ROWS, LANES),
            vmem(2, NC, ROWS, LANES),
            vmem(2, K, ROWS, LANES),
            vmem(2, K, 16, LANES),
            vmem(2, NC, ROWS, LANES),
            vmem(2, NC, ROWS, LANES),
            vmem(2, 4, NC, ROWS, LANES),
            pltpu.SemaphoreType.DMA((2,)),
            pltpu.SemaphoreType.DMA((GROUPS,)),
            pltpu.SemaphoreType.DMA((GROUPS,)),
        ],
        compiler_params=pltpu.CompilerParams(
            collective_id=0, has_side_effects=True, vmem_limit_bytes=24 * 1024 * 1024
        ),
    )(*args)
    return pl.pallas_call(
        finish,
        out_shape=outs,
        in_specs=[pl.BlockSpec(memory_space=pltpu.VMEM)] * 8,
        out_specs=[pl.BlockSpec(memory_space=pltpu.HBM)] * 5,
        scratch_shapes=[
            vmem(K, ROWS, LANES),
            vmem(K, ROWS, LANES),
            pltpu.SemaphoreType.DMA((5,)),
        ],
        compiler_params=pltpu.CompilerParams(vmem_limit_bytes=8 * 1024 * 1024),
    )(*held)


def solution(mesh):
    placed = (P(None, "gy", "gx"),) * 4 + (P("gy", "gx"),) * 3
    return jax.shard_map(
        functools.partial(per_device, mesh.shape["gx"], mesh.shape["gy"]),
        mesh=mesh,
        in_specs=placed,
        out_specs=(P(None, "gy", "gx"),) * 4 + (P("gy", "gx"),),
        check_vma=False,
    )
```

```python
import functools

import jax
import jax.numpy as jnp
from jax import lax
from jax.experimental import pallas as pl
from jax.experimental.pallas import tpu as pltpu
from jax.sharding import PartitionSpec as P

MESH = pl.DeviceIdType.MESH
K = 75
NC = 5
LC = K // NC
NM = 5
LM = K // NM
SUBSTEPS = 8
ROWS = 8
LANES = 128

DT = 0.4
NU = 0.025
KAPPA = 0.01
DTT = 0.2
GRAVITY = 4.0
DB = DT / SUBSTEPS

GROUPS = 9
G_2D, G_A, G_TS, G_SUM, G_B, G_UP, G_DOWN, G_UP_EDGE, G_DOWN_EDGE = range(GROUPS)


def kernel(
    nx,
    ny,
    t_in,
    s_in,
    u_in,
    v_in,
    h_in,
    flag_in,
    bottom_in,
    TN,
    SN,
    UN,
    VN,
    HN,
    AX,
    EM,
    CC,
    X,
    PX,
    D2,
    ET,
    flag_v,
    bottom_v,
    CU,
    CV,
    SC,
    SU,
    SV,
    S4,
    pack,
    PE,
    PW,
    packp,
    PP,
    pack_ts,
    TE,
    TW,
    F2,
    FT,
    FE,
    DV,
    DP,
    U1B,
    V1X,
    pack1,
    P1E,
    P1W,
    for_east,
    for_west,
    AD,
    EUV,
    HC,
    CE,
    CN,
    FW,
    HS,
    HO,
    load_sem,
    send_sem,
    recv_sem,
):
    gx, gy = lax.axis_index("gx"), lax.axis_index("gy")

    def device(dx, dy):
        return (lax.rem(gx + dx + nx, nx), lax.rem(gy + dy + ny, ny))

    def send(group, src, dst, dx, dy):
        pltpu.make_async_remote_copy(
            src_ref=src,
            dst_ref=dst,
            send_sem=send_sem.at[group],
            recv_sem=recv_sem.at[group],
            device_id=device(dx, dy),
            device_id_type=MESH,
        ).start()

    def received(group, size):
        pltpu.make_async_copy(size, size, recv_sem.at[group]).wait()

    def left(group, size):
        pltpu.make_async_copy(size, size, send_sem.at[group]).wait()

    has_south, has_north = gy > 0, gy < ny - 1

    def beside(dy):
        return pl.when(has_north if dy > 0 else has_south)

    barrier = pltpu.get_barrier_semaphore()

    def greet(dx, dy):
        pl.semaphore_signal(barrier, inc=1, device_id=device(dx, dy), device_id_type=MESH)

    for dy in (-1, 1):

        @beside(dy)
        def _():
            for dx in (-1, 1, 0):
                greet(dx, dy)

    for dx in (-1, 1):
        greet(dx, 0)

    pltpu.make_async_copy(flag_in, flag_v, load_sem.at[0]).start()
    pltpu.make_async_copy(bottom_in, bottom_v, load_sem.at[0]).start()
    pltpu.make_async_copy(h_in, D2.at[1, 1, pl.ds(8, 8), :], load_sem.at[0]).start()
    for f, source in enumerate((u_in, v_in, t_in, s_in)):
        pltpu.make_async_copy(source, X.at[f, :, pl.ds(8, 8), :], load_sem.at[1]).start()

    def loaded(sem, size):
        pltpu.make_async_copy(size, size, load_sem.at[sem]).wait()

    lane = lax.broadcasted_iota(jnp.int32, (ROWS, LANES), 1)
    slot = lax.div(lane, 8).astype(jnp.float32)
    row = lax.broadcasted_iota(jnp.int32, (ROWS, LANES), 0)
    first, last = lane == 0, lane == LANES - 1
    half = 0.5 * DTT
    edge4 = jnp.logical_or(lane < 2, lane >= LANES - 2)
    slot4 = lax.div(lane, 4).astype(jnp.float32)
    zero = jnp.zeros((ROWS, LANES), jnp.float32)

    def roll(x, shift):
        return pltpu.roll(x, shift % LANES, x.ndim - 1)

    def packed(x, i, width=8):
        return roll(x, width * i + width // 2)

    def unpacked(x, i, width=8):
        return roll(x, LANES - width // 2 - width * i)

    def in_slots(x, lanes, width=8):
        at = lax.rem(lax.broadcasted_iota(jnp.int32, x.shape, 1), width)
        out = None
        for l in lanes:
            column = jnp.broadcast_to(x[:, l : l + 1], x.shape)
            out = column if out is None else jnp.where(at == (l + width // 2) % LANES, column, out)
        return out

    @pl.when(jnp.logical_not(has_south))
    def _():
        AD[:, :, 0:1, :] = jnp.zeros((2, NC, 1, LANES), jnp.float32)

        @pl.loop(0, K)
        def _(k):
            for f in range(2):
                AX[f, k, 6:8, :] = jnp.zeros((2, LANES), jnp.float32)

    @pl.when(jnp.logical_not(has_north))
    def _():
        AD[:, :, 9:10, :] = jnp.zeros((2, NC, 1, LANES), jnp.float32)

        @pl.loop(0, K)
        def _(k):
            for f in range(2):
                AX[f, k, 16:18, :] = jnp.zeros((2, LANES), jnp.float32)

    loaded(0, AX.at[0, pl.ds(0, 3), pl.ds(8, 8), :])
    own = (flag_v[...] * bottom_v[...]).astype(jnp.float32)
    D2[0, 1, 8:16, :] = own
    ET[...] = jnp.where(jnp.logical_and(lane >= 32, lane < 96), roll(D2[1, 1, 8:16, :], 64), own)

    def rows(group, fields, count, dy):
        src, dst = (16 - count, 8 - count) if dy > 0 else (8, 16)
        send(
            group,
            X.at[fields, :, pl.ds(src, count), :],
            X.at[fields, :, pl.ds(dst, count), :],
            0,
            dy,
        )

    loaded(1, X.at[:, :, pl.ds(8, 8), :])
    def weight(t, s, dz):
        return (0.8 * s - t * (0.2 + 0.05 * t)) * dz

    def thickness(base, i):
        return 0.5 / K + (base + (i + 0.5)) * (1.0 / (K * K))

    def press(c, cum):
        base = (c * LM).astype(jnp.float32)
        depth = D2[0, 1, 8:16, :] - base
        held = held_p = zero
        for i in range(LM):
            k = c * LM + i
            u, v, t, s = [X[f, k, 8:16, :] for f in range(4)]
            w = jnp.where(depth > i, weight(t, s, DT * thickness(base, i)), 0.0)
            cum = cum + w
            load = cum - 0.5 * w
            PX[k, 0:8, :] = load
            held = jnp.where(slot4 == i, packed(u, i, 4), held)
            held = jnp.where(slot4 == i + 16, packed(v, i + 16, 4), held)
            held_p = jnp.where(slot4 == i, packed(load, i, 4), held_p)
        pack[0, c, 1:9, :] = held
        packp[c] = held_p
        return cum

    lax.fori_loop(0, NM, press, zero)

    pl.semaphore_wait(
        barrier, 2 + 3 * (has_south.astype(jnp.int32) + has_north.astype(jnp.int32))
    )

    def corners(group, src, west, east, dy):
        for dx in (1, -1):
            side = west if dx > 0 else east
            r_src, r_dst = (8, 0) if dy > 0 else (1, 9)
            send(
                group,
                src.at[:, :, pl.ds(r_src, 1), :],
                side.at[:, :, pl.ds(r_dst, 1), :],
                dx,
                dy,
            )

    def pole(group, ref, dy):
        src, dst = (8, 0) if dy > 0 else (1, 9)
        send(group, ref.at[:, :, pl.ds(src, 1), :], ref.at[:, :, pl.ds(dst, 1), :], 0, dy)

    def edge_tiles(group, edge, aside, dy):
        for dx in (-1, 1):
            send(group, edge, aside(1 - dx).at[pl.ds(8 * (1 - dy), 8), :], dx, dy)

    def whole_tiles(group, whole, dy):
        send(group, whole.at[:, pl.ds(8, 8), :], whole.at[:, pl.ds(8 * (1 - dy), 8), :], 0, dy)

    def edges_2d(dy):
        edge_tiles(G_2D, ET, lambda n: D2.at[0, n], dy)

    for dy in (-1, 1):

        @beside(dy)
        def _():
            edges_2d(dy)
            corners(G_A, pack, PW, PE, dy)

    edges_2d(0)
    for dx in (1, -1):
        side = PW if dx > 0 else PE
        send(G_A, pack.at[:, :, pl.ds(1, 8), :], side.at[:, :, pl.ds(1, 8), :], dx, 0)
    send(G_A, packp, PP, -1, 0)
    for dy in (-1, 1):

        @beside(dy)
        def _():
            whole_tiles(G_2D, D2.at[:, 1], dy)
            rows(G_A, pl.ds(0, 2), 2, dy)
            pole(G_A, pack, dy)
            if dy < 0:
                send(G_A, PX.at[:, pl.ds(0, 1), :], PX.at[:, pl.ds(8, 1), :], 0, dy)

    @pl.loop(0, NC)
    def _(c):
        held = [zero] * 2
        for i in range(LC):
            for f in range(2):
                held[f] = jnp.where(slot == i, packed(X[2 + f, c * LC + i, 8:16, :], i), held[f])
        for f in range(2):
            pack_ts[f, c, 1:9, :] = held[f]

    for dx in (1, -1):
        side = TW if dx > 0 else TE
        send(G_TS, pack_ts.at[:, :, pl.ds(1, 8), :], side.at[:, :, pl.ds(1, 8), :], dx, 0)
    for dy in (-1, 1):

        @beside(dy)
        def _():
            corners(G_TS, pack_ts, TW, TE, dy)
            rows(G_TS, pl.ds(2, 2), 1, dy)
            pole(G_TS, pack_ts, dy)

    def size(levels, count):
        return X.at[0, pl.ds(0, levels), pl.ds(0, count), :]

    def by_walls(wait, group, inner, southmost, northmost):
        @pl.when(jnp.logical_and(has_south, has_north))
        def _():
            wait(group, size(*inner))

        @pl.when(jnp.logical_not(has_south))
        def _():
            wait(group, size(*southmost))

        @pl.when(jnp.logical_not(has_north))
        def _():
            wait(group, size(*northmost))

    by_walls(received, G_2D, (10, 8), (6, 8), (6, 8))
    row24 = lax.broadcasted_iota(jnp.int32, (24, LANES), 0)
    lane24 = lax.broadcasted_iota(jnp.int32, (24, LANES), 1)
    slot24 = lax.rem(lane24, 8)
    first24, last24 = lane24 == 0, lane24 == LANES - 1
    inside = jnp.logical_and(
        jnp.logical_or(row24 >= 8, has_south), jnp.logical_or(row24 < 16, has_north)
    )

    def ring_east(c, h, seam=first24):
        return (
            roll(jnp.where(seam, h, c), LANES - 1),
            roll(jnp.where(seam, c, h), LANES - 1),
        )

    def ring_west(c, h):
        return (
            roll(jnp.where(last24, h, c), 1),
            roll(jnp.where(last24, c, h), 1),
        )

    def north24(x):
        return pltpu.roll(x, 23, 0)

    def south24(x):
        return pltpu.roll(x, 1, 0)

    edges = jnp.where(lax.rem(lane24, 64) < 32, D2[0, 2], D2[0, 0])
    col = [jnp.where(inside, x, 0.0) for x in (D2[0, 1], edges)]
    ocean = [x > 0.0 for x in col]
    cu = [jnp.minimum(a, b) for a, b in zip(col, ring_east(*col))]
    cv = [jnp.minimum(a, north24(a)) for a in col]
    CC[...] = col[0]
    CU[...] = cu[0]
    CV[...] = cv[0]
    for n in range(2):
        S4[n] = jnp.where(
            lane24 < 64,
            in_slots(cu[1 - n], (126, 127, 0, 1), 4),
            in_slots(cv[1 - n], (126, 127, 0, 1), 4),
        )

    at_wall = jnp.where(
        jnp.logical_or(
            jnp.logical_and(row == 0, jnp.logical_not(has_south)),
            jnp.logical_and(row == ROWS - 1, jnp.logical_not(has_north)),
        ),
        19.0,
        20.0,
    )
    latitude = (row + gy * ROWS).astype(jnp.float32)
    f4 = (0.25 * DT) * (0.2 + 0.3 * (latitude + 0.5) / (ROWS * ny))
    centre_uv = 1.0 - (DT * NU) * at_wall
    centre_ts = 1.0 - KAPPA * at_wall

    by_walls(received, G_A, (K, 11), (51, 10), (29, 15))
    by_walls(left, G_A, (K, 11), (29, 15), (51, 10))

    @pl.loop(0, NC)
    def _(c):
        base = (c * LC).astype(jnp.float32)
        for f, depths in ((0, CU), (1, CV)):
            low, high = depths[6:14, :] - base, depths[10:18, :] - base
            for i in range(LC):
                k = c * LC + i
                a = jnp.where(low > i, X[f, k, 6:14, :], 0.0)
                b = jnp.where(high > i, X[f, k, 10:18, :], 0.0)
                X[f, k, 6:14, :] = a
                X[f, k, 10:18, :] = b

    class Slots:
        def __init__(self, count, width, span):
            shape = (count, ROWS, LANES)
            self.lanes = lax.broadcasted_iota(jnp.int32, shape, 2)
            self.place = lax.rem(self.lanes, width)
            tile = lax.broadcasted_iota(jnp.int32, shape, 0)
            self.level = (lax.div(lax.rem(self.lanes, span), width) + tile * (K // count)).astype(
                jnp.float32
            )
            self.west, self.east = self.place == width // 2 - 1, self.place == width // 2
            self.western = self.place < width // 2

        def beyond(self, west, east, f, r):
            return jnp.where(self.western, west[f, :, r : r + 8, :], east[f, :, r : r + 8, :])

        def if_wet(self, depths, n, r, x):
            return jnp.where(self.level < depths[n, r + 7 : r + 15, :][None], x, 0.0)

        def far(self, d, y):
            z = 2.0 * y - 8.0 * d
            return jnp.where(self.western, roll(d, -2), roll(d, 2)) + jnp.where(
                self.west, roll(z, -1), jnp.where(self.east, roll(z, 1), 0.0)
            )

    by4, by8 = Slots(NM, 4, 64), Slots(NC, 8, LANES)

    def excess(r):
        return by4.if_wet(S4, 0, r, by4.beyond(PW, PE, 0, r)) - by4.if_wet(
            S4, 1, r, pack[0, :, r : r + 8, :]
        )

    d_s, d, d_n = [excess(r) for r in range(3)]
    dp = PP[...] - packp[...]
    u_half = by4.lanes < 64
    EUV[...] = (
        jnp.where(
            jnp.logical_and(by4.west, u_half),
            f4[None] * roll(d + d_s, -65) - roll(dp, -1),
            jnp.where(
                jnp.logical_and(by4.east, jnp.logical_not(u_half)),
                -f4[None] * roll(d + d_n, 65),
                0.0,
            ),
        )
        - (DT * NU) * by4.far(d, d_n + d_s)
    )

    def momentum(c, carry):
        sum_u0, sum_v0, sum_u, sum_v = carry
        base = (c * LM).astype(jnp.float32)
        edge = EUV[c]
        cu0, cv0 = CU[8:16, :] - base, CV[8:16, :] - base
        for i in range(LM):
            k = c * LM + i
            dz = thickness(base, i)
            uss, us, u, un, unn = [X[0, k, r : r + 8, :] for r in range(6, 11)]
            vss, vs, v, vn, vnn = [X[1, k, r : r + 8, :] for r in range(6, 11)]
            load, load_n = PX[k, 0:8, :], PX[k, 1:9, :]
            cross_u = f4 * (v + vs)
            cross_v = f4 * (u + un)
            yu, yv = (DT * NU) * (un + us), (DT * NU) * (vn + vs)
            au, av = (DT * NU) * u, (DT * NU) * v
            zu, zv = 8.0 * au - 2.0 * yu, 8.0 * av - 2.0 * yv
            u1 = (
                centre_uv * u
                + 8.0 * yu
                - (DT * NU) * (unn + uss)
                + (cross_u + load)
                + (roll(zu + (cross_u - load), -1) + roll(zu, 1))
                - (roll(au, -2) + roll(au, 2))
                + jnp.where(edge4, unpacked(edge, i, 4), 0.0)
            )
            v1 = (
                centre_uv * v
                + 8.0 * yv
                - (DT * NU) * (vnn + vss)
                - cross_v
                - (load_n - load)
                + (roll(zv, -1) + roll(zv - cross_v, 1))
                - (roll(av, -2) + roll(av, 2))
                + jnp.where(edge4, unpacked(edge, i + 16, 4), 0.0)
            )
            u1 = jnp.where(cu0 > i, u1, 0.0)
            v1 = jnp.where(cv0 > i, v1, 0.0)
            sum_u0 = sum_u0 + u * dz
            sum_v0 = sum_v0 + v * dz
            sum_u = sum_u + u1 * dz
            sum_v = sum_v + v1 * dz
            U1B[k] = u1
            V1X[k, 8:16, :] = v1
        return sum_u0, sum_v0, sum_u, sum_v

    sums = lax.fori_loop(0, NM, momentum, (zero,) * 4)

    edge = sums[0]
    for n in range(4):
        F2[n, 8:16, :] = sums[n]
        near = jnp.logical_and(lane >= 32 * n - 16, lane < 32 * n + 16)
        edge = jnp.where(near, roll(sums[n], 32 * n), edge)
    FT[...] = edge
    for dy in (-1, 1):

        @beside(dy)
        def _():
            edge_tiles(G_SUM, FT, lambda n: FE.at[n], dy)

    edge_tiles(G_SUM, FT, lambda n: FE.at[n], 0)
    for dy in (-1, 1):

        @beside(dy)
        def _():
            whole_tiles(G_SUM, F2, dy)


    @beside(1)
    def _():
        send(G_B, V1X.at[:, pl.ds(15, 1), :], V1X.at[:, pl.ds(7, 1), :], 0, 1)

    @pl.loop(0, NC)
    def _(c):
        held_u = held_v = zero
        for i in range(LC):
            k = c * LC + i
            held_u = jnp.where(slot == i, packed(U1B[k], i), held_u)
            held_v = jnp.where(slot == i, packed(V1X[k, 8:16, :], i), held_v)
        pack1[0, c, 1:9, :] = held_u
        pack1[1, c, 1:9, :] = held_v

    for_east[...] = jnp.where(by8.western, pack1[0, :, 1:9, :], roll(pack1[1, :, 1:9, :], 4))
    for_west[...] = jnp.where(by8.western, roll(pack1[0, :, 1:9, :], -4), pack1[1, :, 1:9, :])

    @beside(1)
    def _():
        for dx, src, dst in ((1, for_east, P1W), (-1, for_west, P1E)):
            send(G_B, src.at[:, pl.ds(7, 1), :], dst.at[:, pl.ds(0, 1), :], dx, 1)

    for dx, src, dst in ((1, for_east, P1W), (-1, for_west, P1E)):
        send(G_B, src, dst.at[:, pl.ds(1, 8), :], dx, 0)

    @beside(1)
    def _():
        send(G_B, pack1.at[1, :, pl.ds(8, 1), :], pack1.at[1, :, pl.ds(0, 1), :], 0, 1)

    by_walls(left, G_2D, (10, 8), (6, 8), (6, 8))
    by_walls(left, G_TS, (52, 10), (34, 10), (34, 10))
    by_walls(received, G_TS, (52, 10), (34, 10), (34, 10))

    edge_col = [in_slots(x, (124, 125, 126, 127, 0, 1, 2, 3)) for x in (col[1], col[0])]
    edge_cu = [jnp.minimum(a, b) for a, b in zip(edge_col, ring_east(*edge_col, slot24 == 4))]
    for n in range(2):
        SC[n] = edge_col[n]
        SU[n] = edge_cu[n]
        SV[n] = jnp.minimum(edge_col[n], north24(edge_col[n]))

    for f in range(2):
        south, here, north = [
            by8.if_wet(SC, 0, r, by8.beyond(TW, TE, f, r)) for r in range(3)
        ]
        own_s, own, own_n = [
            by8.if_wet(SC, 1, r, pack_ts[f, :, r : r + 8, :]) for r in range(3)
        ]
        HC[f] = here
        HO[f] = own
        HS[f, 0] = half * (here + roll(jnp.where(by8.east, own, here), -1))
        HS[f, 1] = half * (own + roll(jnp.where(by8.east, here, own), -1))
        HS[f, 2] = half * (here + north)
        HS[f, 3] = half * (south + here)
        HS[f, 4] = half * (own + own_n)
        HS[f, 5] = half * (own_s + own)

    @pl.loop(0, NC)
    def _(c):
        base = (c * LC).astype(jnp.float32)
        low, mid, high = [CC[r : r + 8, :] - base for r in (7, 8, 9)]
        for f in range(2):
            edge = HC[f, c]
            for i in range(LC):
                k = c * LC + i
                south = jnp.where(low > i, X[2 + f, k, 7:15, :], 0.0)
                here = jnp.where(mid > i, X[2 + f, k, 8:16, :], 0.0)
                north = jnp.where(high > i, X[2 + f, k, 9:17, :], 0.0)
                X[2 + f, k, 7:15, :] = south
                X[2 + f, k, 9:17, :] = north
                east = jnp.where(last, roll(edge, LANES - 5 - 8 * i), roll(here, -1))
                CE[f, k] = half * (here + east)
                CN[f, k, 7:15, :] = half * (south + here)
                CN[f, k, 8:16, :] = half * (here + north)

    def both(op, *pairs):
        return [op(*xs) for xs in zip(*pairs)]

    def depth_of(c):
        return c * (0.5 / K + c * (0.5 / (K * K)))

    open_u = [(x > 0.0).astype(jnp.float32) for x in cu]
    open_v = [(x > 0.0).astype(jnp.float32) for x in cv]
    depth_u = both(depth_of, cu)
    depth_v = both(depth_of, cv)
    pull_u = both(lambda o, d: o * d * (DB * GRAVITY), open_u, depth_u)
    pull_v = both(lambda o, d: o * d * (DB * GRAVITY), open_v, depth_v)
    pull_w = ring_west(*pull_u)
    ease = both(lambda o: jnp.where(o, DB, 0.0), ocean)
    height = [jnp.where(o, x, 0.0) for o, x in zip(ocean, (D2[1, 1], roll(edges, 64)))]

    inverse_u = both(lambda d, o: 1.0 / (d + (1.0 - o)), depth_u, open_u)
    inverse_v = both(lambda d, o: 1.0 / (d + (1.0 - o)), depth_v, open_v)
    by_walls(received, G_SUM, (14, 8), (8, 8), (8, 8))
    edges = jnp.where(lax.rem(lane24, 32) < 16, FE[2], FE[0])
    u0, v0, u_all, v_all = [[F2[n], roll(edges, -32 * n)] for n in range(4)]
    push_u = both(lambda o, a, b: jnp.where(o > 0.0, (a - b) * (DB / DT), 0.0), open_u, u_all, u0)
    push_v = both(lambda o, a, b: jnp.where(o > 0.0, (a - b) * (DB / DT), 0.0), open_v, v_all, v0)
    trans_u = both(lambda o, a: jnp.where(o > 0.0, a, 0.0), open_u, u0)
    trans_v = both(lambda o, a: jnp.where(o > 0.0, a, 0.0), open_v, v0)
    run_u = [jnp.zeros((24, LANES), jnp.float32)] * 2
    run_v = run_u

    def substep(_, state):
        level, trans_u, trans_w, trans_v, run_u, run_v = state
        level_w = ring_west(*level)
        trans_w = both(
            lambda t, p, q, h, w: t + (p - q * (h - w)), trans_w, push_w, pull_w, level, level_w
        )
        trans_u = both(
            lambda t, p, q, e, h: t + (p - q * (e - h)),
            trans_u,
            push_u,
            pull_u,
            ring_east(*level),
            level,
        )
        trans_v = both(
            lambda t, p, q, h: t + (p - q * (north24(h) - h)), trans_v, push_v, pull_v, level
        )
        level = both(
            lambda h, e, u, w, v: h - e * ((u - w) + (v - south24(v))),
            level,
            ease,
            trans_u,
            trans_w,
            trans_v,
        )
        return level, trans_u, trans_w, trans_v, both(jnp.add, run_u, trans_u), both(jnp.add, run_v, trans_v)

    trans_w, push_w = ring_west(*trans_u), ring_west(*push_u)
    state = height, trans_u, trans_w, trans_v, run_u, run_v
    for n in range(SUBSTEPS):
        state = substep(n, state)
    height, _, _, _, run_u, run_v = state

    HN[...] = height[0][8:16]

    def shift(r, a, inverse):
        return (r * (1.0 / SUBSTEPS) - a) * inverse

    shift_u = both(shift, run_u, u_all, inverse_u)
    shift_v = both(shift, run_v, v_all, inverse_v)
    DV[0] = shift_v[0]
    DV[1] = shift_v[1]
    du, dv, dvs = shift_u[0][8:16], shift_v[0][8:16], DV[0, 7:15, :]
    DP[0] = in_slots(shift_u[1][8:16], (125, 126, 127, 0, 1))
    DP[1] = in_slots(DV[1, 8:16, :], (126, 127, 0, 1))
    DP[2] = in_slots(DV[1, 7:15, :], (126, 127, 0, 1))
    DP[3] = in_slots(du, (125, 126, 127, 0, 1))
    DP[4] = in_slots(dv, (126, 127, 0, 1))
    DP[5] = in_slots(dvs, (126, 127, 0, 1))

    by_walls(received, G_B, (17, 10), (10, 8), (17, 10))
    beyond_u = jnp.where(by8.western, P1W[:, 1:9, :], roll(P1E[:, 1:9, :], 4))
    beyond_v = jnp.where(by8.western, roll(P1W[:, 1:9, :], -4), P1E[:, 1:9, :])
    beyond_vs = jnp.where(by8.western, roll(P1W[:, 0:8, :], -4), P1E[:, 0:8, :])
    edge_u = by8.if_wet(SU, 0, 1, beyond_u + DP[0][None])
    edge_v = by8.if_wet(SV, 0, 1, beyond_v + DP[1][None])
    edge_vs = by8.if_wet(SV, 0, 0, beyond_vs + DP[2][None])
    own_u = by8.if_wet(SU, 1, 1, pack1[0, :, 1:9, :] + DP[3][None])
    own_v = by8.if_wet(SV, 1, 1, pack1[1, :, 1:9, :] + DP[4][None])
    own_vs = by8.if_wet(SV, 1, 0, pack1[1, :, 0:8, :] + DP[5][None])
    for f in range(2):
        flux, flux_own = edge_u * HS[f, 0], own_u * HS[f, 1]
        flux_west = roll(jnp.where(by8.west, flux_own, flux), 1)
        flux_own_west = roll(jnp.where(by8.west, flux, flux_own), 1)
        a = HC[f] - ((flux - flux_west) + (edge_v * HS[f, 2] - edge_vs * HS[f, 3]))
        own = HO[f] - ((flux_own - flux_own_west) + (own_v * HS[f, 4] - own_vs * HS[f, 5]))
        FW[f] = flux
        AD[f, :, 1:9, :] = by8.if_wet(SC, 0, 1, a) - by8.if_wet(SC, 1, 1, own)

    @beside(1)
    def _():
        send(G_UP_EDGE, AD.at[:, :, pl.ds(8, 1), :], AD.at[:, :, pl.ds(0, 1), :], 0, 1)

    @beside(-1)
    def _():
        send(G_DOWN_EDGE, AD.at[:, :, pl.ds(1, 1), :], AD.at[:, :, pl.ds(9, 1), :], 0, -1)

    def send_rows(c, up):
        src, dst, dy, group = (14, 6, 1, G_UP) if up else (8, 16, -1, G_DOWN)
        levels = pl.ds(c * LC, LC)
        send(
            group,
            AX.at[:, levels, pl.ds(src, 2), :],
            AX.at[:, levels, pl.ds(dst, 2), :],
            0,
            dy,
        )

    @pl.loop(0, NC)
    def _(c):
        base = (c * LC).astype(jnp.float32)
        edges = [FW[f, c] for f in range(2)]
        cc0, cu0, cv0 = CC[8:16, :] - base, CU[8:16, :] - base, CV[8:16, :] - base
        cvs = CV[7:15, :] - base
        for i in range(LC):
            k = c * LC + i
            u = jnp.where(cu0 > i, U1B[k] + du, 0.0)
            v = jnp.where(cv0 > i, V1X[k, 8:16, :] + dv, 0.0)
            vs = jnp.where(cvs > i, V1X[k, 7:15, :] + dvs, 0.0)
            UN[k] = u
            VN[k] = v
            for f in range(2):
                flux = u * CE[f, k]
                flux_west = jnp.where(first, roll(edges[f], LANES - 3 - 8 * i), roll(flux, 1))
                a = X[2 + f, k, 8:16, :] - (
                    (flux - flux_west) + (v * CN[f, k, 8:16, :] - vs * CN[f, k, 7:15, :])
                )
                a = jnp.where(cc0 > i, a, 0.0)
                AX[f, k, 8:16, :] = a

        @pl.when(has_north)
        def _():
            send_rows(c, True)

        @pl.when(has_south)
        def _():
            send_rows(c, False)

    by_walls(left, G_SUM, (14, 8), (8, 8), (8, 8))
    by_walls(left, G_B, (17, 10), (17, 10), (10, 8))

    @pl.loop(0, NC)
    def _(c):
        for i in range(LC):
            k = c * LC + i
            for f, out in ((0, TN), (1, SN)):
                a = AX[f, k, 8:16, :]
                b = KAPPA * a
                out[k] = (
                    centre_ts * a
                    + 8.0 * (roll(b, -1) + roll(b, 1))
                    - (roll(b, -2) + roll(b, 2))
                )

    edge_row = AD.at[:, :, pl.ds(0, 1), :]
    two_rows = X.at[pl.ds(0, 2), :, pl.ds(0, 2), :]

    @beside(-1)
    def _():
        received(G_UP_EDGE, edge_row)

    @beside(1)
    def _():
        received(G_DOWN_EDGE, edge_row)

    for f in range(2):
        south, here, north = [AD[f, :, r : r + 8, :] for r in range(3)]
        EM[f] = KAPPA * by8.far(here, south + north)

    @beside(-1)
    def _():
        received(G_UP, two_rows)
        left(G_DOWN, two_rows)
        left(G_DOWN_EDGE, edge_row)

    @beside(1)
    def _():
        received(G_DOWN, two_rows)
        left(G_UP, two_rows)
        left(G_UP_EDGE, edge_row)


def finish(TN, SN, UN, VN, HN, AX, EM, CC, t_out, s_out, u_out, v_out, h_out, TO, SO, sem):
    copies = [
        pltpu.make_async_copy(src, dst, sem.at[n])
        for n, (src, dst) in enumerate(((UN, u_out), (VN, v_out), (HN, h_out)))
    ]
    for copy in copies:
        copy.start()
    lane = lax.broadcasted_iota(jnp.int32, (ROWS, LANES), 1)
    edge4 = jnp.logical_or(lane < 2, lane >= LANES - 2)

    def roll(x, shift):
        return pltpu.roll(x, shift % LANES, 1)

    @pl.loop(0, NC)
    def _(c):
        cc0 = CC[8:16, :] - (c * LC).astype(jnp.float32)
        edges = [EM[f, c] for f in range(2)]
        for i in range(LC):
            k = c * LC + i
            for f, part, out in ((0, TN, TO), (1, SN, SO)):
                ss, s, n, nn = [AX[f, k, r : r + 8, :] for r in (6, 7, 9, 10)]
                y = KAPPA * (n + s)
                mixed = (
                    part[k]
                    + 8.0 * y
                    - 2.0 * (roll(y, -1) + roll(y, 1))
                    - KAPPA * (nn + ss)
                    - jnp.where(edge4, roll(edges[f], LANES - 4 - 8 * i), 0.0)
                )
                out[k] = jnp.where(cc0 > i, mixed, 0.0)
        levels = pl.ds(c * LC, LC)
        pltpu.make_async_copy(TO.at[levels], t_out.at[levels], sem.at[3]).start()
        pltpu.make_async_copy(SO.at[levels], s_out.at[levels], sem.at[4]).start()

    for copy in copies:
        copy.wait()
    pltpu.make_async_copy(TO, t_out, sem.at[3]).wait()
    pltpu.make_async_copy(SO, s_out, sem.at[4]).wait()


def per_device(nx, ny, *args):
    tile3 = jax.ShapeDtypeStruct((K, ROWS, LANES), jnp.float32)
    tile2 = jax.ShapeDtypeStruct((ROWS, LANES), jnp.float32)
    outs = (tile3, tile3, tile3, tile3, tile2)

    def vmem(*shape, dtype=jnp.float32):
        return pltpu.VMEM(shape, dtype)

    args = [pltpu.with_memory_space_constraint(x, pltpu.HBM) for x in args]
    held = pl.pallas_call(
        functools.partial(kernel, nx, ny),
        out_shape=tuple(
            pltpu.VMEM(shape, jnp.float32)
            for shape in [x.shape for x in outs]
            + [(2, K, 24, LANES), (2, NC, ROWS, LANES), (24, LANES)]
        ),
        in_specs=[pl.BlockSpec(memory_space=pltpu.HBM)] * 7,
        out_specs=[pl.BlockSpec(memory_space=pltpu.VMEM)] * 8,
        scratch_shapes=[
            vmem(4, K, 24, LANES),
            vmem(K, 16, LANES),
            vmem(2, 3, 24, LANES),
            vmem(ROWS, LANES),
            vmem(ROWS, LANES, dtype=jnp.int32),
            vmem(ROWS, LANES, dtype=jnp.int32),
            vmem(24, LANES),
            vmem(24, LANES),
            vmem(2, 24, LANES),
            vmem(2, 24, LANES),
            vmem(2, 24, LANES),
            vmem(2, 24, LANES),
            vmem(1, NM, 16, LANES),
            vmem(1, NM, 16, LANES),
            vmem(1, NM, 16, LANES),
            vmem(NM, ROWS, LANES),
            vmem(NM, ROWS, LANES),
            vmem(2, NC, 16, LANES),
            vmem(2, NC, 16, LANES),
            vmem(2, NC, 16, LANES),
            vmem(4, 24, LANES),
            vmem(ROWS, LANES),
            vmem(3, 24, LANES),
            vmem(2, 24, LANES),
            vmem(6, ROWS, LANES),
            vmem(K, ROWS, LANES),
            vmem(K, 16, LANES),
            vmem(2, NC, 16, LANES),
            vmem(NC, 16, LANES),
            vmem(NC, 16, LANES),
            vmem(NC, ROWS, LANES),
            vmem(NC, ROWS, LANES),
            vmem(2, NC, 16, LANES),
            vmem(NM, ROWS, LANES),
            vmem(2, NC, ROWS, LANES),
            vmem(2, K, ROWS, LANES),
            vmem(2, K, 16, LANES),
            vmem(2, NC, ROWS, LANES),
            vmem(2, 6, NC, ROWS, LANES),
            vmem(2, NC, ROWS, LANES),
            pltpu.SemaphoreType.DMA((2,)),
            pltpu.SemaphoreType.DMA((GROUPS,)),
            pltpu.SemaphoreType.DMA((GROUPS,)),
        ],
        compiler_params=pltpu.CompilerParams(
            collective_id=0, has_side_effects=True, vmem_limit_bytes=24 * 1024 * 1024
        ),
    )(*args)
    return pl.pallas_call(
        finish,
        out_shape=outs,
        in_specs=[pl.BlockSpec(memory_space=pltpu.VMEM)] * 8,
        out_specs=[pl.BlockSpec(memory_space=pltpu.HBM)] * 5,
        scratch_shapes=[
            vmem(K, ROWS, LANES),
            vmem(K, ROWS, LANES),
            pltpu.SemaphoreType.DMA((5,)),
        ],
        compiler_params=pltpu.CompilerParams(vmem_limit_bytes=8 * 1024 * 1024),
    )(*held)


def solution(mesh):
    placed = (P(None, "gy", "gx"),) * 4 + (P("gy", "gx"),) * 3
    return jax.shard_map(
        functools.partial(per_device, mesh.shape["gx"], mesh.shape["gy"]),
        mesh=mesh,
        in_specs=placed,
        out_specs=(P(None, "gy", "gx"),) * 4 + (P("gy", "gx"),),
        check_vma=False,
    )
```

```python
import functools

import jax
import jax.numpy as jnp
from jax import lax
from jax.experimental import pallas as pl
from jax.experimental.pallas import tpu as pltpu
from jax.sharding import PartitionSpec as P

MESH = pl.DeviceIdType.MESH
K = 75
NC = 5
LC = K // NC
NM = 5
LM = K // NM
SUBSTEPS = 8
ROWS = 8
LANES = 128

DT = 0.4
NU = 0.025
KAPPA = 0.01
DTT = 0.2
GRAVITY = 4.0
DB = DT / SUBSTEPS

GROUPS = 9
G_2D, G_A, G_TS, G_SUM, G_B, G_UP, G_DOWN, G_UP_EDGE, G_DOWN_EDGE = range(GROUPS)


def kernel(
    nx,
    ny,
    t_in,
    s_in,
    u_in,
    v_in,
    h_in,
    flag_in,
    bottom_in,
    TN,
    SN,
    UN,
    VN,
    HN,
    AX,
    EM,
    CC,
    XM,
    X,
    PX,
    D2,
    ET,
    flag_v,
    bottom_v,
    CU,
    CV,
    SC,
    SU,
    SV,
    S4,
    pack,
    PE,
    PW,
    packp,
    PP,
    pack_ts,
    TE,
    TW,
    F2,
    FT,
    FE,
    DV,
    DP,
    U1B,
    V1X,
    pack1,
    P1E,
    P1W,
    for_east,
    for_west,
    AD,
    EUV,
    HC,
    CE,
    CN,
    FW,
    HS,
    HO,
    load_sem,
    send_sem,
    recv_sem,
):
    gx, gy = lax.axis_index("gx"), lax.axis_index("gy")

    def device(dx, dy):
        return (lax.rem(gx + dx + nx, nx), lax.rem(gy + dy + ny, ny))

    def send(group, src, dst, dx, dy):
        pltpu.make_async_remote_copy(
            src_ref=src,
            dst_ref=dst,
            send_sem=send_sem.at[group],
            recv_sem=recv_sem.at[group],
            device_id=device(dx, dy),
            device_id_type=MESH,
        ).start()

    def received(group, size):
        pltpu.make_async_copy(size, size, recv_sem.at[group]).wait()

    def left(group, size):
        pltpu.make_async_copy(size, size, send_sem.at[group]).wait()

    has_south, has_north = gy > 0, gy < ny - 1

    def beside(dy):
        return pl.when(has_north if dy > 0 else has_south)

    barrier = pltpu.get_barrier_semaphore()

    def greet(dx, dy):
        pl.semaphore_signal(barrier, inc=1, device_id=device(dx, dy), device_id_type=MESH)

    for dy in (-1, 1):

        @beside(dy)
        def _():
            for dx in (-1, 1, 0):
                greet(dx, dy)

    for dx in (-1, 1):
        greet(dx, 0)

    pltpu.make_async_copy(flag_in, flag_v, load_sem.at[0]).start()
    pltpu.make_async_copy(bottom_in, bottom_v, load_sem.at[0]).start()
    pltpu.make_async_copy(h_in, D2.at[1, 1, pl.ds(8, 8), :], load_sem.at[0]).start()
    for f, source in enumerate((u_in, v_in, t_in, s_in)):
        pltpu.make_async_copy(source, X.at[f, :, pl.ds(8, 8), :], load_sem.at[1]).start()

    def loaded(sem, size):
        pltpu.make_async_copy(size, size, load_sem.at[sem]).wait()

    lane = lax.broadcasted_iota(jnp.int32, (ROWS, LANES), 1)
    slot = lax.div(lane, 8).astype(jnp.float32)
    row = lax.broadcasted_iota(jnp.int32, (ROWS, LANES), 0)
    first, last = lane == 0, lane == LANES - 1
    half = 0.5 * DTT
    edge4 = jnp.logical_or(lane < 2, lane >= LANES - 2)
    slot4 = lax.div(lane, 4).astype(jnp.float32)
    zero = jnp.zeros((ROWS, LANES), jnp.float32)

    def roll(x, shift):
        return pltpu.roll(x, shift % LANES, x.ndim - 1)

    def packed(x, i, width=8):
        return roll(x, width * i + width // 2)

    def unpacked(x, i, width=8):
        return roll(x, LANES - width // 2 - width * i)

    def in_slots(x, lanes, width=8):
        at = lax.rem(lax.broadcasted_iota(jnp.int32, x.shape, 1), width)
        out = None
        for l in lanes:
            column = jnp.broadcast_to(x[:, l : l + 1], x.shape)
            out = column if out is None else jnp.where(at == (l + width // 2) % LANES, column, out)
        return out

    @pl.when(jnp.logical_not(has_south))
    def _():
        AD[:, :, 0:1, :] = jnp.zeros((2, NC, 1, LANES), jnp.float32)

        @pl.loop(0, K)
        def _(k):
            for f in range(2):
                AX[f, k, 6:8, :] = jnp.zeros((2, LANES), jnp.float32)

    @pl.when(jnp.logical_not(has_north))
    def _():
        AD[:, :, 9:10, :] = jnp.zeros((2, NC, 1, LANES), jnp.float32)

        @pl.loop(0, K)
        def _(k):
            for f in range(2):
                AX[f, k, 16:18, :] = jnp.zeros((2, LANES), jnp.float32)

    loaded(0, AX.at[0, pl.ds(0, 3), pl.ds(8, 8), :])
    own = (flag_v[...] * bottom_v[...]).astype(jnp.float32)
    D2[0, 1, 8:16, :] = own
    ET[...] = jnp.where(jnp.logical_and(lane >= 32, lane < 96), roll(D2[1, 1, 8:16, :], 64), own)

    def rows(group, fields, count, dy):
        src, dst = (16 - count, 8 - count) if dy > 0 else (8, 16)
        send(
            group,
            X.at[fields, :, pl.ds(src, count), :],
            X.at[fields, :, pl.ds(dst, count), :],
            0,
            dy,
        )

    loaded(1, X.at[:, :, pl.ds(8, 8), :])
    def weight(t, s, dz):
        return (0.8 * s - t * (0.2 + 0.05 * t)) * dz

    def thickness(base, i):
        return 0.5 / K + (base + (i + 0.5)) * (1.0 / (K * K))

    def press(c, cum):
        base = (c * LM).astype(jnp.float32)
        depth = D2[0, 1, 8:16, :] - base
        held = held_p = zero
        for i in range(LM):
            k = c * LM + i
            u, v, t, s = [X[f, k, 8:16, :] for f in range(4)]
            w = jnp.where(depth > i, weight(t, s, DT * thickness(base, i)), 0.0)
            cum = cum + w
            load = cum - 0.5 * w
            PX[k, 0:8, :] = load
            held = jnp.where(slot4 == i, packed(u, i, 4), held)
            held = jnp.where(slot4 == i + 16, packed(v, i + 16, 4), held)
            held_p = jnp.where(slot4 == i, packed(load, i, 4), held_p)
        pack[0, c, 1:9, :] = held
        packp[c] = held_p
        return cum

    lax.fori_loop(0, NM, press, zero)

    pl.semaphore_wait(
        barrier, 2 + 3 * (has_south.astype(jnp.int32) + has_north.astype(jnp.int32))
    )

    def corners(group, src, west, east, dy):
        for dx in (1, -1):
            side = west if dx > 0 else east
            r_src, r_dst = (8, 0) if dy > 0 else (1, 9)
            send(
                group,
                src.at[:, :, pl.ds(r_src, 1), :],
                side.at[:, :, pl.ds(r_dst, 1), :],
                dx,
                dy,
            )

    def pole(group, ref, dy):
        src, dst = (8, 0) if dy > 0 else (1, 9)
        send(group, ref.at[:, :, pl.ds(src, 1), :], ref.at[:, :, pl.ds(dst, 1), :], 0, dy)

    def edge_tiles(group, edge, aside, dy):
        for dx in (-1, 1):
            send(group, edge, aside(1 - dx).at[pl.ds(8 * (1 - dy), 8), :], dx, dy)

    def whole_tiles(group, whole, dy):
        send(group, whole.at[:, pl.ds(8, 8), :], whole.at[:, pl.ds(8 * (1 - dy), 8), :], 0, dy)

    def edges_2d(dy):
        edge_tiles(G_2D, ET, lambda n: D2.at[0, n], dy)

    for dy in (-1, 1):

        @beside(dy)
        def _():
            edges_2d(dy)
            corners(G_A, pack, PW, PE, dy)

    edges_2d(0)
    for dx in (1, -1):
        side = PW if dx > 0 else PE
        send(G_A, pack.at[:, :, pl.ds(1, 8), :], side.at[:, :, pl.ds(1, 8), :], dx, 0)
    send(G_A, packp, PP, -1, 0)
    for dy in (-1, 1):

        @beside(dy)
        def _():
            whole_tiles(G_2D, D2.at[:, 1], dy)
            rows(G_A, pl.ds(0, 2), 2, dy)
            pole(G_A, pack, dy)
            if dy < 0:
                send(G_A, PX.at[:, pl.ds(0, 1), :], PX.at[:, pl.ds(8, 1), :], 0, dy)

    @pl.loop(0, NC)
    def _(c):
        held = [zero] * 2
        for i in range(LC):
            for f in range(2):
                held[f] = jnp.where(slot == i, packed(X[2 + f, c * LC + i, 8:16, :], i), held[f])
        for f in range(2):
            pack_ts[f, c, 1:9, :] = held[f]

    for dx in (1, -1):
        side = TW if dx > 0 else TE
        send(G_TS, pack_ts.at[:, :, pl.ds(1, 8), :], side.at[:, :, pl.ds(1, 8), :], dx, 0)
    for dy in (-1, 1):

        @beside(dy)
        def _():
            corners(G_TS, pack_ts, TW, TE, dy)
            rows(G_TS, pl.ds(2, 2), 1, dy)
            pole(G_TS, pack_ts, dy)

    def size(levels, count):
        return X.at[0, pl.ds(0, levels), pl.ds(0, count), :]

    def by_walls(wait, group, inner, southmost, northmost):
        @pl.when(jnp.logical_and(has_south, has_north))
        def _():
            wait(group, size(*inner))

        @pl.when(jnp.logical_not(jnp.logical_and(has_south, has_north)))
        def _():
            @pl.when(has_north)
            def _():
                wait(group, size(*southmost))

            @pl.when(has_south)
            def _():
                wait(group, size(*northmost))

    by_walls(received, G_2D, (10, 8), (6, 8), (6, 8))
    row24 = lax.broadcasted_iota(jnp.int32, (24, LANES), 0)
    lane24 = lax.broadcasted_iota(jnp.int32, (24, LANES), 1)
    slot24 = lax.rem(lane24, 8)
    first24, last24 = lane24 == 0, lane24 == LANES - 1
    inside = jnp.logical_and(
        jnp.logical_or(row24 >= 8, has_south), jnp.logical_or(row24 < 16, has_north)
    )

    def ring_east(c, h, seam=first24):
        return (
            roll(jnp.where(seam, h, c), LANES - 1),
            roll(jnp.where(seam, c, h), LANES - 1),
        )

    def ring_west(c, h):
        return (
            roll(jnp.where(last24, h, c), 1),
            roll(jnp.where(last24, c, h), 1),
        )

    def north24(x):
        return pltpu.roll(x, 23, 0)

    def south24(x):
        return pltpu.roll(x, 1, 0)

    edges = jnp.where(lax.rem(lane24, 64) < 32, D2[0, 2], D2[0, 0])
    col = [jnp.where(inside, x, 0.0) for x in (D2[0, 1], edges)]
    ocean = [x > 0.0 for x in col]
    cu = [jnp.minimum(a, b) for a, b in zip(col, ring_east(*col))]
    cv = [jnp.minimum(a, north24(a)) for a in col]
    CC[...] = col[0]
    CU[...] = cu[0]
    CV[...] = cv[0]
    for n in range(2):
        S4[n] = jnp.where(
            lane24 < 64,
            in_slots(cu[1 - n], (126, 127, 0, 1), 4),
            in_slots(cv[1 - n], (126, 127, 0, 1), 4),
        )

    at_wall = jnp.where(
        jnp.logical_or(
            jnp.logical_and(row == 0, jnp.logical_not(has_south)),
            jnp.logical_and(row == ROWS - 1, jnp.logical_not(has_north)),
        ),
        19.0,
        20.0,
    )
    latitude = (row + gy * ROWS).astype(jnp.float32)
    f4 = (0.25 * DT) * (0.2 + 0.3 * (latitude + 0.5) / (ROWS * ny))
    centre_uv = 1.0 - (DT * NU) * at_wall
    centre_ts = 1.0 - KAPPA * at_wall

    by_walls(received, G_A, (K, 11), (51, 10), (29, 15))

    @pl.loop(0, NC)
    def _(c):
        base = (c * LC).astype(jnp.float32)
        for f, depths in ((0, CU), (1, CV)):
            low, high = depths[6:14, :] - base, depths[10:18, :] - base
            for i in range(LC):
                k = c * LC + i
                a = jnp.where(low > i, X[f, k, 6:14, :], 0.0)
                b = jnp.where(high > i, X[f, k, 10:18, :], 0.0)
                XM[f, k, 6:14, :] = a
                XM[f, k, 10:18, :] = b

    class Slots:
        def __init__(self, count, width, span):
            shape = (count, ROWS, LANES)
            self.lanes = lax.broadcasted_iota(jnp.int32, shape, 2)
            self.place = lax.rem(self.lanes, width)
            tile = lax.broadcasted_iota(jnp.int32, shape, 0)
            self.level = (lax.div(lax.rem(self.lanes, span), width) + tile * (K // count)).astype(
                jnp.float32
            )
            self.west, self.east = self.place == width // 2 - 1, self.place == width // 2
            self.western = self.place < width // 2

        def beyond(self, west, east, f, r):
            return jnp.where(self.western, west[f, :, r : r + 8, :], east[f, :, r : r + 8, :])

        def if_wet(self, depths, n, r, x):
            return jnp.where(self.level < depths[n, r + 7 : r + 15, :][None], x, 0.0)

        def far(self, d, y):
            z = 2.0 * y - 8.0 * d
            return jnp.where(self.western, roll(d, -2), roll(d, 2)) + jnp.where(
                self.west, roll(z, -1), jnp.where(self.east, roll(z, 1), 0.0)
            )

    by4, by8 = Slots(NM, 4, 64), Slots(NC, 8, LANES)

    def excess(r):
        return by4.if_wet(S4, 0, r, by4.beyond(PW, PE, 0, r)) - by4.if_wet(
            S4, 1, r, pack[0, :, r : r + 8, :]
        )

    d_s, d, d_n = [excess(r) for r in range(3)]
    dp = PP[...] - packp[...]
    u_half = by4.lanes < 64
    EUV[...] = (
        jnp.where(
            jnp.logical_and(by4.west, u_half),
            f4[None] * roll(d + d_s, -65) - roll(dp, -1),
            jnp.where(
                jnp.logical_and(by4.east, jnp.logical_not(u_half)),
                -f4[None] * roll(d + d_n, 65),
                0.0,
            ),
        )
        - (DT * NU) * by4.far(d, d_n + d_s)
    )

    def momentum(c, carry):
        sum_u0, sum_v0, sum_u, sum_v = carry
        base = (c * LM).astype(jnp.float32)
        edge = EUV[c]
        cu0, cv0 = CU[8:16, :] - base, CV[8:16, :] - base
        for i in range(LM):
            k = c * LM + i
            dz = thickness(base, i)
            uss, us, u, un, unn = [XM[0, k, r : r + 8, :] for r in range(6, 11)]
            vss, vs, v, vn, vnn = [XM[1, k, r : r + 8, :] for r in range(6, 11)]
            load, load_n = PX[k, 0:8, :], PX[k, 1:9, :]
            cross_u = f4 * (v + vs)
            cross_v = f4 * (u + un)
            yu, yv = (DT * NU) * (un + us), (DT * NU) * (vn + vs)
            au, av = (DT * NU) * u, (DT * NU) * v
            zu, zv = 8.0 * au - 2.0 * yu, 8.0 * av - 2.0 * yv
            u1 = (
                centre_uv * u
                + 8.0 * yu
                - (DT * NU) * (unn + uss)
                + (cross_u + load)
                + (roll(zu + (cross_u - load), -1) + roll(zu, 1))
                - (roll(au, -2) + roll(au, 2))
                + jnp.where(edge4, unpacked(edge, i, 4), 0.0)
            )
            v1 = (
                centre_uv * v
                + 8.0 * yv
                - (DT * NU) * (vnn + vss)
                - cross_v
                - (load_n - load)
                + (roll(zv, -1) + roll(zv - cross_v, 1))
                - (roll(av, -2) + roll(av, 2))
                + jnp.where(edge4, unpacked(edge, i + 16, 4), 0.0)
            )
            u1 = jnp.where(cu0 > i, u1, 0.0)
            v1 = jnp.where(cv0 > i, v1, 0.0)
            sum_u0 = sum_u0 + u * dz
            sum_v0 = sum_v0 + v * dz
            sum_u = sum_u + u1 * dz
            sum_v = sum_v + v1 * dz
            U1B[k] = u1
            V1X[k, 8:16, :] = v1
        return sum_u0, sum_v0, sum_u, sum_v

    sums = lax.fori_loop(0, NM, momentum, (zero,) * 4)

    edge = sums[0]
    for n in range(4):
        F2[n, 8:16, :] = sums[n]
        near = jnp.logical_and(lane >= 32 * n - 16, lane < 32 * n + 16)
        edge = jnp.where(near, roll(sums[n], 32 * n), edge)
    FT[...] = edge
    for dy in (-1, 1):

        @beside(dy)
        def _():
            edge_tiles(G_SUM, FT, lambda n: FE.at[n], dy)

    edge_tiles(G_SUM, FT, lambda n: FE.at[n], 0)
    for dy in (-1, 1):

        @beside(dy)
        def _():
            whole_tiles(G_SUM, F2, dy)


    @beside(1)
    def _():
        send(G_B, V1X.at[:, pl.ds(15, 1), :], V1X.at[:, pl.ds(7, 1), :], 0, 1)

    @pl.loop(0, NC)
    def _(c):
        held_u = held_v = zero
        for i in range(LC):
            k = c * LC + i
            held_u = jnp.where(slot == i, packed(U1B[k], i), held_u)
            held_v = jnp.where(slot == i, packed(V1X[k, 8:16, :], i), held_v)
        pack1[0, c, 1:9, :] = held_u
        pack1[1, c, 1:9, :] = held_v

    for_east[...] = jnp.where(by8.western, pack1[0, :, 1:9, :], roll(pack1[1, :, 1:9, :], 4))
    for_west[...] = jnp.where(by8.western, roll(pack1[0, :, 1:9, :], -4), pack1[1, :, 1:9, :])

    @beside(1)
    def _():
        for dx, src, dst in ((1, for_east, P1W), (-1, for_west, P1E)):
            send(G_B, src.at[:, pl.ds(7, 1), :], dst.at[:, pl.ds(0, 1), :], dx, 1)

    for dx, src, dst in ((1, for_east, P1W), (-1, for_west, P1E)):
        send(G_B, src, dst.at[:, pl.ds(1, 8), :], dx, 0)

    @beside(1)
    def _():
        send(G_B, pack1.at[1, :, pl.ds(8, 1), :], pack1.at[1, :, pl.ds(0, 1), :], 0, 1)

    by_walls(left, G_2D, (10, 8), (6, 8), (6, 8))
    by_walls(left, G_A, (K, 11), (29, 15), (51, 10))
    by_walls(left, G_TS, (52, 10), (34, 10), (34, 10))
    by_walls(received, G_TS, (52, 10), (34, 10), (34, 10))

    edge_col = [in_slots(x, (124, 125, 126, 127, 0, 1, 2, 3)) for x in (col[1], col[0])]
    edge_cu = [jnp.minimum(a, b) for a, b in zip(edge_col, ring_east(*edge_col, slot24 == 4))]
    for n in range(2):
        SC[n] = edge_col[n]
        SU[n] = edge_cu[n]
        SV[n] = jnp.minimum(edge_col[n], north24(edge_col[n]))

    for f in range(2):
        south, here, north = [
            by8.if_wet(SC, 0, r, by8.beyond(TW, TE, f, r)) for r in range(3)
        ]
        own_s, own, own_n = [
            by8.if_wet(SC, 1, r, pack_ts[f, :, r : r + 8, :]) for r in range(3)
        ]
        HC[f] = here
        HO[f] = own
        HS[f, 0] = half * (here + roll(jnp.where(by8.east, own, here), -1))
        HS[f, 1] = half * (own + roll(jnp.where(by8.east, here, own), -1))
        HS[f, 2] = half * (here + north)
        HS[f, 3] = half * (south + here)
        HS[f, 4] = half * (own + own_n)
        HS[f, 5] = half * (own_s + own)

    @pl.loop(0, NC)
    def _(c):
        base = (c * LC).astype(jnp.float32)
        low, mid, high = [CC[r : r + 8, :] - base for r in (7, 8, 9)]
        for f in range(2):
            edge = HC[f, c]
            for i in range(LC):
                k = c * LC + i
                south = jnp.where(low > i, X[2 + f, k, 7:15, :], 0.0)
                here = jnp.where(mid > i, X[2 + f, k, 8:16, :], 0.0)
                north = jnp.where(high > i, X[2 + f, k, 9:17, :], 0.0)
                X[2 + f, k, 7:15, :] = south
                X[2 + f, k, 9:17, :] = north
                east = jnp.where(last, roll(edge, LANES - 5 - 8 * i), roll(here, -1))
                CE[f, k] = half * (here + east)
                CN[f, k, 7:15, :] = half * (south + here)
                CN[f, k, 8:16, :] = half * (here + north)

    def both(op, *pairs):
        return [op(*xs) for xs in zip(*pairs)]

    def depth_of(c):
        return c * (0.5 / K + c * (0.5 / (K * K)))

    open_u = [(x > 0.0).astype(jnp.float32) for x in cu]
    open_v = [(x > 0.0).astype(jnp.float32) for x in cv]
    depth_u = both(depth_of, cu)
    depth_v = both(depth_of, cv)
    pull_u = both(lambda o, d: o * d * (DB * GRAVITY), open_u, depth_u)
    pull_v = both(lambda o, d: o * d * (DB * GRAVITY), open_v, depth_v)
    pull_w = ring_west(*pull_u)
    ease = both(lambda o: jnp.where(o, DB, 0.0), ocean)
    height = [jnp.where(o, x, 0.0) for o, x in zip(ocean, (D2[1, 1], roll(edges, 64)))]

    inverse_u = both(lambda d, o: 1.0 / (d + (1.0 - o)), depth_u, open_u)
    inverse_v = both(lambda d, o: 1.0 / (d + (1.0 - o)), depth_v, open_v)
    by_walls(received, G_SUM, (14, 8), (8, 8), (8, 8))
    edges = jnp.where(lax.rem(lane24, 32) < 16, FE[2], FE[0])
    u0, v0, u_all, v_all = [[F2[n], roll(edges, -32 * n)] for n in range(4)]
    push_u = both(lambda o, a, b: jnp.where(o > 0.0, (a - b) * (DB / DT), 0.0), open_u, u_all, u0)
    push_v = both(lambda o, a, b: jnp.where(o > 0.0, (a - b) * (DB / DT), 0.0), open_v, v_all, v0)
    trans_u = both(lambda o, a: jnp.where(o > 0.0, a, 0.0), open_u, u0)
    trans_v = both(lambda o, a: jnp.where(o > 0.0, a, 0.0), open_v, v0)
    run_u = [jnp.zeros((24, LANES), jnp.float32)] * 2
    run_v = run_u

    def substep(_, state):
        level, trans_u, trans_w, trans_v, run_u, run_v = state
        level_w = ring_west(*level)
        trans_w = both(
            lambda t, p, q, h, w: t + (p - q * (h - w)), trans_w, push_w, pull_w, level, level_w
        )
        trans_u = both(
            lambda t, p, q, e, h: t + (p - q * (e - h)),
            trans_u,
            push_u,
            pull_u,
            ring_east(*level),
            level,
        )
        trans_v = both(
            lambda t, p, q, h: t + (p - q * (north24(h) - h)), trans_v, push_v, pull_v, level
        )
        level = both(
            lambda h, e, u, w, v: h - e * ((u - w) + (v - south24(v))),
            level,
            ease,
            trans_u,
            trans_w,
            trans_v,
        )
        return level, trans_u, trans_w, trans_v, both(jnp.add, run_u, trans_u), both(jnp.add, run_v, trans_v)

    trans_w, push_w = ring_west(*trans_u), ring_west(*push_u)
    state = height, trans_u, trans_w, trans_v, run_u, run_v
    for n in range(SUBSTEPS):
        state = substep(n, state)
    height, _, _, _, run_u, run_v = state

    HN[...] = height[0][8:16]

    def shift(r, a, inverse):
        return (r * (1.0 / SUBSTEPS) - a) * inverse

    shift_u = both(shift, run_u, u_all, inverse_u)
    shift_v = both(shift, run_v, v_all, inverse_v)
    DV[0] = shift_v[0]
    DV[1] = shift_v[1]
    du, dv, dvs = shift_u[0][8:16], shift_v[0][8:16], DV[0, 7:15, :]
    DP[0] = in_slots(shift_u[1][8:16], (125, 126, 127, 0, 1))
    DP[1] = in_slots(DV[1, 8:16, :], (126, 127, 0, 1))
    DP[2] = in_slots(DV[1, 7:15, :], (126, 127, 0, 1))
    DP[3] = in_slots(du, (125, 126, 127, 0, 1))
    DP[4] = in_slots(dv, (126, 127, 0, 1))
    DP[5] = in_slots(dvs, (126, 127, 0, 1))

    by_walls(received, G_B, (17, 10), (10, 8), (17, 10))
    beyond_u = jnp.where(by8.western, P1W[:, 1:9, :], roll(P1E[:, 1:9, :], 4))
    beyond_v = jnp.where(by8.western, roll(P1W[:, 1:9, :], -4), P1E[:, 1:9, :])
    beyond_vs = jnp.where(by8.western, roll(P1W[:, 0:8, :], -4), P1E[:, 0:8, :])
    edge_u = by8.if_wet(SU, 0, 1, beyond_u + DP[0][None])
    edge_v = by8.if_wet(SV, 0, 1, beyond_v + DP[1][None])
    edge_vs = by8.if_wet(SV, 0, 0, beyond_vs + DP[2][None])
    own_u = by8.if_wet(SU, 1, 1, pack1[0, :, 1:9, :] + DP[3][None])
    own_v = by8.if_wet(SV, 1, 1, pack1[1, :, 1:9, :] + DP[4][None])
    own_vs = by8.if_wet(SV, 1, 0, pack1[1, :, 0:8, :] + DP[5][None])
    for f in range(2):
        flux, flux_own = edge_u * HS[f, 0], own_u * HS[f, 1]
        flux_west = roll(jnp.where(by8.west, flux_own, flux), 1)
        flux_own_west = roll(jnp.where(by8.west, flux, flux_own), 1)
        a = HC[f] - ((flux - flux_west) + (edge_v * HS[f, 2] - edge_vs * HS[f, 3]))
        own = HO[f] - ((flux_own - flux_own_west) + (own_v * HS[f, 4] - own_vs * HS[f, 5]))
        FW[f] = flux
        AD[f, :, 1:9, :] = by8.if_wet(SC, 0, 1, a) - by8.if_wet(SC, 1, 1, own)

    @beside(1)
    def _():
        send(G_UP_EDGE, AD.at[:, :, pl.ds(8, 1), :], AD.at[:, :, pl.ds(0, 1), :], 0, 1)

    @beside(-1)
    def _():
        send(G_DOWN_EDGE, AD.at[:, :, pl.ds(1, 1), :], AD.at[:, :, pl.ds(9, 1), :], 0, -1)

    def send_rows(c, up):
        src, dst, dy, group = (14, 6, 1, G_UP) if up else (8, 16, -1, G_DOWN)
        levels = pl.ds(c * LC, LC)
        send(
            group,
            AX.at[:, levels, pl.ds(src, 2), :],
            AX.at[:, levels, pl.ds(dst, 2), :],
            0,
            dy,
        )

    @pl.loop(0, NC)
    def _(c):
        base = (c * LC).astype(jnp.float32)
        edges = [FW[f, c] for f in range(2)]
        cc0, cu0, cv0 = CC[8:16, :] - base, CU[8:16, :] - base, CV[8:16, :] - base
        cvs = CV[7:15, :] - base
        for i in range(LC):
            k = c * LC + i
            u = jnp.where(cu0 > i, U1B[k] + du, 0.0)
            v = jnp.where(cv0 > i, V1X[k, 8:16, :] + dv, 0.0)
            vs = jnp.where(cvs > i, V1X[k, 7:15, :] + dvs, 0.0)
            UN[k] = u
            VN[k] = v
            for f in range(2):
                flux = u * CE[f, k]
                flux_west = jnp.where(first, roll(edges[f], LANES - 3 - 8 * i), roll(flux, 1))
                a = X[2 + f, k, 8:16, :] - (
                    (flux - flux_west) + (v * CN[f, k, 8:16, :] - vs * CN[f, k, 7:15, :])
                )
                a = jnp.where(cc0 > i, a, 0.0)
                AX[f, k, 8:16, :] = a

        @pl.when(has_north)
        def _():
            send_rows(c, True)

        @pl.when(has_south)
        def _():
            send_rows(c, False)

    by_walls(left, G_SUM, (14, 8), (8, 8), (8, 8))
    by_walls(left, G_B, (17, 10), (17, 10), (10, 8))

    @pl.loop(0, NC)
    def _(c):
        for i in range(LC):
            k = c * LC + i
            for f, out in ((0, TN), (1, SN)):
                a = AX[f, k, 8:16, :]
                b = KAPPA * a
                out[k] = (
                    centre_ts * a
                    + 8.0 * (roll(b, -1) + roll(b, 1))
                    - (roll(b, -2) + roll(b, 2))
                )

    edge_row = AD.at[:, :, pl.ds(0, 1), :]
    two_rows = X.at[pl.ds(0, 2), :, pl.ds(0, 2), :]

    @beside(-1)
    def _():
        received(G_UP_EDGE, edge_row)

    @beside(1)
    def _():
        received(G_DOWN_EDGE, edge_row)

    for f in range(2):
        south, here, north = [AD[f, :, r : r + 8, :] for r in range(3)]
        EM[f] = KAPPA * by8.far(here, south + north)

    @beside(-1)
    def _():
        received(G_UP, two_rows)
        left(G_DOWN, two_rows)
        left(G_DOWN_EDGE, edge_row)

    @beside(1)
    def _():
        received(G_DOWN, two_rows)
        left(G_UP, two_rows)
        left(G_UP_EDGE, edge_row)


def finish(TN, SN, UN, VN, HN, AX, EM, CC, t_out, s_out, u_out, v_out, h_out, TO, SO, sem):
    copies = [
        pltpu.make_async_copy(src, dst, sem.at[n])
        for n, (src, dst) in enumerate(((UN, u_out), (VN, v_out), (HN, h_out)))
    ]
    for copy in copies:
        copy.start()
    lane = lax.broadcasted_iota(jnp.int32, (ROWS, LANES), 1)
    edge4 = jnp.logical_or(lane < 2, lane >= LANES - 2)

    def roll(x, shift):
        return pltpu.roll(x, shift % LANES, 1)

    @pl.loop(0, NC)
    def _(c):
        cc0 = CC[8:16, :] - (c * LC).astype(jnp.float32)
        edges = [EM[f, c] for f in range(2)]
        for i in range(LC):
            k = c * LC + i
            for f, part, out in ((0, TN, TO), (1, SN, SO)):
                ss, s, n, nn = [AX[f, k, r : r + 8, :] for r in (6, 7, 9, 10)]
                y = KAPPA * (n + s)
                mixed = (
                    part[k]
                    + 8.0 * y
                    - 2.0 * (roll(y, -1) + roll(y, 1))
                    - KAPPA * (nn + ss)
                    - jnp.where(edge4, roll(edges[f], LANES - 4 - 8 * i), 0.0)
                )
                out[k] = jnp.where(cc0 > i, mixed, 0.0)
        levels = pl.ds(c * LC, LC)
        pltpu.make_async_copy(TO.at[levels], t_out.at[levels], sem.at[3]).start()
        pltpu.make_async_copy(SO.at[levels], s_out.at[levels], sem.at[4]).start()

    for copy in copies:
        copy.wait()
    pltpu.make_async_copy(TO, t_out, sem.at[3]).wait()
    pltpu.make_async_copy(SO, s_out, sem.at[4]).wait()


def per_device(nx, ny, *args):
    tile3 = jax.ShapeDtypeStruct((K, ROWS, LANES), jnp.float32)
    tile2 = jax.ShapeDtypeStruct((ROWS, LANES), jnp.float32)
    outs = (tile3, tile3, tile3, tile3, tile2)

    def vmem(*shape, dtype=jnp.float32):
        return pltpu.VMEM(shape, dtype)

    args = [pltpu.with_memory_space_constraint(x, pltpu.HBM) for x in args]
    held = pl.pallas_call(
        functools.partial(kernel, nx, ny),
        out_shape=tuple(
            pltpu.VMEM(shape, jnp.float32)
            for shape in [x.shape for x in outs]
            + [(2, K, 24, LANES), (2, NC, ROWS, LANES), (24, LANES)]
        ),
        in_specs=[pl.BlockSpec(memory_space=pltpu.HBM)] * 7,
        out_specs=[pl.BlockSpec(memory_space=pltpu.VMEM)] * 8,
        scratch_shapes=[
            vmem(2, K, 24, LANES),
            vmem(4, K, 24, LANES),
            vmem(K, 16, LANES),
            vmem(2, 3, 24, LANES),
            vmem(ROWS, LANES),
            vmem(ROWS, LANES, dtype=jnp.int32),
            vmem(ROWS, LANES, dtype=jnp.int32),
            vmem(24, LANES),
            vmem(24, LANES),
            vmem(2, 24, LANES),
            vmem(2, 24, LANES),
            vmem(2, 24, LANES),
            vmem(2, 24, LANES),
            vmem(1, NM, 16, LANES),
            vmem(1, NM, 16, LANES),
            vmem(1, NM, 16, LANES),
            vmem(NM, ROWS, LANES),
            vmem(NM, ROWS, LANES),
            vmem(2, NC, 16, LANES),
            vmem(2, NC, 16, LANES),
            vmem(2, NC, 16, LANES),
            vmem(4, 24, LANES),
            vmem(ROWS, LANES),
            vmem(3, 24, LANES),
            vmem(2, 24, LANES),
            vmem(6, ROWS, LANES),
            vmem(K, ROWS, LANES),
            vmem(K, 16, LANES),
            vmem(2, NC, 16, LANES),
            vmem(NC, 16, LANES),
            vmem(NC, 16, LANES),
            vmem(NC, ROWS, LANES),
            vmem(NC, ROWS, LANES),
            vmem(2, NC, 16, LANES),
            vmem(NM, ROWS, LANES),
            vmem(2, NC, ROWS, LANES),
            vmem(2, K, ROWS, LANES),
            vmem(2, K, 16, LANES),
            vmem(2, NC, ROWS, LANES),
            vmem(2, 6, NC, ROWS, LANES),
            vmem(2, NC, ROWS, LANES),
            pltpu.SemaphoreType.DMA((2,)),
            pltpu.SemaphoreType.DMA((GROUPS,)),
            pltpu.SemaphoreType.DMA((GROUPS,)),
        ],
        compiler_params=pltpu.CompilerParams(
            collective_id=0, has_side_effects=True, vmem_limit_bytes=24 * 1024 * 1024
        ),
    )(*args)
    return pl.pallas_call(
        finish,
        out_shape=outs,
        in_specs=[pl.BlockSpec(memory_space=pltpu.VMEM)] * 8,
        out_specs=[pl.BlockSpec(memory_space=pltpu.HBM)] * 5,
        scratch_shapes=[
            vmem(K, ROWS, LANES),
            vmem(K, ROWS, LANES),
            pltpu.SemaphoreType.DMA((5,)),
        ],
        compiler_params=pltpu.CompilerParams(vmem_limit_bytes=8 * 1024 * 1024),
    )(*held)


def solution(mesh):
    placed = (P(None, "gy", "gx"),) * 4 + (P("gy", "gx"),) * 3
    return jax.shard_map(
        functools.partial(per_device, mesh.shape["gx"], mesh.shape["gy"]),
        mesh=mesh,
        in_specs=placed,
        out_specs=(P(None, "gy", "gx"),) * 4 + (P("gy", "gx"),),
        check_vma=False,
    )
```

```python
import functools

import jax
import jax.numpy as jnp
from jax import lax
from jax.experimental import pallas as pl
from jax.experimental.pallas import tpu as pltpu
from jax.sharding import PartitionSpec as P

MESH = pl.DeviceIdType.MESH
K = 75
NC = 5
LC = K // NC
NM = 5
LM = K // NM
SUBSTEPS = 8
ROWS = 8
LANES = 128

DT = 0.4
NU = 0.025
KAPPA = 0.01
DTT = 0.2
GRAVITY = 4.0
DB = DT / SUBSTEPS

GROUPS = 9
G_2D, G_A, G_TS, G_SUM, G_B, G_UP, G_DOWN, G_UP_EDGE, G_DOWN_EDGE = range(GROUPS)


def kernel(
    nx,
    ny,
    t_in,
    s_in,
    u_in,
    v_in,
    h_in,
    flag_in,
    bottom_in,
    TN,
    SN,
    UN,
    VN,
    HN,
    AX,
    EM,
    CC,
    X,
    PX,
    D2,
    ET,
    flag_v,
    bottom_v,
    CU,
    CV,
    SC,
    SU,
    SV,
    S4,
    pack,
    PE,
    PW,
    packp,
    PP,
    pack_ts,
    TE,
    TW,
    F2,
    FT,
    FE,
    DV,
    DP,
    U1B,
    V1X,
    pack1,
    P1E,
    P1W,
    for_east,
    for_west,
    AD,
    EUV,
    HC,
    CE,
    CN,
    FW,
    HS,
    HO,
    load_sem,
    send_sem,
    recv_sem,
):
    gx, gy = lax.axis_index("gx"), lax.axis_index("gy")

    def device(dx, dy):
        return (lax.rem(gx + dx + nx, nx), lax.rem(gy + dy + ny, ny))

    def send(group, src, dst, dx, dy):
        pltpu.make_async_remote_copy(
            src_ref=src,
            dst_ref=dst,
            send_sem=send_sem.at[group],
            recv_sem=recv_sem.at[group],
            device_id=device(dx, dy),
            device_id_type=MESH,
        ).start()

    def received(group, size):
        pltpu.make_async_copy(size, size, recv_sem.at[group]).wait()

    def left(group, size):
        pltpu.make_async_copy(size, size, send_sem.at[group]).wait()

    has_south, has_north = gy > 0, gy < ny - 1

    def beside(dy):
        return pl.when(has_north if dy > 0 else has_south)

    barrier = pltpu.get_barrier_semaphore()

    def greet(dx, dy):
        pl.semaphore_signal(barrier, inc=1, device_id=device(dx, dy), device_id_type=MESH)

    for dy in (-1, 1):

        @beside(dy)
        def _():
            for dx in (-1, 1, 0):
                greet(dx, dy)

    for dx in (-1, 1):
        greet(dx, 0)

    pltpu.make_async_copy(flag_in, flag_v, load_sem.at[0]).start()
    pltpu.make_async_copy(bottom_in, bottom_v, load_sem.at[0]).start()
    pltpu.make_async_copy(h_in, D2.at[1, 1, pl.ds(8, 8), :], load_sem.at[0]).start()
    for f, source in enumerate((u_in, v_in, t_in, s_in)):
        pltpu.make_async_copy(source, X.at[f, :, pl.ds(8, 8), :], load_sem.at[1]).start()

    def loaded(sem, size):
        pltpu.make_async_copy(size, size, load_sem.at[sem]).wait()

    lane = lax.broadcasted_iota(jnp.int32, (ROWS, LANES), 1)
    slot = lax.div(lane, 8).astype(jnp.float32)
    row = lax.broadcasted_iota(jnp.int32, (ROWS, LANES), 0)
    first, last = lane == 0, lane == LANES - 1
    half = 0.5 * DTT
    edge4 = jnp.logical_or(lane < 2, lane >= LANES - 2)
    slot4 = lax.div(lane, 4).astype(jnp.float32)
    zero = jnp.zeros((ROWS, LANES), jnp.float32)

    def roll(x, shift):
        return pltpu.roll(x, shift % LANES, x.ndim - 1)

    def packed(x, i, width=8):
        return roll(x, width * i + width // 2)

    def unpacked(x, i, width=8):
        return roll(x, LANES - width // 2 - width * i)

    def in_slots(x, lanes, width=8):
        at = lax.rem(lax.broadcasted_iota(jnp.int32, x.shape, 1), width)
        out = None
        for l in lanes:
            column = jnp.broadcast_to(x[:, l : l + 1], x.shape)
            out = column if out is None else jnp.where(at == (l + width // 2) % LANES, column, out)
        return out

    @pl.when(jnp.logical_not(has_south))
    def _():
        AD[:, :, 0:1, :] = jnp.zeros((2, NC, 1, LANES), jnp.float32)

        @pl.loop(0, K)
        def _(k):
            for f in range(2):
                AX[f, k, 6:8, :] = jnp.zeros((2, LANES), jnp.float32)

    @pl.when(jnp.logical_not(has_north))
    def _():
        AD[:, :, 9:10, :] = jnp.zeros((2, NC, 1, LANES), jnp.float32)

        @pl.loop(0, K)
        def _(k):
            for f in range(2):
                AX[f, k, 16:18, :] = jnp.zeros((2, LANES), jnp.float32)

    loaded(0, AX.at[0, pl.ds(0, 3), pl.ds(8, 8), :])
    own = (flag_v[...] * bottom_v[...]).astype(jnp.float32)
    D2[0, 1, 8:16, :] = own
    ET[...] = jnp.where(jnp.logical_and(lane >= 32, lane < 96), roll(D2[1, 1, 8:16, :], 64), own)

    def rows(group, fields, count, dy):
        src, dst = (16 - count, 8 - count) if dy > 0 else (8, 16)
        send(
            group,
            X.at[fields, :, pl.ds(src, count), :],
            X.at[fields, :, pl.ds(dst, count), :],
            0,
            dy,
        )

    loaded(1, X.at[:, :, pl.ds(8, 8), :])
    def weight(t, s, dz):
        return (0.8 * s - t * (0.2 + 0.05 * t)) * dz

    def thickness(base, i):
        return 0.5 / K + (base + (i + 0.5)) * (1.0 / (K * K))

    def press(c, cum):
        base = (c * LM).astype(jnp.float32)
        depth = D2[0, 1, 8:16, :] - base
        held = held_p = zero
        for i in range(LM):
            k = c * LM + i
            u, v, t, s = [X[f, k, 8:16, :] for f in range(4)]
            w = jnp.where(depth > i, weight(t, s, DT * thickness(base, i)), 0.0)
            cum = cum + w
            load = cum - 0.5 * w
            PX[k, 0:8, :] = load
            held = jnp.where(slot4 == i, packed(u, i, 4), held)
            held = jnp.where(slot4 == i + 16, packed(v, i + 16, 4), held)
            held_p = jnp.where(slot4 == i, packed(load, i, 4), held_p)
        pack[0, c, 1:9, :] = held
        packp[c] = held_p
        return cum

    lax.fori_loop(0, NM, press, zero)

    pl.semaphore_wait(
        barrier, 2 + 3 * (has_south.astype(jnp.int32) + has_north.astype(jnp.int32))
    )

    def corners(group, src, west, east, dy):
        for dx in (1, -1):
            side = west if dx > 0 else east
            r_src, r_dst = (8, 0) if dy > 0 else (1, 9)
            send(
                group,
                src.at[:, :, pl.ds(r_src, 1), :],
                side.at[:, :, pl.ds(r_dst, 1), :],
                dx,
                dy,
            )

    def pole(group, ref, dy):
        src, dst = (8, 0) if dy > 0 else (1, 9)
        send(group, ref.at[:, :, pl.ds(src, 1), :], ref.at[:, :, pl.ds(dst, 1), :], 0, dy)

    def edge_tiles(group, edge, aside, dy):
        for dx in (-1, 1):
            send(group, edge, aside(1 - dx).at[pl.ds(8 * (1 - dy), 8), :], dx, dy)

    def whole_tiles(group, whole, dy):
        send(group, whole.at[:, pl.ds(8, 8), :], whole.at[:, pl.ds(8 * (1 - dy), 8), :], 0, dy)

    def edges_2d(dy):
        edge_tiles(G_2D, ET, lambda n: D2.at[0, n], dy)

    edges_2d(0)
    for dx in (1, -1):
        side = PW if dx > 0 else PE
        send(G_A, pack.at[:, :, pl.ds(1, 8), :], side.at[:, :, pl.ds(1, 8), :], dx, 0)
    send(G_A, packp, PP, -1, 0)
    for dy in (-1, 1):

        @beside(dy)
        def _():
            edges_2d(dy)
            corners(G_A, pack, PW, PE, dy)

    for dy in (-1, 1):

        @beside(dy)
        def _():
            whole_tiles(G_2D, D2.at[:, 1], dy)
            rows(G_A, pl.ds(0, 2), 2, dy)
            pole(G_A, pack, dy)
            if dy < 0:
                send(G_A, PX.at[:, pl.ds(0, 1), :], PX.at[:, pl.ds(8, 1), :], 0, dy)

    @pl.loop(0, NC)
    def _(c):
        held = [zero] * 2
        for i in range(LC):
            for f in range(2):
                held[f] = jnp.where(slot == i, packed(X[2 + f, c * LC + i, 8:16, :], i), held[f])
        for f in range(2):
            pack_ts[f, c, 1:9, :] = held[f]

    for dx in (1, -1):
        side = TW if dx > 0 else TE
        send(G_TS, pack_ts.at[:, :, pl.ds(1, 8), :], side.at[:, :, pl.ds(1, 8), :], dx, 0)
    for dy in (-1, 1):

        @beside(dy)
        def _():
            corners(G_TS, pack_ts, TW, TE, dy)
            rows(G_TS, pl.ds(2, 2), 1, dy)
            pole(G_TS, pack_ts, dy)

    def size(levels, count):
        return X.at[0, pl.ds(0, levels), pl.ds(0, count), :]

    def by_walls(wait, group, inner, southmost, northmost):
        @pl.when(jnp.logical_and(has_south, has_north))
        def _():
            wait(group, size(*inner))

        @pl.when(jnp.logical_not(has_south))
        def _():
            wait(group, size(*southmost))

        @pl.when(jnp.logical_not(has_north))
        def _():
            wait(group, size(*northmost))

    by_walls(received, G_2D, (10, 8), (6, 8), (6, 8))
    row24 = lax.broadcasted_iota(jnp.int32, (24, LANES), 0)
    lane24 = lax.broadcasted_iota(jnp.int32, (24, LANES), 1)
    slot24 = lax.rem(lane24, 8)
    first24, last24 = lane24 == 0, lane24 == LANES - 1
    inside = jnp.logical_and(
        jnp.logical_or(row24 >= 8, has_south), jnp.logical_or(row24 < 16, has_north)
    )

    def ring_east(c, h, seam=first24):
        return (
            roll(jnp.where(seam, h, c), LANES - 1),
            roll(jnp.where(seam, c, h), LANES - 1),
        )

    def ring_west(c, h):
        return (
            roll(jnp.where(last24, h, c), 1),
            roll(jnp.where(last24, c, h), 1),
        )

    def north24(x):
        return pltpu.roll(x, 23, 0)

    def south24(x):
        return pltpu.roll(x, 1, 0)

    edges = jnp.where(lax.rem(lane24, 64) < 32, D2[0, 2], D2[0, 0])
    col = [jnp.where(inside, x, 0.0) for x in (D2[0, 1], edges)]
    ocean = [x > 0.0 for x in col]
    cu = [jnp.minimum(a, b) for a, b in zip(col, ring_east(*col))]
    cv = [jnp.minimum(a, north24(a)) for a in col]
    CC[...] = col[0]
    CU[...] = cu[0]
    CV[...] = cv[0]
    for n in range(2):
        S4[n] = jnp.where(
            lane24 < 64,
            in_slots(cu[1 - n], (126, 127, 0, 1), 4),
            in_slots(cv[1 - n], (126, 127, 0, 1), 4),
        )

    at_wall = jnp.where(
        jnp.logical_or(
            jnp.logical_and(row == 0, jnp.logical_not(has_south)),
            jnp.logical_and(row == ROWS - 1, jnp.logical_not(has_north)),
        ),
        19.0,
        20.0,
    )
    latitude = (row + gy * ROWS).astype(jnp.float32)
    f4 = (0.25 * DT) * (0.2 + 0.3 * (latitude + 0.5) / (ROWS * ny))
    centre_uv = 1.0 - (DT * NU) * at_wall
    centre_ts = 1.0 - KAPPA * at_wall

    by_walls(received, G_A, (K, 11), (51, 10), (29, 15))
    by_walls(left, G_A, (K, 11), (29, 15), (51, 10))

    @pl.loop(0, NC)
    def _(c):
        base = (c * LC).astype(jnp.float32)
        for f, depths in ((0, CU), (1, CV)):
            low, high = depths[6:14, :] - base, depths[10:18, :] - base
            for i in range(LC):
                k = c * LC + i
                a = jnp.where(low > i, X[f, k, 6:14, :], 0.0)
                b = jnp.where(high > i, X[f, k, 10:18, :], 0.0)
                X[f, k, 6:14, :] = a
                X[f, k, 10:18, :] = b

    class Slots:
        def __init__(self, count, width, span):
            shape = (count, ROWS, LANES)
            self.lanes = lax.broadcasted_iota(jnp.int32, shape, 2)
            self.place = lax.rem(self.lanes, width)
            tile = lax.broadcasted_iota(jnp.int32, shape, 0)
            self.level = (lax.div(lax.rem(self.lanes, span), width) + tile * (K // count)).astype(
                jnp.float32
            )
            self.west, self.east = self.place == width // 2 - 1, self.place == width // 2
            self.western = self.place < width // 2

        def beyond(self, west, east, f, r):
            return jnp.where(self.western, west[f, :, r : r + 8, :], east[f, :, r : r + 8, :])

        def if_wet(self, depths, n, r, x):
            return jnp.where(self.level < depths[n, r + 7 : r + 15, :][None], x, 0.0)

        def far(self, d, y):
            z = 2.0 * y - 8.0 * d
            return jnp.where(self.western, roll(d, -2), roll(d, 2)) + jnp.where(
                self.west, roll(z, -1), jnp.where(self.east, roll(z, 1), 0.0)
            )

    by4, by8 = Slots(NM, 4, 64), Slots(NC, 8, LANES)

    def excess(r):
        return by4.if_wet(S4, 0, r, by4.beyond(PW, PE, 0, r)) - by4.if_wet(
            S4, 1, r, pack[0, :, r : r + 8, :]
        )

    d_s, d, d_n = [excess(r) for r in range(3)]
    dp = PP[...] - packp[...]
    u_half = by4.lanes < 64
    EUV[...] = (
        jnp.where(
            jnp.logical_and(by4.west, u_half),
            f4[None] * roll(d + d_s, -65) - roll(dp, -1),
            jnp.where(
                jnp.logical_and(by4.east, jnp.logical_not(u_half)),
                -f4[None] * roll(d + d_n, 65),
                0.0,
            ),
        )
        - (DT * NU) * by4.far(d, d_n + d_s)
    )

    def momentum(c, carry):
        sum_u0, sum_v0, sum_u, sum_v = carry
        base = (c * LM).astype(jnp.float32)
        edge = EUV[c]
        cu0, cv0 = CU[8:16, :] - base, CV[8:16, :] - base
        for i in range(LM):
            k = c * LM + i
            dz = thickness(base, i)
            uss, us, u, un, unn = [X[0, k, r : r + 8, :] for r in range(6, 11)]
            vss, vs, v, vn, vnn = [X[1, k, r : r + 8, :] for r in range(6, 11)]
            load, load_n = PX[k, 0:8, :], PX[k, 1:9, :]
            cross_u = f4 * (v + vs)
            cross_v = f4 * (u + un)
            yu, yv = (DT * NU) * (un + us), (DT * NU) * (vn + vs)
            au, av = (DT * NU) * u, (DT * NU) * v
            zu, zv = 8.0 * au - 2.0 * yu, 8.0 * av - 2.0 * yv
            u1 = (
                centre_uv * u
                + 8.0 * yu
                - (DT * NU) * (unn + uss)
                + (cross_u + load)
                + (roll(zu + (cross_u - load), -1) + roll(zu, 1))
                - (roll(au, -2) + roll(au, 2))
                + jnp.where(edge4, unpacked(edge, i, 4), 0.0)
            )
            v1 = (
                centre_uv * v
                + 8.0 * yv
                - (DT * NU) * (vnn + vss)
                - cross_v
                - (load_n - load)
                + (roll(zv, -1) + roll(zv - cross_v, 1))
                - (roll(av, -2) + roll(av, 2))
                + jnp.where(edge4, unpacked(edge, i + 16, 4), 0.0)
            )
            u1 = jnp.where(cu0 > i, u1, 0.0)
            v1 = jnp.where(cv0 > i, v1, 0.0)
            sum_u0 = sum_u0 + u * dz
            sum_v0 = sum_v0 + v * dz
            sum_u = sum_u + u1 * dz
            sum_v = sum_v + v1 * dz
            U1B[k] = u1
            V1X[k, 8:16, :] = v1
        return sum_u0, sum_v0, sum_u, sum_v

    sums = lax.fori_loop(0, NM, momentum, (zero,) * 4)

    edge = sums[0]
    for n in range(4):
        F2[n, 8:16, :] = sums[n]
        near = jnp.logical_and(lane >= 32 * n - 16, lane < 32 * n + 16)
        edge = jnp.where(near, roll(sums[n], 32 * n), edge)
    FT[...] = edge
    for dy in (-1, 1):

        @beside(dy)
        def _():
            edge_tiles(G_SUM, FT, lambda n: FE.at[n], dy)

    edge_tiles(G_SUM, FT, lambda n: FE.at[n], 0)
    for dy in (-1, 1):

        @beside(dy)
        def _():
            whole_tiles(G_SUM, F2, dy)


    @beside(1)
    def _():
        send(G_B, V1X.at[:, pl.ds(15, 1), :], V1X.at[:, pl.ds(7, 1), :], 0, 1)

    @pl.loop(0, NC)
    def _(c):
        held_u = held_v = zero
        for i in range(LC):
            k = c * LC + i
            held_u = jnp.where(slot == i, packed(U1B[k], i), held_u)
            held_v = jnp.where(slot == i, packed(V1X[k, 8:16, :], i), held_v)
        pack1[0, c, 1:9, :] = held_u
        pack1[1, c, 1:9, :] = held_v

    for_east[...] = jnp.where(by8.western, pack1[0, :, 1:9, :], roll(pack1[1, :, 1:9, :], 4))
    for_west[...] = jnp.where(by8.western, roll(pack1[0, :, 1:9, :], -4), pack1[1, :, 1:9, :])

    @beside(1)
    def _():
        for dx, src, dst in ((1, for_east, P1W), (-1, for_west, P1E)):
            send(G_B, src.at[:, pl.ds(7, 1), :], dst.at[:, pl.ds(0, 1), :], dx, 1)

    for dx, src, dst in ((1, for_east, P1W), (-1, for_west, P1E)):
        send(G_B, src, dst.at[:, pl.ds(1, 8), :], dx, 0)

    @beside(1)
    def _():
        send(G_B, pack1.at[1, :, pl.ds(8, 1), :], pack1.at[1, :, pl.ds(0, 1), :], 0, 1)

    by_walls(left, G_2D, (10, 8), (6, 8), (6, 8))
    by_walls(left, G_TS, (52, 10), (34, 10), (34, 10))
    by_walls(received, G_TS, (52, 10), (34, 10), (34, 10))

    edge_col = [in_slots(x, (124, 125, 126, 127, 0, 1, 2, 3)) for x in (col[1], col[0])]
    edge_cu = [jnp.minimum(a, b) for a, b in zip(edge_col, ring_east(*edge_col, slot24 == 4))]
    for n in range(2):
        SC[n] = edge_col[n]
        SU[n] = edge_cu[n]
        SV[n] = jnp.minimum(edge_col[n], north24(edge_col[n]))

    for f in range(2):
        south, here, north = [
            by8.if_wet(SC, 0, r, by8.beyond(TW, TE, f, r)) for r in range(3)
        ]
        own_s, own, own_n = [
            by8.if_wet(SC, 1, r, pack_ts[f, :, r : r + 8, :]) for r in range(3)
        ]
        HC[f] = here
        HO[f] = own
        HS[f, 0] = half * (here + roll(jnp.where(by8.east, own, here), -1))
        HS[f, 1] = half * (own + roll(jnp.where(by8.east, here, own), -1))
        HS[f, 2] = half * (here + north)
        HS[f, 3] = half * (south + here)
        HS[f, 4] = half * (own + own_n)
        HS[f, 5] = half * (own_s + own)

    @pl.loop(0, NC)
    def _(c):
        base = (c * LC).astype(jnp.float32)
        low, mid, high = [CC[r : r + 8, :] - base for r in (7, 8, 9)]
        for f in range(2):
            edge = HC[f, c]
            for i in range(LC):
                k = c * LC + i
                south = jnp.where(low > i, X[2 + f, k, 7:15, :], 0.0)
                here = jnp.where(mid > i, X[2 + f, k, 8:16, :], 0.0)
                north = jnp.where(high > i, X[2 + f, k, 9:17, :], 0.0)
                X[2 + f, k, 7:15, :] = south
                X[2 + f, k, 9:17, :] = north
                east = jnp.where(last, roll(edge, LANES - 5 - 8 * i), roll(here, -1))
                CE[f, k] = half * (here + east)
                CN[f, k, 7:15, :] = half * (south + here)
                CN[f, k, 8:16, :] = half * (here + north)

    def both(op, *pairs):
        return [op(*xs) for xs in zip(*pairs)]

    def depth_of(c):
        return c * (0.5 / K + c * (0.5 / (K * K)))

    open_u = [(x > 0.0).astype(jnp.float32) for x in cu]
    open_v = [(x > 0.0).astype(jnp.float32) for x in cv]
    depth_u = both(depth_of, cu)
    depth_v = both(depth_of, cv)
    pull_u = both(lambda o, d: o * d * (DB * GRAVITY), open_u, depth_u)
    pull_v = both(lambda o, d: o * d * (DB * GRAVITY), open_v, depth_v)
    pull_w = ring_west(*pull_u)
    ease = both(lambda o: jnp.where(o, DB, 0.0), ocean)
    height = [jnp.where(o, x, 0.0) for o, x in zip(ocean, (D2[1, 1], roll(edges, 64)))]

    inverse_u = both(lambda d, o: 1.0 / (d + (1.0 - o)), depth_u, open_u)
    inverse_v = both(lambda d, o: 1.0 / (d + (1.0 - o)), depth_v, open_v)
    by_walls(received, G_SUM, (14, 8), (8, 8), (8, 8))
    edges = jnp.where(lax.rem(lane24, 32) < 16, FE[2], FE[0])
    u0, v0, u_all, v_all = [[F2[n], roll(edges, -32 * n)] for n in range(4)]
    push_u = both(lambda o, a, b: jnp.where(o > 0.0, (a - b) * (DB / DT), 0.0), open_u, u_all, u0)
    push_v = both(lambda o, a, b: jnp.where(o > 0.0, (a - b) * (DB / DT), 0.0), open_v, v_all, v0)
    trans_u = both(lambda o, a: jnp.where(o > 0.0, a, 0.0), open_u, u0)
    trans_v = both(lambda o, a: jnp.where(o > 0.0, a, 0.0), open_v, v0)
    run_u = [jnp.zeros((24, LANES), jnp.float32)] * 2
    run_v = run_u

    def substep(_, state):
        level, trans_u, trans_w, trans_v, run_u, run_v = state
        level_w = ring_west(*level)
        trans_w = both(
            lambda t, p, q, h, w: t + (p - q * (h - w)), trans_w, push_w, pull_w, level, level_w
        )
        trans_u = both(
            lambda t, p, q, e, h: t + (p - q * (e - h)),
            trans_u,
            push_u,
            pull_u,
            ring_east(*level),
            level,
        )
        trans_v = both(
            lambda t, p, q, h: t + (p - q * (north24(h) - h)), trans_v, push_v, pull_v, level
        )
        level = both(
            lambda h, e, u, w, v: h - e * ((u - w) + (v - south24(v))),
            level,
            ease,
            trans_u,
            trans_w,
            trans_v,
        )
        return level, trans_u, trans_w, trans_v, both(jnp.add, run_u, trans_u), both(jnp.add, run_v, trans_v)

    trans_w, push_w = ring_west(*trans_u), ring_west(*push_u)
    state = height, trans_u, trans_w, trans_v, run_u, run_v
    for n in range(SUBSTEPS):
        state = substep(n, state)
    height, _, _, _, run_u, run_v = state

    HN[...] = height[0][8:16]

    def shift(r, a, inverse):
        return (r * (1.0 / SUBSTEPS) - a) * inverse

    shift_u = both(shift, run_u, u_all, inverse_u)
    shift_v = both(shift, run_v, v_all, inverse_v)
    DV[0] = shift_v[0]
    DV[1] = shift_v[1]
    du, dv, dvs = shift_u[0][8:16], shift_v[0][8:16], DV[0, 7:15, :]
    DP[0] = in_slots(shift_u[1][8:16], (125, 126, 127, 0, 1))
    DP[1] = in_slots(DV[1, 8:16, :], (126, 127, 0, 1))
    DP[2] = in_slots(DV[1, 7:15, :], (126, 127, 0, 1))
    DP[3] = in_slots(du, (125, 126, 127, 0, 1))
    DP[4] = in_slots(dv, (126, 127, 0, 1))
    DP[5] = in_slots(dvs, (126, 127, 0, 1))

    by_walls(received, G_B, (17, 10), (10, 8), (17, 10))
    beyond_u = jnp.where(by8.western, P1W[:, 1:9, :], roll(P1E[:, 1:9, :], 4))
    beyond_v = jnp.where(by8.western, roll(P1W[:, 1:9, :], -4), P1E[:, 1:9, :])
    beyond_vs = jnp.where(by8.western, roll(P1W[:, 0:8, :], -4), P1E[:, 0:8, :])
    edge_u = by8.if_wet(SU, 0, 1, beyond_u + DP[0][None])
    edge_v = by8.if_wet(SV, 0, 1, beyond_v + DP[1][None])
    edge_vs = by8.if_wet(SV, 0, 0, beyond_vs + DP[2][None])
    own_u = by8.if_wet(SU, 1, 1, pack1[0, :, 1:9, :] + DP[3][None])
    own_v = by8.if_wet(SV, 1, 1, pack1[1, :, 1:9, :] + DP[4][None])
    own_vs = by8.if_wet(SV, 1, 0, pack1[1, :, 0:8, :] + DP[5][None])
    for f in range(2):
        flux, flux_own = edge_u * HS[f, 0], own_u * HS[f, 1]
        flux_west = roll(jnp.where(by8.west, flux_own, flux), 1)
        flux_own_west = roll(jnp.where(by8.west, flux, flux_own), 1)
        a = HC[f] - ((flux - flux_west) + (edge_v * HS[f, 2] - edge_vs * HS[f, 3]))
        own = HO[f] - ((flux_own - flux_own_west) + (own_v * HS[f, 4] - own_vs * HS[f, 5]))
        FW[f] = flux
        AD[f, :, 1:9, :] = by8.if_wet(SC, 0, 1, a) - by8.if_wet(SC, 1, 1, own)

    @beside(1)
    def _():
        send(G_UP_EDGE, AD.at[:, :, pl.ds(8, 1), :], AD.at[:, :, pl.ds(0, 1), :], 0, 1)

    @beside(-1)
    def _():
        send(G_DOWN_EDGE, AD.at[:, :, pl.ds(1, 1), :], AD.at[:, :, pl.ds(9, 1), :], 0, -1)

    def send_rows(c, up):
        src, dst, dy, group = (14, 6, 1, G_UP) if up else (8, 16, -1, G_DOWN)
        levels = pl.ds(c * LC, LC)
        send(
            group,
            AX.at[:, levels, pl.ds(src, 2), :],
            AX.at[:, levels, pl.ds(dst, 2), :],
            0,
            dy,
        )

    @pl.loop(0, NC)
    def _(c):
        base = (c * LC).astype(jnp.float32)
        edges = [FW[f, c] for f in range(2)]
        cc0, cu0, cv0 = CC[8:16, :] - base, CU[8:16, :] - base, CV[8:16, :] - base
        cvs = CV[7:15, :] - base
        for i in range(LC):
            k = c * LC + i
            u = jnp.where(cu0 > i, U1B[k] + du, 0.0)
            v = jnp.where(cv0 > i, V1X[k, 8:16, :] + dv, 0.0)
            vs = jnp.where(cvs > i, V1X[k, 7:15, :] + dvs, 0.0)
            UN[k] = u
            VN[k] = v
            for f in range(2):
                flux = u * CE[f, k]
                flux_west = jnp.where(first, roll(edges[f], LANES - 3 - 8 * i), roll(flux, 1))
                a = X[2 + f, k, 8:16, :] - (
                    (flux - flux_west) + (v * CN[f, k, 8:16, :] - vs * CN[f, k, 7:15, :])
                )
                a = jnp.where(cc0 > i, a, 0.0)
                AX[f, k, 8:16, :] = a

        @pl.when(has_north)
        def _():
            send_rows(c, True)

        @pl.when(has_south)
        def _():
            send_rows(c, False)

    by_walls(left, G_SUM, (14, 8), (8, 8), (8, 8))
    by_walls(left, G_B, (17, 10), (17, 10), (10, 8))

    @pl.loop(0, NC)
    def _(c):
        for i in range(LC):
            k = c * LC + i
            for f, out in ((0, TN), (1, SN)):
                a = AX[f, k, 8:16, :]
                b = KAPPA * a
                out[k] = (
                    centre_ts * a
                    + 8.0 * (roll(b, -1) + roll(b, 1))
                    - (roll(b, -2) + roll(b, 2))
                )

    edge_row = AD.at[:, :, pl.ds(0, 1), :]
    two_rows = X.at[pl.ds(0, 2), :, pl.ds(0, 2), :]

    @beside(-1)
    def _():
        received(G_UP_EDGE, edge_row)

    @beside(1)
    def _():
        received(G_DOWN_EDGE, edge_row)

    for f in range(2):
        south, here, north = [AD[f, :, r : r + 8, :] for r in range(3)]
        EM[f] = KAPPA * by8.far(here, south + north)

    @beside(-1)
    def _():
        received(G_UP, two_rows)
        left(G_DOWN, two_rows)
        left(G_DOWN_EDGE, edge_row)

    @beside(1)
    def _():
        received(G_DOWN, two_rows)
        left(G_UP, two_rows)
        left(G_UP_EDGE, edge_row)


def finish(TN, SN, UN, VN, HN, AX, EM, CC, t_out, s_out, u_out, v_out, h_out, TO, SO, sem):
    copies = [
        pltpu.make_async_copy(src, dst, sem.at[n])
        for n, (src, dst) in enumerate(((UN, u_out), (VN, v_out), (HN, h_out)))
    ]
    for copy in copies:
        copy.start()
    lane = lax.broadcasted_iota(jnp.int32, (ROWS, LANES), 1)
    edge4 = jnp.logical_or(lane < 2, lane >= LANES - 2)

    def roll(x, shift):
        return pltpu.roll(x, shift % LANES, 1)

    @pl.loop(0, NC)
    def _(c):
        cc0 = CC[8:16, :] - (c * LC).astype(jnp.float32)
        edges = [EM[f, c] for f in range(2)]
        for i in range(LC):
            k = c * LC + i
            for f, part, out in ((0, TN, TO), (1, SN, SO)):
                ss, s, n, nn = [AX[f, k, r : r + 8, :] for r in (6, 7, 9, 10)]
                y = KAPPA * (n + s)
                mixed = (
                    part[k]
                    + 8.0 * y
                    - 2.0 * (roll(y, -1) + roll(y, 1))
                    - KAPPA * (nn + ss)
                    - jnp.where(edge4, roll(edges[f], LANES - 4 - 8 * i), 0.0)
                )
                out[k] = jnp.where(cc0 > i, mixed, 0.0)
        levels = pl.ds(c * LC, LC)
        pltpu.make_async_copy(TO.at[levels], t_out.at[levels], sem.at[3]).start()
        pltpu.make_async_copy(SO.at[levels], s_out.at[levels], sem.at[4]).start()

    for copy in copies:
        copy.wait()
    pltpu.make_async_copy(TO, t_out, sem.at[3]).wait()
    pltpu.make_async_copy(SO, s_out, sem.at[4]).wait()


def per_device(nx, ny, *args):
    tile3 = jax.ShapeDtypeStruct((K, ROWS, LANES), jnp.float32)
    tile2 = jax.ShapeDtypeStruct((ROWS, LANES), jnp.float32)
    outs = (tile3, tile3, tile3, tile3, tile2)

    def vmem(*shape, dtype=jnp.float32):
        return pltpu.VMEM(shape, dtype)

    args = [pltpu.with_memory_space_constraint(x, pltpu.HBM) for x in args]
    held = pl.pallas_call(
        functools.partial(kernel, nx, ny),
        out_shape=tuple(
            pltpu.VMEM(shape, jnp.float32)
            for shape in [x.shape for x in outs]
            + [(2, K, 24, LANES), (2, NC, ROWS, LANES), (24, LANES)]
        ),
        in_specs=[pl.BlockSpec(memory_space=pltpu.HBM)] * 7,
        out_specs=[pl.BlockSpec(memory_space=pltpu.VMEM)] * 8,
        scratch_shapes=[
            vmem(4, K, 24, LANES),
            vmem(K, 16, LANES),
            vmem(2, 3, 24, LANES),
            vmem(ROWS, LANES),
            vmem(ROWS, LANES, dtype=jnp.int32),
            vmem(ROWS, LANES, dtype=jnp.int32),
            vmem(24, LANES),
            vmem(24, LANES),
            vmem(2, 24, LANES),
            vmem(2, 24, LANES),
            vmem(2, 24, LANES),
            vmem(2, 24, LANES),
            vmem(1, NM, 16, LANES),
            vmem(1, NM, 16, LANES),
            vmem(1, NM, 16, LANES),
            vmem(NM, ROWS, LANES),
            vmem(NM, ROWS, LANES),
            vmem(2, NC, 16, LANES),
            vmem(2, NC, 16, LANES),
            vmem(2, NC, 16, LANES),
            vmem(4, 24, LANES),
            vmem(ROWS, LANES),
            vmem(3, 24, LANES),
            vmem(2, 24, LANES),
            vmem(6, ROWS, LANES),
            vmem(K, ROWS, LANES),
            vmem(K, 16, LANES),
            vmem(2, NC, 16, LANES),
            vmem(NC, 16, LANES),
            vmem(NC, 16, LANES),
            vmem(NC, ROWS, LANES),
            vmem(NC, ROWS, LANES),
            vmem(2, NC, 16, LANES),
            vmem(NM, ROWS, LANES),
            vmem(2, NC, ROWS, LANES),
            vmem(2, K, ROWS, LANES),
            vmem(2, K, 16, LANES),
            vmem(2, NC, ROWS, LANES),
            vmem(2, 6, NC, ROWS, LANES),
            vmem(2, NC, ROWS, LANES),
            pltpu.SemaphoreType.DMA((2,)),
            pltpu.SemaphoreType.DMA((GROUPS,)),
            pltpu.SemaphoreType.DMA((GROUPS,)),
        ],
        compiler_params=pltpu.CompilerParams(
            collective_id=0, has_side_effects=True, vmem_limit_bytes=24 * 1024 * 1024
        ),
    )(*args)
    return pl.pallas_call(
        finish,
        out_shape=outs,
        in_specs=[pl.BlockSpec(memory_space=pltpu.VMEM)] * 8,
        out_specs=[pl.BlockSpec(memory_space=pltpu.HBM)] * 5,
        scratch_shapes=[
            vmem(K, ROWS, LANES),
            vmem(K, ROWS, LANES),
            pltpu.SemaphoreType.DMA((5,)),
        ],
        compiler_params=pltpu.CompilerParams(vmem_limit_bytes=8 * 1024 * 1024),
    )(*held)


def solution(mesh):
    placed = (P(None, "gy", "gx"),) * 4 + (P("gy", "gx"),) * 3
    return jax.shard_map(
        functools.partial(per_device, mesh.shape["gx"], mesh.shape["gy"]),
        mesh=mesh,
        in_specs=placed,
        out_specs=(P(None, "gy", "gx"),) * 4 + (P("gy", "gx"),),
        check_vma=False,
    )
```
